256 devices in a mesh: dp: 32 (over z, x), tensor: 8 (over y, core).
Axes of the slice: x: 4, y: 4, z: 8, core: 2. Of those that a mesh axis runs over, the one named last changes fastest.
Arguments:
- hidden: bfloat16 [1024, 8192], P('dp', 'tensor'), may hold values from -6 to 6
- queries: bfloat16 [1024, 8192], P('dp', 'tensor'), may hold values from -128 to 128
- rotated_key_cache: bfloat16 [1024, 384, 1024], P('dp', None, 'tensor'), may hold values from -4 to 4
- stored_value_cache: bfloat16 [1024, 384, 1024], P('dp', None, 'tensor'), may hold values from -6 to 6
- lengths: int32 [1024], P('dp'), may hold values from 2 to 384, as said below
- tenants: int32 [1024], P('dp'), may hold values from 0 to 511, as said below
- key_value_weight: bfloat16 [8192, 2048], P(None, 'tensor'), may hold values from -0.0625 to 0.0625
- adapter_down_maps: bfloat16 [512, 8192, 64], P('dp', 'tensor'), may hold values from -0.0625 to 0.0625
- adapter_up_maps: bfloat16 [512, 64, 1024], P('dp', None, 'tensor'), may hold values from -0.75 to 0.75
Outputs:
- attended: bfloat16 [1024, 8192], P('dp', 'tensor')
- new_entries: bfloat16 [1024, 2048], P('dp', 'tensor')
The draws below stay inside these ranges and needn't reach their ends.
Inputs may be any that keep to these rules, and one draw needn't show every extreme that they name: `tenants`: adapters k * 16 to (k + 1) * 16 - 1 form the k-th block of the pool. Among the 32 rows of one index of dp at most 2 use adapters of one block; one block is used by exactly 2 rows of every index of dp. `lengths`: the first row of each index of dp has 384 cached positions.
All inputs are finite; a program needn't handle non-finite values.
Results may differ from the reference program's by a relative error of at most 0.0075.
Values may be sent and summed in bfloat16 or wider, within the bound.
No kernel may reach another device: no remote copies, remote signals or barrier semaphores. Data moves between devices by JAX's collectives and lax.ppermute only.
A program may use at most 64 MiB of HBM per device.

```python
import jax
import jax.numpy as jnp
from jax import lax

MODEL_WIDTH = 8192
HEADS = 64
KEY_VALUE_HEADS = 8
HEAD_SIZE = 128
ADAPTER_RANK = 64
ADP_DEV = 16
ROWS_PER_SHARD = 32
LEN = 384
DECODE_ROWS = 1024
ADAPTER_POOL = 512
CAP = 2
N_DP = 32


def shared_front(key):
    return jax.random.normal(jax.random.fold_in(key, 3), (DECODE_ROWS, 2, KEY_VALUE_HEADS * HEAD_SIZE), jnp.float32)


def draw_rotated_key_cache(key, part):
    front = shared_front(key)
    key = jax.random.fold_in(key, 17)
    remainder = jax.random.normal(key, (DECODE_ROWS, LEN - 2, KEY_VALUE_HEADS * HEAD_SIZE), jnp.float32)
    return jnp.clip(jnp.concatenate([front, remainder], axis=1), -4.0, 4.0).astype(jnp.bfloat16)


def draw_queries(key, part):
    key = jax.random.fold_in(key, 19)
    entries = jax.random.normal(key, (DECODE_ROWS, HEADS * HEAD_SIZE), jnp.float32)
    return entries.astype(jnp.bfloat16)


def draw_lengths(key, part):
    key = jax.random.fold_in(key, 13)
    drawn = jax.random.randint(key, (DECODE_ROWS,), 2, LEN + 1)
    leading = jnp.arange(DECODE_ROWS) % ROWS_PER_SHARD == 0
    return jnp.where(leading, LEN, drawn).astype(jnp.int32)


def draw_tenants(key, part):
    key = jax.random.fold_in(key, 11)
    hot_owner = jax.random.randint(jax.random.fold_in(key, 1), (), 0, N_DP)
    slot_owner = jnp.repeat(jnp.arange(N_DP, dtype=jnp.int32), CAP)

    def one_block(block_key):
        order_key, shuffle_key, adapter_key = jax.random.split(block_key, 3)
        ranking = jax.random.permutation(order_key, N_DP * CAP).astype(jnp.int32)
        ranking = ranking - (slot_owner == hot_owner).astype(jnp.int32) * (4 * N_DP * CAP)
        chosen = slot_owner[jnp.argsort(ranking)[:ROWS_PER_SHARD]]
        chosen = jax.random.permutation(shuffle_key, chosen)
        local_pick = jax.random.randint(adapter_key, (ROWS_PER_SHARD,), 0, ADP_DEV)
        return (chosen * ADP_DEV + local_pick).astype(jnp.int32)
    block_keys = jax.random.split(jax.random.fold_in(key, 2), DECODE_ROWS // ROWS_PER_SHARD)
    return jax.vmap(one_block)(block_keys).reshape(DECODE_ROWS)


def block_levels(rng, dims, pieces, smallest, top_value):
    gain, own = 1.0, jax.random.fold_in(rng, 6)
    for axis_at, parts in pieces:
        draws = jnp.exp(jax.random.uniform(jax.random.fold_in(own, axis_at), (parts,), jnp.float32, smallest / len(pieces), top_value / len(pieces)))
        gain = gain * jnp.repeat(draws, dims[axis_at] // parts).reshape([-1 if axis == axis_at else 1 for axis in range(len(dims))])
    return gain


def scatter_about(own_key, shape, deviation, most, cuts=(), kind=jnp.bfloat16):
    loudness = block_levels(own_key, shape, cuts, -0.22, 0.18) if cuts else 1.0
    values = jax.random.normal(own_key, shape, jnp.float32) * deviation * loudness
    return jnp.minimum(jnp.maximum(values, -most), most).astype(kind)


def setup_inputs(seed: int = 0) -> dict:
    arg_keys = jax.random.split(jax.random.key(seed), 10)
    hidden = scatter_about(arg_keys[0], (DECODE_ROWS, MODEL_WIDTH), 1.0, 6.0, ((0, 32), (1, 8)))
    queries = draw_queries(jax.random.fold_in(arg_keys[9], 71), 0)
    rotated_key_cache = draw_rotated_key_cache(jax.random.fold_in(arg_keys[9], 71), 0)
    stored_value_cache = scatter_about(arg_keys[3], (DECODE_ROWS, LEN, KEY_VALUE_HEADS * HEAD_SIZE), 1.0, 6.0, ((0, 32), (2, 8)))
    lengths = draw_lengths(jax.random.fold_in(arg_keys[9], 71), 0)
    tenants = draw_tenants(jax.random.fold_in(arg_keys[9], 71), 0)
    key_value_weight = scatter_about(arg_keys[6], (MODEL_WIDTH, KEY_VALUE_HEADS * 2 * HEAD_SIZE), MODEL_WIDTH ** -0.5, 0.0625, ((1, 8),))
    adapter_down_maps = scatter_about(arg_keys[7], (ADAPTER_POOL, MODEL_WIDTH, ADAPTER_RANK), MODEL_WIDTH ** -0.5, 0.0625, ((0, 32), (1, 8)))
    adapter_up_maps = scatter_about(arg_keys[8], (ADAPTER_POOL, ADAPTER_RANK, KEY_VALUE_HEADS * HEAD_SIZE), ADAPTER_RANK ** -0.5, 0.75, ((0, 32), (2, 8)))
    return {"hidden": hidden, "queries": queries, "rotated_key_cache": rotated_key_cache, "stored_value_cache": stored_value_cache, "lengths": lengths, "tenants": tenants, "key_value_weight": key_value_weight, "adapter_down_maps": adapter_down_maps, "adapter_up_maps": adapter_up_maps}


rope_base = 500000.0


def rotate(values, positions):
    half_dim = values.shape[-1] // 2
    inverse = rope_base ** (-(jnp.arange(half_dim, dtype=jnp.float32) * 2.0) / values.shape[-1])
    angles = positions.astype(jnp.float32)[:, None] * inverse[None, :]
    cosine = jnp.cos(angles)[:, None, :]
    sine_part = jnp.sin(angles)[:, None, :]
    front_half = values[..., :half_dim]
    back_half = values[..., half_dim:]
    return jnp.concatenate([front_half * cosine - back_half * sine_part, back_half * cosine + front_half * sine_part], axis=-1)


def attend_block(kernel_inputs):
    query_heads, cache_keys, cache_values, new_key, fresh_value, row_lengths = kernel_inputs
    score_scale = query_heads.shape[-1] ** -0.5
    query_wide = query_heads.astype(jnp.float32)
    scores = jnp.einsum("rkgd,rlkd->rkgl", query_wide, cache_keys.astype(jnp.float32), precision=lax.Precision.HIGHEST) * score_scale
    visible = jnp.arange(cache_keys.shape[1], dtype=jnp.int32)[None, :] < row_lengths[:, None]
    scores = jnp.where(visible[:, None, None, :], scores, -jnp.inf)
    own_score = jnp.einsum("rkgd,rkd->rkg", query_wide, new_key.astype(jnp.float32), precision=lax.Precision.HIGHEST) * score_scale
    largest = jnp.maximum(jnp.max(scores, axis=-1), own_score)
    weights = jnp.exp(scores - largest[..., None])
    own_weight = jnp.exp(own_score - largest)
    denominator = jnp.sum(weights, axis=-1) + own_weight
    weights = (weights / denominator[..., None]).astype(jnp.bfloat16)
    own_weight = (own_weight / denominator).astype(jnp.bfloat16)
    attended = jnp.einsum("rkgl,rlkd->rkgd", weights.astype(jnp.float32), cache_values.astype(jnp.float32), precision=lax.Precision.HIGHEST)
    attended = attended + own_weight.astype(jnp.float32)[..., None] * fresh_value.astype(jnp.float32)[:, :, None, :]
    return attended.astype(jnp.bfloat16)


def reference(hidden, queries, rotated_key_cache, stored_value_cache, lengths, tenants, key_value_weight, adapter_down_maps, adapter_up_maps):
    projected_values = jnp.dot(hidden, key_value_weight, preferred_element_type=jnp.float32).reshape(DECODE_ROWS, KEY_VALUE_HEADS, 2, HEAD_SIZE)
    new_key = rotate(projected_values[:, :, 0], lengths).astype(jnp.bfloat16)
    count_of_blocks = DECODE_ROWS // ROWS_PER_SHARD

    def adapter_block(kernel_inputs):
        block_rows, block_indices = kernel_inputs
        down_matrix_rows = adapter_down_maps[block_indices].astype(jnp.float32)
        rank_reduced = jnp.einsum("rd,rdk->rk", block_rows.astype(jnp.float32), down_matrix_rows, precision=lax.Precision.HIGHEST).astype(jnp.bfloat16)
        up_matrix_rows = adapter_up_maps[block_indices].astype(jnp.float32)
        return jnp.einsum("rk,rkc->rc", rank_reduced.astype(jnp.float32), up_matrix_rows, precision=lax.Precision.HIGHEST).astype(jnp.bfloat16)

    adapter_delta = lax.map(adapter_block, (hidden.reshape(count_of_blocks, ROWS_PER_SHARD, MODEL_WIDTH), tenants.reshape(count_of_blocks, ROWS_PER_SHARD)))
    adapter_delta = adapter_delta.reshape(DECODE_ROWS, KEY_VALUE_HEADS, HEAD_SIZE)
    fresh_value = (projected_values[:, :, 1] + adapter_delta.astype(jnp.float32)).astype(jnp.bfloat16)
    new_entries = jnp.stack([new_key, fresh_value], axis=2).reshape(DECODE_ROWS, KEY_VALUE_HEADS * 2 * HEAD_SIZE)
    group_size = HEADS // KEY_VALUE_HEADS
    attended = lax.map(attend_block, (
        queries.reshape(count_of_blocks, ROWS_PER_SHARD, KEY_VALUE_HEADS, group_size, HEAD_SIZE),
        rotated_key_cache.reshape(count_of_blocks, ROWS_PER_SHARD, LEN, KEY_VALUE_HEADS, HEAD_SIZE),
        stored_value_cache.reshape(count_of_blocks, ROWS_PER_SHARD, LEN, KEY_VALUE_HEADS, HEAD_SIZE),
        new_key.reshape(count_of_blocks, ROWS_PER_SHARD, KEY_VALUE_HEADS, HEAD_SIZE),
        fresh_value.reshape(count_of_blocks, ROWS_PER_SHARD, KEY_VALUE_HEADS, HEAD_SIZE),
        lengths.reshape(count_of_blocks, ROWS_PER_SHARD)))
    return attended.reshape(DECODE_ROWS, HEADS * HEAD_SIZE), new_entries
```

```python
import jax
import jax.numpy as jnp
import numpy as np
from jax import lax
from jax.experimental import pallas as pl
from jax.experimental.pallas import tpu as pltpu
from jax.sharding import PartitionSpec as P

HEAD_SIZE = 128
GROUP = 8
CAPACITY = 2
LANES = 128
ROPE_BASE = 500000.0
MIB = 1 << 20

F32, BF16, I32 = jnp.float32, jnp.bfloat16, jnp.int32
VMEM = pl.BlockSpec(memory_space=pltpu.VMEM)
SMEM = pl.BlockSpec(memory_space=pltpu.SMEM)


def iota(shape, dim):
    return lax.broadcasted_iota(I32, shape, dim)


def dot(a, b):
    return jnp.dot(a, b, preferred_element_type=F32)


def dot_t(a, b):
    return lax.dot_general(a, b, (((1,), (1,)), ((), ())), preferred_element_type=F32)


def upright(row):
    n = row.shape[1]
    spread = jnp.broadcast_to(row, (n, n))
    return jnp.sum(jnp.where(iota((n, n), 0) == iota((n, n), 1), spread, 0.0), axis=1, keepdims=True)


def shuffle(chunks, forward):
    wide = 16 * chunks
    row, col = iota((wide, wide), 0), iota((wide, wide), 1)
    chunked, message = (col, row) if forward else (row, col)
    k, s, c = chunked >> 4, (chunked >> 1) & 7, chunked & 1
    return jnp.where(message == s * (2 * chunks) + k * 2 + c, 1.0, 0.0).astype(BF16)


def slots_of(tenant_row, pool):
    n = tenant_row.shape[1]
    owner_row = jnp.floor(tenant_row * (1.0 / pool))
    owner_col = upright(owner_row)
    same = (owner_col == owner_row) & (iota((n, n), 0) < iota((n, n), 1))
    rank = jnp.sum(jnp.where(same, 1.0, 0.0), axis=0, keepdims=True)
    return owner_row * CAPACITY + rank


def place_kernel(pool, tenant_ref, hidden_ref, out_ref):
    rows, width = hidden_ref.shape
    chunks = width // LANES + 1
    slots = out_ref.shape[0] // chunks
    tenant_row = tenant_ref[...].astype(F32)
    slot_row = slots_of(tenant_row, pool)
    place = jnp.where(slot_row == iota((slots, rows), 0).astype(F32), 1.0, 0.0).astype(BF16)
    local = tenant_row - pool * jnp.floor(tenant_row * (1.0 / pool))
    local = jnp.broadcast_to(upright(local), (rows, LANES)).astype(BF16)
    placed = jnp.concatenate([dot(place, hidden_ref[...]), dot(place, local)], axis=1).astype(BF16)
    groups = slots // 16
    side = jnp.concatenate(
        [
            jnp.concatenate(
                [placed[g * 16 : g * 16 + 16, k * LANES : (k + 1) * LANES] for k in range(chunks)], axis=0
            )
            for g in range(groups)
        ],
        axis=1,
    )
    turned = dot(shuffle(chunks, True), side).astype(BF16)
    wide = 16 * chunks
    for g in range(groups):
        out_ref[g * wide : (g + 1) * wide, :] = turned[:, g * LANES : (g + 1) * LANES]


def down_kernel(got_ref, down_ref, partial_ref, ids_ref):
    slots = ids_ref.shape[0]
    chunks = got_ref.shape[0] // slots
    groups, wide = slots // 16, 16 * chunks
    side = jnp.concatenate([got_ref[g * wide : (g + 1) * wide, :] for g in range(groups)], axis=1)
    turned = dot(shuffle(chunks, False), side)
    ids = jnp.concatenate([turned[wide - 16 :, g * LANES : (g + 1) * LANES] for g in range(groups)], axis=0)
    turned = turned.astype(BF16)
    rows = jnp.concatenate(
        [
            jnp.concatenate(
                [turned[k * 16 : k * 16 + 16, g * LANES : (g + 1) * LANES] for k in range(chunks - 1)], axis=1
            )
            for g in range(groups)
        ],
        axis=0,
    )
    full = dot_t(rows, down_ref[...])
    lane = iota((slots, LANES), 1)
    right = (lane >= 64).astype(F32)
    total = jnp.zeros((slots, LANES), F32)
    for q in range(full.shape[1] // LANES):
        total += jnp.where(ids == right + 2.0 * q, full[:, q * LANES : (q + 1) * LANES], 0.0)
    total = total + pltpu.roll(total, 64, 1)
    half = slots // 2
    partial_ref[...] = jnp.where(lane[:half] < 64, total[:half], total[half:])
    ids_ref[...] = ids


def up_kernel(a_ref, b_ref, c_ref, d_ref, ids_ref, up_ref, out_ref):
    total = (a_ref[...] + b_ref[...]) + (c_ref[...] + d_ref[...])
    turned = pltpu.roll(total, 64, 1)
    left = iota(total.shape, 1) < 64
    both = jnp.concatenate([jnp.where(left, total, turned), jnp.where(left, turned, total)], axis=0)
    ids = ids_ref[...]
    right = (iota(ids.shape, 1) >= 64).astype(F32)
    spread = [
        jnp.where(ids == right + 2.0 * q, both, 0.0).astype(BF16) for q in range(up_ref.shape[0] // LANES)
    ]
    out_ref[...] = dot(jnp.concatenate(spread, axis=1), up_ref[...]).astype(BF16)


def cache_kernel(scale, length_ref, query_ref, key_ref, value_ref, sum_ref, top_ref, weight_ref):
    step = pl.program_id(0)
    some, length = key_ref.shape[0], key_ref.shape[1]
    rows = sum_ref.shape[0] // GROUP
    wide = some * GROUP
    by_head = jnp.concatenate(
        [query_ref[:, h * LANES : (h + 1) * LANES] for h in range(GROUP)], axis=0
    )
    row, col = iota((wide, wide), 0), iota((wide, wide), 1)
    turn = jnp.where(col == (row % GROUP) * some + row // GROUP, 1.0, 0.0).astype(BF16)
    by_row = dot(turn, by_head)
    position = iota((GROUP, length), 1)
    for r in range(some):
        query = by_row[r * GROUP : (r + 1) * GROUP].astype(BF16)
        scores = dot_t(query, key_ref[r]) * scale
        scores = jnp.where(position < length_ref[step * some + r], scores, -jnp.inf)
        top = jnp.max(scores, axis=1, keepdims=True)
        weights = jnp.exp(scores - top)
        whole = jnp.sum(weights, axis=1, keepdims=True)
        place = pl.ds(step * some + r, GROUP, stride=rows)
        sum_ref[place, :] = dot(weights.astype(BF16), value_ref[r])
        top_ref[place, :] = jnp.broadcast_to(top, (GROUP, LANES))
        weight_ref[place, :] = jnp.broadcast_to(whole, (GROUP, LANES))


def project_kernel(scale, pool, index_ref, tenant_ref, length_ref, inverse_ref, query_ref, own_ref, core_ref, y1_ref,
                   y2_ref, y3_ref, weight_ref, sum_ref, top_ref, whole_ref, value_ref, key_ref, mixed_ref, share_ref,
                   back_ref):
    rows, depth = own_ref.shape
    me = index_ref[0]

    def part(block, other):
        start = pl.multiple_of(other * depth, depth)
        return dot(block, weight_ref[pl.ds(start, depth), :])

    total = part(own_ref[...], me) + part(core_ref[...], me ^ 1)
    count = weight_ref.shape[0] // depth
    for shift, ref in ((1, y1_ref), (2, y2_ref), (3, y3_ref)):
        other = (me + count - 2 * shift) % count
        total += part(ref[:rows], other) + part(ref[rows:], other ^ 1)
    value_ref[...] = total[:, LANES:]
    angle = upright(length_ref[...].astype(F32)) * inverse_ref[...]
    lane = iota((rows, LANES), 1)
    sine = jnp.sin(angle)
    key = total[:, :LANES]
    key = key * jnp.cos(angle) + pltpu.roll(key, 64, 1) * jnp.where(lane < 64, -sine, sine)
    key = key.astype(BF16)
    key_ref[...] = key
    key = key.astype(F32)
    for h in range(GROUP):
        place = slice(h * rows, (h + 1) * rows)
        query = query_ref[:, h * LANES : (h + 1) * LANES].astype(F32)
        own = jnp.sum(query * key, axis=1, keepdims=True) * scale
        top = top_ref[place, :]
        highest = jnp.maximum(top, own)
        old, new = jnp.exp(top - highest), jnp.exp(own - highest)
        under = 1.0 / (old * whole_ref[place, :] + new)
        mixed_ref[place, :] = sum_ref[place, :] * (old * under)
        share_ref[place, :] = new * under
    slot_col = upright(slots_of(tenant_ref[...].astype(F32), pool))
    back_ref[...] = jnp.where(slot_col == lane.astype(F32), 1.0, 0.0).astype(BF16)


def final_kernel(got_ref, back_ref, value_ref, key_ref, mixed_ref, share_ref, out_ref, entry_ref):
    rows = value_ref.shape[0]
    slots = got_ref.shape[0]
    delta = dot(back_ref[:, :slots], got_ref[...])
    value = (value_ref[...] + delta).astype(BF16)
    entry_ref[:, :LANES] = key_ref[...]
    entry_ref[:, LANES:] = value
    value = value.astype(F32)
    for h in range(GROUP):
        place = slice(h * rows, (h + 1) * rows)
        out_ref[:, h * LANES : (h + 1) * LANES] = (mixed_ref[place, :] + share_ref[place, :] * value).astype(BF16)


def on_device(hidden, queries, key_cache, value_cache, lengths, tenants, weight, down, up):
    rows, depth = hidden.shape
    peers = lax.axis_size("dp")
    count = lax.axis_size("tensor")
    slots = peers * CAPACITY
    pool, _, rank = down.shape
    chunks = depth // LANES + 1
    length = key_cache.shape[1]
    scale = HEAD_SIZE ** -0.5
    shape = jax.ShapeDtypeStruct
    params = lambda size: pltpu.CompilerParams(vmem_limit_bytes=size * MIB)
    cost = lambda flops, size: pl.CostEstimate(flops=flops, bytes_accessed=size, transcendentals=0)

    tenant_row = tenants.reshape(1, rows)
    length_row = lengths.reshape(1, rows)
    me = lax.axis_index("tensor").astype(I32).reshape(1)
    over_core = lambda x: lax.ppermute(x, "tensor", [(i, i ^ 1) for i in range(count)])
    over_y = lambda x, k: lax.ppermute(x, "tensor", [(i, (i + 2 * k) % count) for i in range(count)])

    with jax.named_scope("place"):
        placed = pl.pallas_call(
            lambda *refs: place_kernel(pool, *refs),
            out_shape=shape((slots * chunks, LANES), BF16),
            in_specs=[VMEM] * 2, out_specs=VMEM, compiler_params=params(8),
        )(tenant_row, hidden)
    with jax.named_scope("rows_to_owners"):
        got = lax.all_to_all(
            placed.reshape(peers, chunks, CAPACITY, LANES), "dp", split_axis=0, concat_axis=0, tiled=True
        ).reshape(slots * chunks, LANES)
    with jax.named_scope("gather_hidden"):
        core_hidden = over_core(hidden)
        pair = jnp.concatenate([hidden, core_hidden], axis=0)
        others = [over_y(pair, k) for k in (1, 2, 3)]
    with jax.named_scope("cache"):
        some = 8
        full = lambda n: pl.BlockSpec((GROUP * rows, LANES), lambda i: (0, 0))
        sums, tops, wholes = pl.pallas_call(
            lambda *refs: cache_kernel(scale, *refs),
            grid=(rows // some,),
            out_shape=[shape((GROUP * rows, LANES), F32)] * 3,
            in_specs=[
                SMEM,
                pl.BlockSpec((some, GROUP * LANES), lambda i: (i, 0)),
                pl.BlockSpec((some, length, LANES), lambda i: (i, 0, 0)),
                pl.BlockSpec((some, length, LANES), lambda i: (i, 0, 0)),
            ],
            out_specs=[full(0)] * 3,
            compiler_params=params(16),
            cost_estimate=cost(2 * 2 * rows * GROUP * length * LANES, 2 * rows * length * LANES * 2),
        )(lengths, queries, key_cache, value_cache)
    with jax.named_scope("down"):
        partial, ids = pl.pallas_call(
            down_kernel,
            out_shape=[shape((slots // 2, LANES), F32), shape((slots, LANES), F32)],
            in_specs=[VMEM] * 2, out_specs=[VMEM] * 2, compiler_params=params(16),
        )(got, jnp.swapaxes(down, 1, 2).reshape(pool * rank, depth))
    with jax.named_scope("reduce"):
        pair_sum = partial + over_core(partial)
        sums_y = [over_y(pair_sum, k) for k in (1, 2, 3)]
    with jax.named_scope("project"):
        inverse = ROPE_BASE ** (-(np.arange(HEAD_SIZE // 2, dtype=np.float32) * 2.0) / HEAD_SIZE)
        inverse = jnp.asarray(np.concatenate([inverse, inverse])[None, :], F32)
        value, key, mixed, share, back = pl.pallas_call(
            lambda *refs: project_kernel(scale, pool, *refs),
            out_shape=[
                shape((rows, LANES), F32), shape((rows, LANES), BF16),
                shape((GROUP * rows, LANES), F32), shape((GROUP * rows, LANES), F32),
                shape((rows, LANES), BF16),
            ],
            in_specs=[SMEM] + [VMEM] * 13, out_specs=[VMEM] * 5, compiler_params=params(24),
            cost_estimate=cost(2 * rows * count * depth * 2 * LANES, weight.size * 2),
        )(me, tenant_row, length_row, inverse, queries, hidden, core_hidden, *others, weight, sums, tops, wholes)
    with jax.named_scope("up"):
        served = pl.pallas_call(
            up_kernel, out_shape=shape((slots, LANES), BF16),
            in_specs=[VMEM] * 6, out_specs=VMEM, compiler_params=params(8),
        )(pair_sum, *sums_y, ids, up.reshape(pool * rank, LANES))
    with jax.named_scope("answers"):
        returned = lax.all_to_all(
            served.reshape(peers, CAPACITY, LANES), "dp", split_axis=0, concat_axis=0, tiled=True
        ).reshape(slots, LANES)
    with jax.named_scope("finish"):
        return tuple(pl.pallas_call(
            final_kernel,
            out_shape=[shape((rows, GROUP * LANES), BF16), shape((rows, 2 * LANES), BF16)],
            in_specs=[VMEM] * 6, out_specs=[VMEM] * 2, compiler_params=params(8),
        )(returned, back, value, key, mixed, share))


def solution(mesh):
    in_specs = (
        P("dp", "tensor"),
        P("dp", "tensor"),
        P("dp", None, "tensor"),
        P("dp", None, "tensor"),
        P("dp"),
        P("dp"),
        P(None, "tensor"),
        P("dp", "tensor", None),
        P("dp", None, "tensor"),
    )
    out_specs = (P("dp", "tensor"), P("dp", "tensor"))
    return jax.shard_map(
        on_device, mesh=mesh, in_specs=in_specs, out_specs=out_specs, check_vma=False
    )
```

```python
import jax
import jax.numpy as jnp
import numpy as np
from jax import lax
from jax.experimental import pallas as pl
from jax.experimental.pallas import tpu as pltpu
from jax.sharding import PartitionSpec as P

HEAD_SIZE = 128
GROUP = 8
CAPACITY = 2
LANES = 128
ROPE_BASE = 500000.0
MIB = 1 << 20
EARLY_ROWS = 16

F32, BF16, I32 = jnp.float32, jnp.bfloat16, jnp.int32
VMEM = pl.BlockSpec(memory_space=pltpu.VMEM)
SMEM = pl.BlockSpec(memory_space=pltpu.SMEM)
HBM = pl.BlockSpec(memory_space=pltpu.HBM)
ANY = pl.BlockSpec(memory_space=pl.ANY)


def iota(shape, dim):
    return lax.broadcasted_iota(I32, shape, dim)


def dot(a, b):
    return jnp.dot(a, b, preferred_element_type=F32)


def dot_t(a, b):
    return lax.dot_general(a, b, (((1,), (1,)), ((), ())), preferred_element_type=F32)


def upright(row):
    n = row.shape[1]
    spread = jnp.broadcast_to(row, (n, n))
    return jnp.sum(jnp.where(iota((n, n), 0) == iota((n, n), 1), spread, 0.0), axis=1, keepdims=True)


def shuffle(chunks, forward):
    wide = 16 * chunks
    row, col = iota((wide, wide), 0), iota((wide, wide), 1)
    chunked, message = (col, row) if forward else (row, col)
    k, s, c = chunked >> 4, (chunked >> 1) & 7, chunked & 1
    return jnp.where(message == s * (2 * chunks) + k * 2 + c, 1.0, 0.0).astype(BF16)


def slots_of(tenant_row, pool):
    n = tenant_row.shape[1]
    owner_row = jnp.floor(tenant_row * (1.0 / pool))
    owner_col = upright(owner_row)
    same = (owner_col == owner_row) & (iota((n, n), 0) < iota((n, n), 1))
    rank = jnp.sum(jnp.where(same, 1.0, 0.0), axis=0, keepdims=True)
    return owner_row * CAPACITY + rank


def place_kernel(pool, tenant_hbm, hidden_hbm, out_ref, tenant_ref, hidden_ref, sems):
    fetch_hidden = pltpu.make_async_copy(hidden_hbm, hidden_ref, sems.at[0])
    fetch_tenant = pltpu.make_async_copy(tenant_hbm, tenant_ref, sems.at[1])
    fetch_tenant.start()
    fetch_hidden.start()
    rows, width = hidden_ref.shape
    chunks = width // LANES + 1
    slots = out_ref.shape[0] // chunks
    mix = shuffle(chunks, True)
    fetch_tenant.wait()
    tenant_row = tenant_ref[...].astype(F32)
    slot_row = slots_of(tenant_row, pool)
    place = jnp.where(slot_row == iota((slots, rows), 0).astype(F32), 1.0, 0.0).astype(BF16)
    local = tenant_row - pool * jnp.floor(tenant_row * (1.0 / pool))
    local = jnp.broadcast_to(upright(local), (rows, LANES)).astype(BF16)
    fetch_hidden.wait()
    placed = jnp.concatenate([dot(place, hidden_ref[...]), dot(place, local)], axis=1).astype(BF16)
    groups = slots // 16
    side = jnp.concatenate(
        [
            jnp.concatenate(
                [placed[g * 16 : g * 16 + 16, k * LANES : (k + 1) * LANES] for k in range(chunks)], axis=0
            )
            for g in range(groups)
        ],
        axis=1,
    )
    turned = dot(mix, side).astype(BF16)
    wide = 16 * chunks
    for g in range(groups):
        out_ref[g * wide : (g + 1) * wide, :] = turned[:, g * LANES : (g + 1) * LANES]


def down_kernel(got_ref, down_ref, up_hbm, after_ref, partial_ref, ids_ref, up_ref, sem):
    fetch_up = pltpu.make_async_copy(up_hbm, up_ref, sem)
    fetch_up.start()
    slots = ids_ref.shape[0]
    chunks = got_ref.shape[0] // slots
    groups, wide = slots // 16, 16 * chunks
    side = jnp.concatenate([got_ref[g * wide : (g + 1) * wide, :] for g in range(groups)], axis=1)
    turned = dot(shuffle(chunks, False), side)
    ids = jnp.concatenate([turned[wide - 16 :, g * LANES : (g + 1) * LANES] for g in range(groups)], axis=0)
    turned = turned.astype(BF16)
    rows = jnp.concatenate(
        [
            jnp.concatenate(
                [turned[k * 16 : k * 16 + 16, g * LANES : (g + 1) * LANES] for k in range(chunks - 1)], axis=1
            )
            for g in range(groups)
        ],
        axis=0,
    )
    full = dot_t(rows, down_ref[...])
    lane = iota((slots, LANES), 1)
    right = (lane >= 64).astype(F32)
    total = jnp.zeros((slots, LANES), F32)
    for q in range(full.shape[1] // LANES):
        total += jnp.where(ids == right + 2.0 * q, full[:, q * LANES : (q + 1) * LANES], 0.0)
    total = total + pltpu.roll(total, 64, 1)
    half = slots // 2
    partial_ref[...] = jnp.where(lane[:half] < 64, total[:half], total[half:])
    ids_ref[...] = ids
    fetch_up.wait()


def up_kernel(a_ref, b_ref, c_ref, d_ref, ids_ref, up_ref, out_ref):
    total = (a_ref[...] + b_ref[...]) + (c_ref[...] + d_ref[...])
    turned = pltpu.roll(total, 64, 1)
    left = iota(total.shape, 1) < 64
    both = jnp.concatenate([jnp.where(left, total, turned), jnp.where(left, turned, total)], axis=0)
    ids = ids_ref[...]
    right = (iota(ids.shape, 1) >= 64).astype(F32)
    spread = [
        jnp.where(ids == right + 2.0 * q, both, 0.0).astype(BF16) for q in range(up_ref.shape[0] // LANES)
    ]
    out_ref[...] = dot(jnp.concatenate(spread, axis=1), up_ref[...]).astype(BF16)


def attend_cache(scale, first, count, rows, length_at, query_ref, key_ref, value_ref, wait_key, wait_value, sum_ref,
                 top_ref, whole_ref):
    length = key_ref.shape[1]
    wide = count * GROUP
    by_head = jnp.concatenate([query_ref[:, h * LANES : (h + 1) * LANES] for h in range(GROUP)], axis=0)
    row, col = iota((wide, GROUP * rows), 0), iota((wide, GROUP * rows), 1)
    turn = jnp.where(col == (row % GROUP) * rows + row // GROUP + first, 1.0, 0.0).astype(BF16)
    by_row = dot(turn, by_head)
    position = iota((GROUP, length), 1)
    wait_key()
    scores = []
    for r in range(count):
        query = by_row[r * GROUP : (r + 1) * GROUP].astype(BF16)
        score = dot_t(query, key_ref[r]) * scale
        scores.append(jnp.where(position < length_at(first + r), score, -jnp.inf))
    scores = jnp.concatenate(scores, axis=0)
    top = jnp.max(scores, axis=1, keepdims=True)
    weights = jnp.exp(scores - top)
    whole = jnp.broadcast_to(jnp.sum(weights, axis=1, keepdims=True), (wide, LANES))
    top = jnp.broadcast_to(top, (wide, LANES))
    wait_value()
    for r in range(count):
        some = slice(r * GROUP, (r + 1) * GROUP)
        place = pl.ds(r, GROUP, stride=count)
        sum_ref[place, :] = dot(weights[some].astype(BF16), value_ref[r])
        top_ref[place, :] = top[some]
        whole_ref[place, :] = whole[some]


def fetches(pairs, sems):
    copies = [pltpu.make_async_copy(source, target, sems.at[i]) for i, (source, target) in enumerate(pairs)]
    for copy in copies:
        copy.start()
    return copies


def early_kernel(scale, count, after_ref, length_hbm, query_hbm, key_hbm, value_hbm, own_hbm, core_hbm, sum_ref,
                 top_ref, whole_ref, pair_ref, length_ref, query_ref, key_ref, value_ref, sems):
    rows = query_ref.shape[0]
    some = pl.ds(0, count)
    copies = fetches(
        [
            (query_hbm, query_ref), (length_hbm, length_ref), (key_hbm.at[some], key_ref),
            (value_hbm.at[some], value_ref), (own_hbm, pair_ref.at[pl.ds(0, rows)]),
            (core_hbm, pair_ref.at[pl.ds(rows, rows)]),
        ],
        sems,
    )
    copies[0].wait()
    copies[1].wait()
    attend_cache(scale, 0, count, rows, lambda r: length_ref[r], query_ref, key_ref, value_ref, copies[2].wait,
                 copies[3].wait, sum_ref, top_ref, whole_ref)
    copies[4].wait()
    copies[5].wait()


def late_kernel(scale, pool, index_ref, after_ref, tenant_hbm, length_hbm, row_hbm, inverse_hbm, query_hbm, key_hbm,
                value_hbm, own_hbm, core_hbm, y1_hbm, y2_hbm, y3_hbm, weight_hbm, sum_ref, top_ref, whole_ref,
                projected_ref, entry_ref, mixed_ref, share_ref, back_ref, tenant_ref, length_ref, row_ref, inverse_ref,
                query_ref, key_ref, value_ref, own_ref, core_ref, y1_ref, y2_ref, y3_ref, weight_ref, sum2_ref, top2_ref,
                whole2_ref, sems, weight_sems):
    rows, depth = own_ref.shape
    count = key_ref.shape[0]
    first = rows - count
    some = pl.ds(first, count)
    me = index_ref[0]
    devices = weight_ref.shape[0] // depth
    copies = fetches(
        [
            (query_hbm, query_ref), (length_hbm, length_ref), (key_hbm.at[some], key_ref),
            (value_hbm.at[some], value_ref), (tenant_hbm, tenant_ref), (row_hbm, row_ref),
            (inverse_hbm, inverse_ref), (own_hbm, own_ref), (core_hbm, core_ref), (y1_hbm, y1_ref), (y2_hbm, y2_ref),
            (y3_hbm, y3_ref),
        ],
        sems,
    )
    blocks = [pl.ds(k * depth, depth) for k in range(devices)]
    weights = fetches([(weight_hbm.at[block], weight_ref.at[block]) for block in blocks], weight_sems)
    copies[0].wait()
    copies[1].wait()
    attend_cache(scale, first, count, rows, lambda r: length_ref[r], query_ref, key_ref, value_ref, copies[2].wait,
                 copies[3].wait, sum2_ref, top2_ref, whole2_ref)
    for copy in copies[4:] + weights:
        copy.wait()

    def part(block, other):
        start = pl.multiple_of(other * depth, depth)
        return dot(block, weight_ref[pl.ds(start, depth), :])

    total = part(own_ref[...], me) + part(core_ref[...], me ^ 1)
    for shift, ref in ((1, y1_ref), (2, y2_ref), (3, y3_ref)):
        other = (me + devices - 2 * shift) % devices
        total += part(ref[:rows], other) + part(ref[rows:], other ^ 1)
    projected_ref[...] = total[:, LANES:]
    angle = upright(row_ref[...].astype(F32)) * inverse_ref[...]
    lane = iota((rows, LANES), 1)
    sine = jnp.sin(angle)
    key = total[:, :LANES]
    key = key * jnp.cos(angle) + pltpu.roll(key, 64, 1) * jnp.where(lane < 64, -sine, sine)
    key = key.astype(BF16)
    entry_ref[...] = key
    key = key.astype(F32)
    halves = ((0, first, sum_ref, top_ref, whole_ref), (first, count, sum2_ref, top2_ref, whole2_ref))
    for h in range(GROUP):
        query = query_ref[:, h * LANES : (h + 1) * LANES].astype(F32)
        own = jnp.sum(query * key, axis=1, keepdims=True) * scale
        for start, many, sums, tops, wholes in halves:
            if many:
                here, place = slice(h * many, (h + 1) * many), slice(h * rows + start, h * rows + start + many)
                mine, top = own[start : start + many], tops[here, :]
                highest = jnp.maximum(top, mine)
                old, new = jnp.exp(top - highest), jnp.exp(mine - highest)
                under = 1.0 / (old * wholes[here, :] + new)
                mixed_ref[place, :] = sums[here, :] * (old * under)
                share_ref[place, :] = new * under
    slot_col = upright(slots_of(tenant_ref[...].astype(F32), pool))
    back_ref[...] = jnp.where(slot_col == lane.astype(F32), 1.0, 0.0).astype(BF16)


def final_kernel(got_ref, back_ref, value_ref, key_ref, mixed_ref, share_ref, out_ref, entry_ref):
    rows = value_ref.shape[0]
    slots = got_ref.shape[0]
    delta = dot(back_ref[:, :slots], got_ref[...])
    value = (value_ref[...] + delta).astype(BF16)
    entry_ref[:, :LANES] = key_ref[...]
    entry_ref[:, LANES:] = value
    value = value.astype(F32)
    for h in range(GROUP):
        place = slice(h * rows, (h + 1) * rows)
        out_ref[:, h * LANES : (h + 1) * LANES] = (mixed_ref[place, :] + share_ref[place, :] * value).astype(BF16)


def on_device(hidden, queries, key_cache, value_cache, lengths, tenants, weight, down, up):
    rows, depth = hidden.shape
    peers = lax.axis_size("dp")
    count = lax.axis_size("tensor")
    slots = peers * CAPACITY
    pool, _, rank = down.shape
    chunks = depth // LANES + 1
    length = key_cache.shape[1]
    scale = HEAD_SIZE ** -0.5
    early = EARLY_ROWS
    late = rows - early
    shape, vmem, dma = jax.ShapeDtypeStruct, pltpu.VMEM, pltpu.SemaphoreType.DMA
    params = lambda size: pltpu.CompilerParams(vmem_limit_bytes=size * MIB)
    far = lambda *arrays: [pltpu.with_memory_space_constraint(x, pltpu.HBM) for x in arrays]
    cost = lambda flops, size: pl.CostEstimate(flops=flops, bytes_accessed=size, transcendentals=0)

    tenant_row = tenants.reshape(1, rows)
    length_row = lengths.reshape(1, rows)
    me = lax.axis_index("tensor").astype(I32).reshape(1)
    over_core = lambda x: lax.ppermute(x, "tensor", [(i, i ^ 1) for i in range(count)])
    over_y = lambda x, k: lax.ppermute(x, "tensor", [(i, (i + 2 * k) % count) for i in range(count)])
    states = lambda n: [shape((GROUP * n, LANES), F32)] * 3
    cache = lambda n: [vmem((n, length, LANES), BF16)] * 2

    with jax.named_scope("place"):
        placed = pl.pallas_call(
            lambda *refs: place_kernel(pool, *refs),
            out_shape=shape((slots * chunks, LANES), BF16),
            in_specs=[HBM] * 2, out_specs=VMEM, compiler_params=params(8),
            scratch_shapes=[vmem((1, rows), I32), vmem((rows, depth), BF16), dma((2,))],
        )(*far(tenant_row, hidden))
    with jax.named_scope("rows_to_owners"):
        got = lax.all_to_all(
            placed.reshape(peers, chunks, CAPACITY, LANES), "dp", split_axis=0, concat_axis=0, tiled=True
        ).reshape(slots * chunks, LANES)
    with jax.named_scope("early"):
        core_hidden = over_core(hidden)
        *first_state, pair = pl.pallas_call(
            lambda *refs: early_kernel(scale, early, *refs),
            out_shape=states(early) + [shape((2 * rows, depth), BF16)],
            in_specs=[ANY] + [HBM] * 6,
            out_specs=[VMEM] * 4,
            scratch_shapes=[pltpu.SMEM((rows,), I32), vmem((rows, GROUP * LANES), BF16)] + cache(early) + [dma((6,))],
            compiler_params=params(12),
            cost_estimate=cost(4 * early * GROUP * length * LANES, 4 * early * length * LANES),
        )(placed, *far(lengths, queries, key_cache, value_cache, hidden, core_hidden))
    with jax.named_scope("gather_hidden"):
        others = [over_y(pair, k) for k in (1, 2, 3)]
    with jax.named_scope("down"):
        partial, ids, up_near = pl.pallas_call(
            down_kernel,
            out_shape=[
                shape((slots // 2, LANES), F32), shape((slots, LANES), F32), shape((pool * rank, LANES), BF16)
            ],
            in_specs=[VMEM] * 2 + [HBM, ANY], out_specs=[VMEM] * 3, compiler_params=params(16),
            scratch_shapes=[dma],
        )(got, jnp.swapaxes(down, 1, 2).reshape(pool * rank, depth), *far(up.reshape(pool * rank, LANES)), first_state[0])
    with jax.named_scope("reduce"):
        pair_sum = partial + over_core(partial)
        sums_y = [over_y(pair_sum, k) for k in (1, 2, 3)]
    with jax.named_scope("up"):
        served = pl.pallas_call(
            up_kernel, out_shape=shape((slots, LANES), BF16),
            in_specs=[VMEM] * 6, out_specs=VMEM, compiler_params=params(8),
        )(pair_sum, *sums_y, ids, up_near)
    with jax.named_scope("answers"):
        returned = lax.all_to_all(
            served.reshape(peers, CAPACITY, LANES), "dp", split_axis=0, concat_axis=0, tiled=True
        ).reshape(slots, LANES)
    with jax.named_scope("late"):
        inverse = ROPE_BASE ** (-(np.arange(HEAD_SIZE // 2, dtype=np.float32) * 2.0) / HEAD_SIZE)
        inverse = jnp.asarray(np.concatenate([inverse, inverse])[None, :], F32)
        block = vmem((rows, depth), BF16)
        value, key, mixed, share, back = pl.pallas_call(
            lambda *refs: late_kernel(scale, pool, *refs),
            out_shape=[
                shape((rows, LANES), F32), shape((rows, LANES), BF16),
                shape((GROUP * rows, LANES), F32), shape((GROUP * rows, LANES), F32),
                shape((rows, LANES), BF16),
            ],
            in_specs=[SMEM, ANY] + [HBM] * 13 + [VMEM] * 3, out_specs=[VMEM] * 5,
            scratch_shapes=[
                vmem((1, rows), I32), pltpu.SMEM((rows,), I32), vmem((1, rows), I32), vmem((1, LANES), F32),
                vmem((rows, GROUP * LANES), BF16),
            ] + cache(late) + [block] * 2 + [vmem((2 * rows, depth), BF16)] * 3 + [
                vmem((count * depth, 2 * LANES), BF16)
            ] + [vmem((GROUP * late, LANES), F32)] * 3 + [dma((12,)), dma((count,))],
            compiler_params=params(20),
            cost_estimate=cost(2 * rows * count * depth * 2 * LANES, weight.size * 2),
        )(me, served, *far(tenant_row, lengths, length_row, inverse, queries, key_cache, value_cache, hidden, core_hidden,
                          *others, weight), *first_state)
    with jax.named_scope("finish"):
        return tuple(pl.pallas_call(
            final_kernel,
            out_shape=[shape((rows, GROUP * LANES), BF16), shape((rows, 2 * LANES), BF16)],
            in_specs=[VMEM] * 6, out_specs=[VMEM] * 2, compiler_params=params(8),
        )(returned, back, value, key, mixed, share))


def solution(mesh):
    in_specs = (
        P("dp", "tensor"),
        P("dp", "tensor"),
        P("dp", None, "tensor"),
        P("dp", None, "tensor"),
        P("dp"),
        P("dp"),
        P(None, "tensor"),
        P("dp", "tensor", None),
        P("dp", None, "tensor"),
    )
    out_specs = (P("dp", "tensor"), P("dp", "tensor"))
    return jax.shard_map(
        on_device, mesh=mesh, in_specs=in_specs, out_specs=out_specs, check_vma=False
    )
```

```python
import jax
import jax.numpy as jnp
import numpy as np
from jax import lax
from jax.experimental import pallas as pl
from jax.experimental.pallas import tpu as pltpu
from jax.sharding import PartitionSpec as P

HEAD_SIZE = 128
GROUP = 8
CAPACITY = 2
LANES = 128
ROPE_BASE = 500000.0
MIB = 1 << 20
EARLY_ROWS = 16

F32, BF16, I32 = jnp.float32, jnp.bfloat16, jnp.int32
VMEM = pl.BlockSpec(memory_space=pltpu.VMEM)
SMEM = pl.BlockSpec(memory_space=pltpu.SMEM)
HBM = pl.BlockSpec(memory_space=pltpu.HBM)
ANY = pl.BlockSpec(memory_space=pl.ANY)


def iota(shape, dim):
    return lax.broadcasted_iota(I32, shape, dim)


def dot(a, b):
    return jnp.dot(a, b, preferred_element_type=F32)


def dot_t(a, b):
    return lax.dot_general(a, b, (((1,), (1,)), ((), ())), preferred_element_type=F32)


def upright(row):
    n = row.shape[1]
    spread = jnp.broadcast_to(row, (n, n))
    return jnp.sum(jnp.where(iota((n, n), 0) == iota((n, n), 1), spread, 0.0), axis=1, keepdims=True)


def shuffle(chunks, forward):
    wide = 16 * chunks
    row, col = iota((wide, wide), 0), iota((wide, wide), 1)
    chunked, message = (col, row) if forward else (row, col)
    k, s, c = chunked >> 4, (chunked >> 1) & 7, chunked & 1
    return jnp.where(message == s * (2 * chunks) + k * 2 + c, 1.0, 0.0).astype(BF16)


def slots_of(tenant_row, pool):
    n = tenant_row.shape[1]
    owner_row = jnp.floor(tenant_row * (1.0 / pool))
    owner_col = upright(owner_row)
    same = (owner_col == owner_row) & (iota((n, n), 0) < iota((n, n), 1))
    rank = jnp.sum(jnp.where(same, 1.0, 0.0), axis=0, keepdims=True)
    return owner_row * CAPACITY + rank


def fetches(pairs, sems):
    copies = [pltpu.make_async_copy(source, target, sems.at[i]) for i, (source, target) in enumerate(pairs)]
    for copy in copies:
        copy.start()
    return copies


def place_kernel(pool, tenant_hbm, hidden_hbm, out_ref, hidden_ref, tenant_ref, sems):
    fetch_hidden = pltpu.make_async_copy(hidden_hbm, hidden_ref, sems.at[0])
    fetch_tenant = pltpu.make_async_copy(tenant_hbm, tenant_ref, sems.at[1])
    fetch_tenant.start()
    fetch_hidden.start()
    rows, width = hidden_ref.shape
    chunks = width // LANES + 1
    slots = out_ref.shape[0] // chunks
    mix = shuffle(chunks, True)
    fetch_tenant.wait()
    tenant_row = tenant_ref[...].astype(F32)
    slot_row = slots_of(tenant_row, pool)
    place = jnp.where(slot_row == iota((slots, rows), 0).astype(F32), 1.0, 0.0).astype(BF16)
    local = tenant_row - pool * jnp.floor(tenant_row * (1.0 / pool))
    local = jnp.broadcast_to(upright(local), (rows, LANES)).astype(BF16)
    fetch_hidden.wait()
    placed = jnp.concatenate([dot(place, hidden_ref[...]), dot(place, local)], axis=1).astype(BF16)
    groups = slots // 16
    side = jnp.concatenate(
        [
            jnp.concatenate(
                [placed[g * 16 : g * 16 + 16, k * LANES : (k + 1) * LANES] for k in range(chunks)], axis=0
            )
            for g in range(groups)
        ],
        axis=1,
    )
    turned = dot(mix, side).astype(BF16)
    wide = 16 * chunks
    for g in range(groups):
        out_ref[g * wide : (g + 1) * wide, :] = turned[:, g * LANES : (g + 1) * LANES]


def down_kernel(got_ref, down_ref, up_hbm, after_ref, own_any, y1_any, y2_any, y3_any, partial_ref, ids_ref, up_ref,
                quad_hbm, sems):
    rows = own_any.shape[0]
    copies = fetches(
        [(up_hbm, up_ref)]
        + [(block, quad_hbm.at[pl.ds(k * rows, rows)]) for k, block in enumerate((own_any, y1_any, y2_any, y3_any))],
        sems,
    )
    slots = ids_ref.shape[0]
    chunks = got_ref.shape[0] // slots
    groups, wide = slots // 16, 16 * chunks
    side = jnp.concatenate([got_ref[g * wide : (g + 1) * wide, :] for g in range(groups)], axis=1)
    turned = dot(shuffle(chunks, False), side)
    ids = jnp.concatenate([turned[wide - 16 :, g * LANES : (g + 1) * LANES] for g in range(groups)], axis=0)
    turned = turned.astype(BF16)
    rows = jnp.concatenate(
        [
            jnp.concatenate(
                [turned[k * 16 : k * 16 + 16, g * LANES : (g + 1) * LANES] for k in range(chunks - 1)], axis=1
            )
            for g in range(groups)
        ],
        axis=0,
    )
    full = dot_t(rows, down_ref[...])
    lane = iota((slots, LANES), 1)
    right = (lane >= 64).astype(F32)
    total = jnp.zeros((slots, LANES), F32)
    for q in range(full.shape[1] // LANES):
        total += jnp.where(ids == right + 2.0 * q, full[:, q * LANES : (q + 1) * LANES], 0.0)
    total = total + pltpu.roll(total, 64, 1)
    half = slots // 2
    partial_ref[...] = jnp.where(lane[:half] < 64, total[:half], total[half:])
    ids_ref[...] = ids
    for copy in copies:
        copy.wait()


def up_kernel(after_ref, a_ref, b_ref, c_ref, d_ref, ids_ref, up_ref, out_ref):
    total = (a_ref[...] + b_ref[...]) + (c_ref[...] + d_ref[...])
    turned = pltpu.roll(total, 64, 1)
    left = iota(total.shape, 1) < 64
    both = jnp.concatenate([jnp.where(left, total, turned), jnp.where(left, turned, total)], axis=0)
    ids = ids_ref[...]
    right = (iota(ids.shape, 1) >= 64).astype(F32)
    spread = [
        jnp.where(ids == right + 2.0 * q, both, 0.0).astype(BF16) for q in range(up_ref.shape[0] // LANES)
    ]
    out_ref[...] = dot(jnp.concatenate(spread, axis=1), up_ref[...]).astype(BF16)


def attend_cache(scale, first, count, rows, length_at, query_ref, key_ref, value_ref, wait_key, wait_value, sum_ref,
                 top_ref, whole_ref):
    length = key_ref.shape[1]
    wide = count * GROUP
    by_head = jnp.concatenate([query_ref[:, h * LANES : (h + 1) * LANES] for h in range(GROUP)], axis=0)
    row, col = iota((wide, GROUP * rows), 0), iota((wide, GROUP * rows), 1)
    turn = jnp.where(col == (row % GROUP) * rows + row // GROUP + first, 1.0, 0.0).astype(BF16)
    by_row = dot(turn, by_head)
    position = iota((GROUP, length), 1)
    wait_key()
    scores = []
    for r in range(count):
        query = by_row[r * GROUP : (r + 1) * GROUP].astype(BF16)
        score = dot_t(query, key_ref[r]) * scale
        scores.append(jnp.where(position < length_at(first + r), score, -jnp.inf))
    scores = jnp.concatenate(scores, axis=0)
    top = jnp.max(scores, axis=1, keepdims=True)
    weights = jnp.exp(scores - top)
    whole = jnp.broadcast_to(jnp.sum(weights, axis=1, keepdims=True), (wide, LANES))
    top = jnp.broadcast_to(top, (wide, LANES))
    wait_value()
    for r in range(count):
        some = slice(r * GROUP, (r + 1) * GROUP)
        place = pl.ds(r, GROUP, stride=count)
        sum_ref[place, :] = dot(weights[some].astype(BF16), value_ref[r])
        top_ref[place, :] = top[some]
        whole_ref[place, :] = whole[some]


def cache_kernel(scale, first, after_ref, length_hbm, query_hbm, key_hbm, value_hbm, sum_ref, top_ref, whole_ref,
                 length_ref, query_ref, key_ref, value_ref, sems):
    rows, count = query_ref.shape[0], key_ref.shape[0]
    some = pl.ds(first, count)
    copies = fetches(
        [
            (query_hbm, query_ref), (length_hbm, length_ref), (key_hbm.at[some], key_ref),
            (value_hbm.at[some], value_ref),
        ],
        sems,
    )
    copies[0].wait()
    copies[1].wait()
    attend_cache(scale, first, count, rows, lambda r: length_ref[r], query_ref, key_ref, value_ref, copies[2].wait,
                 copies[3].wait, sum_ref, top_ref, whole_ref)


def late_kernel(scale, pool, index_ref, after_ref, tenant_hbm, row_hbm, inverse_hbm, query_hbm, near_hbm, far_hbm,
                weight_hbm, *refs):
    state_refs, refs = refs[:6], refs[6:]
    (projected_ref, entry_ref, mixed_ref, share_ref, back_ref, tenant_ref, row_ref, inverse_ref, query_ref, near_ref,
     far_ref, weight_ref, sems, weight_sems) = refs
    rows, depth = query_ref.shape[0], near_ref.shape[1]
    first = state_refs[0].shape[0] // GROUP
    me = index_ref[0]
    devices = weight_ref.shape[0] // depth
    copies = fetches(
        [
            (near_hbm, near_ref), (far_hbm, far_ref), (query_hbm, query_ref), (tenant_hbm, tenant_ref),
            (row_hbm, row_ref), (inverse_hbm, inverse_ref),
        ],
        sems,
    )
    blocks = [pl.ds(k * depth, depth) for k in range(devices)]
    weights = fetches([(weight_hbm.at[block], weight_ref.at[block]) for block in blocks], weight_sems)
    for copy in copies:
        copy.wait()
    slot_col = upright(slots_of(tenant_ref[...].astype(F32), pool))
    lane = iota((rows, LANES), 1)
    back_ref[...] = jnp.where(slot_col == lane.astype(F32), 1.0, 0.0).astype(BF16)
    angle = upright(row_ref[...].astype(F32)) * inverse_ref[...]
    sine, cosine = jnp.sin(angle), jnp.cos(angle)
    for copy in weights:
        copy.wait()

    def part(block, other):
        start = pl.multiple_of(other * depth, depth)
        return dot(block, weight_ref[pl.ds(start, depth), :])

    total = jnp.zeros((rows, 2 * LANES), F32)
    for shift in range(devices // 2):
        other = (me + devices - 2 * shift) % devices
        block = slice(shift * rows, (shift + 1) * rows)
        total += part(near_ref[block], other) + part(far_ref[block], other ^ 1)
    projected_ref[...] = total[:, LANES:]
    key = total[:, :LANES]
    key = key * cosine + pltpu.roll(key, 64, 1) * jnp.where(lane < 64, -sine, sine)
    key = key.astype(BF16)
    entry_ref[...] = key
    key = key.astype(F32)
    halves = ((0, first, state_refs[:3]), (first, rows - first, state_refs[3:]))
    for h in range(GROUP):
        query = query_ref[:, h * LANES : (h + 1) * LANES].astype(F32)
        own = jnp.sum(query * key, axis=1, keepdims=True) * scale
        for start, many, (sums, tops, wholes) in halves:
            here, place = slice(h * many, (h + 1) * many), slice(h * rows + start, h * rows + start + many)
            mine, top = own[start : start + many], tops[here, :]
            highest = jnp.maximum(top, mine)
            old, new = jnp.exp(top - highest), jnp.exp(mine - highest)
            under = 1.0 / (old * wholes[here, :] + new)
            mixed_ref[place, :] = sums[here, :] * (old * under)
            share_ref[place, :] = new * under


def final_kernel(got_ref, back_ref, value_ref, key_ref, mixed_ref, share_ref, out_ref, entry_ref):
    rows = value_ref.shape[0]
    slots = got_ref.shape[0]
    delta = dot(back_ref[:, :slots], got_ref[...])
    value = (value_ref[...] + delta).astype(BF16)
    entry_ref[:, :LANES] = key_ref[...]
    entry_ref[:, LANES:] = value
    value = value.astype(F32)
    for h in range(GROUP):
        place = slice(h * rows, (h + 1) * rows)
        out_ref[:, h * LANES : (h + 1) * LANES] = (mixed_ref[place, :] + share_ref[place, :] * value).astype(BF16)


def on_device(hidden, queries, key_cache, value_cache, lengths, tenants, weight, down, up):
    rows, depth = hidden.shape
    peers = lax.axis_size("dp")
    count = lax.axis_size("tensor")
    slots = peers * CAPACITY
    pool, _, rank = down.shape
    chunks = depth // LANES + 1
    length = key_cache.shape[1]
    scale = HEAD_SIZE ** -0.5
    early = EARLY_ROWS
    late = rows - early
    shape, vmem, dma = jax.ShapeDtypeStruct, pltpu.VMEM, pltpu.SemaphoreType.DMA
    params = lambda size: pltpu.CompilerParams(vmem_limit_bytes=size * MIB)
    far = lambda *arrays: [pltpu.with_memory_space_constraint(x, pltpu.HBM) for x in arrays]
    cost = lambda flops, size: pl.CostEstimate(flops=flops, bytes_accessed=size, transcendentals=0)

    tenant_row = tenants.reshape(1, rows)
    length_row = lengths.reshape(1, rows)
    me = lax.axis_index("tensor").astype(I32).reshape(1)
    over_core = lambda x: lax.ppermute(x, "tensor", [(i, i ^ 1) for i in range(count)])
    over_y = lambda x, k: lax.ppermute(x, "tensor", [(i, (i + 2 * k) % count) for i in range(count)])
    states = lambda n: [shape((GROUP * n, LANES), F32)] * 3

    def attend(first, many, after):
        return pl.pallas_call(
            lambda *refs: cache_kernel(scale, first, *refs),
            out_shape=states(many),
            in_specs=[ANY] + [HBM] * 4,
            out_specs=[VMEM] * 3,
            scratch_shapes=[pltpu.SMEM((rows,), I32), vmem((rows, GROUP * LANES), BF16)]
            + [vmem((many, length, LANES), BF16)] * 2 + [dma((4,))],
            compiler_params=params(12),
            cost_estimate=cost(4 * many * GROUP * length * LANES, 4 * many * length * LANES),
        )(after, *far(lengths, queries, key_cache, value_cache))

    with jax.named_scope("place"):
        placed, handed = pl.pallas_call(
            lambda *refs: place_kernel(pool, *refs),
            out_shape=[shape((slots * chunks, LANES), BF16), shape((rows, depth), BF16)],
            in_specs=[HBM] * 2, out_specs=[VMEM] * 2, compiler_params=params(8),
            scratch_shapes=[vmem((1, rows), I32), dma((2,))],
        )(*far(tenant_row, hidden))
    with jax.named_scope("rows_to_owners"):
        got = lax.all_to_all(
            placed.reshape(peers, chunks, CAPACITY, LANES), "dp", split_axis=0, concat_axis=0, tiled=True
        ).reshape(slots * chunks, LANES)
    with jax.named_scope("gather_hidden"):
        others = [over_y(handed, k) for k in (1, 2, 3)]
    with jax.named_scope("early"):
        first_state = attend(0, early, placed)
    with jax.named_scope("down"):
        partial, ids, up_near, near = pl.pallas_call(
            down_kernel,
            out_shape=[
                shape((slots // 2, LANES), F32), shape((slots, LANES), F32), shape((pool * rank, LANES), BF16),
                shape((4 * rows, depth), BF16),
            ],
            in_specs=[VMEM] * 2 + [HBM] + [ANY] * 5, out_specs=[VMEM] * 3 + [ANY], compiler_params=params(16),
            scratch_shapes=[dma((5,))],
        )(got, jnp.swapaxes(down, 1, 2).reshape(pool * rank, depth), *far(up.reshape(pool * rank, LANES)),
          first_state[0], handed, *others)
    with jax.named_scope("reduce"):
        pair_sum = partial + over_core(partial)
        sums_y = [over_y(pair_sum, k) for k in (1, 2, 3)]
    with jax.named_scope("middle"):
        second_state = attend(early, late, pair_sum)
    with jax.named_scope("gather_core"):
        other = over_core(near)
    with jax.named_scope("up"):
        served = pl.pallas_call(
            up_kernel, out_shape=shape((slots, LANES), BF16),
            in_specs=[ANY] + [VMEM] * 6, out_specs=VMEM, compiler_params=params(8),
        )(second_state[0], pair_sum, *sums_y, ids, up_near)
    with jax.named_scope("answers"):
        returned = lax.all_to_all(
            served.reshape(peers, CAPACITY, LANES), "dp", split_axis=0, concat_axis=0, tiled=True
        ).reshape(slots, LANES)
    with jax.named_scope("late"):
        inverse = ROPE_BASE ** (-(np.arange(HEAD_SIZE // 2, dtype=np.float32) * 2.0) / HEAD_SIZE)
        inverse = jnp.asarray(np.concatenate([inverse, inverse])[None, :], F32)
        value, key, mixed, share, back = pl.pallas_call(
            lambda *refs: late_kernel(scale, pool, *refs),
            out_shape=[
                shape((rows, LANES), F32), shape((rows, LANES), BF16),
                shape((GROUP * rows, LANES), F32), shape((GROUP * rows, LANES), F32),
                shape((rows, LANES), BF16),
            ],
            in_specs=[SMEM, ANY] + [HBM] * 4 + [ANY] * 2 + [HBM] + [VMEM] * 6, out_specs=[VMEM] * 5,
            scratch_shapes=[
                vmem((1, rows), I32), vmem((1, rows), I32), vmem((1, LANES), F32),
                vmem((rows, GROUP * LANES), BF16), vmem((4 * rows, depth), BF16), vmem((4 * rows, depth), BF16),
                vmem((count * depth, 2 * LANES), BF16), dma((6,)), dma((count,)),
            ],
            compiler_params=params(12),
            cost_estimate=cost(2 * rows * count * depth * 2 * LANES, weight.size * 2),
        )(me, served, *far(tenant_row, length_row, inverse, queries), near, other, *far(weight), *first_state,
          *second_state)
    with jax.named_scope("finish"):
        return tuple(pl.pallas_call(
            final_kernel,
            out_shape=[shape((rows, GROUP * LANES), BF16), shape((rows, 2 * LANES), BF16)],
            in_specs=[VMEM] * 6, out_specs=[VMEM] * 2, compiler_params=params(8),
        )(returned, back, value, key, mixed, share))


def solution(mesh):
    in_specs = (
        P("dp", "tensor"),
        P("dp", "tensor"),
        P("dp", None, "tensor"),
        P("dp", None, "tensor"),
        P("dp"),
        P("dp"),
        P(None, "tensor"),
        P("dp", "tensor", None),
        P("dp", None, "tensor"),
    )
    out_specs = (P("dp", "tensor"), P("dp", "tensor"))
    return jax.shard_map(
        on_device, mesh=mesh, in_specs=in_specs, out_specs=out_specs, check_vma=False
    )
```

```python
import jax
import jax.numpy as jnp
import numpy as np
from jax import lax
from jax.experimental import pallas as pl
from jax.experimental.pallas import tpu as pltpu
from jax.sharding import PartitionSpec as P

HEAD_SIZE = 128
GROUP = 8
CAPACITY = 2
LANES = 128
ROPE_BASE = 500000.0
MIB = 1 << 20
EARLY_ROWS = 16

F32, BF16, I32 = jnp.float32, jnp.bfloat16, jnp.int32
VMEM = pl.BlockSpec(memory_space=pltpu.VMEM)
SMEM = pl.BlockSpec(memory_space=pltpu.SMEM)
HBM = pl.BlockSpec(memory_space=pltpu.HBM)
ANY = pl.BlockSpec(memory_space=pl.ANY)


def iota(shape, dim):
    return lax.broadcasted_iota(I32, shape, dim)


def dot(a, b):
    return jnp.dot(a, b, preferred_element_type=F32)


def dot_t(a, b):
    return lax.dot_general(a, b, (((1,), (1,)), ((), ())), preferred_element_type=F32)


def upright(row):
    n = row.shape[1]
    spread = jnp.broadcast_to(row, (n, n))
    return jnp.sum(jnp.where(iota((n, n), 0) == iota((n, n), 1), spread, 0.0), axis=1, keepdims=True)


def shuffle(chunks, forward):
    wide = 16 * chunks
    row, col = iota((wide, wide), 0), iota((wide, wide), 1)
    chunked, message = (col, row) if forward else (row, col)
    k, s, c = chunked >> 4, (chunked >> 1) & 7, chunked & 1
    return jnp.where(message == s * (2 * chunks) + k * 2 + c, 1.0, 0.0).astype(BF16)


def slots_of(tenant_row, pool):
    n = tenant_row.shape[1]
    owner_row = jnp.floor(tenant_row * (1.0 / pool))
    owner_col = upright(owner_row)
    same = (owner_col == owner_row) & (iota((n, n), 0) < iota((n, n), 1))
    rank = jnp.sum(jnp.where(same, 1.0, 0.0), axis=0, keepdims=True)
    return owner_row * CAPACITY + rank


def fetches(pairs, sems):
    copies = [pltpu.make_async_copy(source, target, sems.at[i]) for i, (source, target) in enumerate(pairs)]
    for copy in copies:
        copy.start()
    return copies


def place_kernel(pool, tenant_hbm, hidden_hbm, out_ref, hidden_ref, tenant_ref, sems):
    fetch_hidden = pltpu.make_async_copy(hidden_hbm, hidden_ref, sems.at[0])
    fetch_tenant = pltpu.make_async_copy(tenant_hbm, tenant_ref, sems.at[1])
    fetch_tenant.start()
    fetch_hidden.start()
    rows, width = hidden_ref.shape
    chunks = width // LANES + 1
    slots = out_ref.shape[0] // chunks
    mix = shuffle(chunks, True)
    fetch_tenant.wait()
    tenant_row = tenant_ref[...].astype(F32)
    slot_row = slots_of(tenant_row, pool)
    place = jnp.where(slot_row == iota((slots, rows), 0).astype(F32), 1.0, 0.0).astype(BF16)
    local = tenant_row - pool * jnp.floor(tenant_row * (1.0 / pool))
    local = jnp.broadcast_to(upright(local), (rows, LANES)).astype(BF16)
    fetch_hidden.wait()
    placed = jnp.concatenate([dot(place, hidden_ref[...]), dot(place, local)], axis=1).astype(BF16)
    groups = slots // 16
    side = jnp.concatenate(
        [
            jnp.concatenate(
                [placed[g * 16 : g * 16 + 16, k * LANES : (k + 1) * LANES] for k in range(chunks)], axis=0
            )
            for g in range(groups)
        ],
        axis=1,
    )
    turned = dot(mix, side).astype(BF16)
    wide = 16 * chunks
    for g in range(groups):
        out_ref[g * wide : (g + 1) * wide, :] = turned[:, g * LANES : (g + 1) * LANES]


def down_kernel(got_ref, down_ref, up_hbm, after_ref, partial_ref, ids_ref, up_ref, sem):
    fetch_up = pltpu.make_async_copy(up_hbm, up_ref, sem)
    fetch_up.start()
    slots = ids_ref.shape[0]
    chunks = got_ref.shape[0] // slots
    groups, wide = slots // 16, 16 * chunks
    side = jnp.concatenate([got_ref[g * wide : (g + 1) * wide, :] for g in range(groups)], axis=1)
    turned = dot(shuffle(chunks, False), side)
    ids = jnp.concatenate([turned[wide - 16 :, g * LANES : (g + 1) * LANES] for g in range(groups)], axis=0)
    turned = turned.astype(BF16)
    rows = jnp.concatenate(
        [
            jnp.concatenate(
                [turned[k * 16 : k * 16 + 16, g * LANES : (g + 1) * LANES] for k in range(chunks - 1)], axis=1
            )
            for g in range(groups)
        ],
        axis=0,
    )
    full = dot_t(rows, down_ref[...])
    lane = iota((slots, LANES), 1)
    right = (lane >= 64).astype(F32)
    total = jnp.zeros((slots, LANES), F32)
    for q in range(full.shape[1] // LANES):
        total += jnp.where(ids == right + 2.0 * q, full[:, q * LANES : (q + 1) * LANES], 0.0)
    total = total + pltpu.roll(total, 64, 1)
    half = slots // 2
    partial_ref[...] = jnp.where(lane[:half] < 64, total[:half], total[half:])
    ids_ref[...] = ids
    fetch_up.wait()


def up_kernel(after_ref, a_ref, b_ref, c_ref, d_ref, ids_ref, up_ref, out_ref):
    total = (a_ref[...] + b_ref[...]) + (c_ref[...] + d_ref[...])
    turned = pltpu.roll(total, 64, 1)
    left = iota(total.shape, 1) < 64
    both = jnp.concatenate([jnp.where(left, total, turned), jnp.where(left, turned, total)], axis=0)
    ids = ids_ref[...]
    right = (iota(ids.shape, 1) >= 64).astype(F32)
    spread = [
        jnp.where(ids == right + 2.0 * q, both, 0.0).astype(BF16) for q in range(up_ref.shape[0] // LANES)
    ]
    out_ref[...] = dot(jnp.concatenate(spread, axis=1), up_ref[...]).astype(BF16)


def attend_cache(scale, first, count, rows, length_at, query_ref, key_ref, value_ref, wait_key, wait_value, sum_ref,
                 top_ref, whole_ref):
    length = key_ref.shape[1]
    wide = count * GROUP
    by_head = jnp.concatenate([query_ref[:, h * LANES : (h + 1) * LANES] for h in range(GROUP)], axis=0)
    row, col = iota((wide, GROUP * rows), 0), iota((wide, GROUP * rows), 1)
    turn = jnp.where(col == (row % GROUP) * rows + row // GROUP + first, 1.0, 0.0).astype(BF16)
    by_row = dot(turn, by_head)
    position = iota((GROUP, length), 1)
    wait_key()
    scores = []
    for r in range(count):
        query = by_row[r * GROUP : (r + 1) * GROUP].astype(BF16)
        score = dot_t(query, key_ref[r]) * scale
        scores.append(jnp.where(position < length_at(first + r), score, -jnp.inf))
    scores = jnp.concatenate(scores, axis=0)
    top = jnp.max(scores, axis=1, keepdims=True)
    weights = jnp.exp(scores - top)
    whole = jnp.broadcast_to(jnp.sum(weights, axis=1, keepdims=True), (wide, LANES))
    top = jnp.broadcast_to(top, (wide, LANES))
    wait_value()
    for r in range(count):
        some = slice(r * GROUP, (r + 1) * GROUP)
        place = pl.ds(r, GROUP, stride=count)
        sum_ref[place, :] = dot(weights[some].astype(BF16), value_ref[r])
        top_ref[place, :] = top[some]
        whole_ref[place, :] = whole[some]


def early_kernel(scale, after_ref, length_hbm, query_hbm, key_hbm, value_hbm, sum_ref, top_ref, whole_ref, length_ref,
                 query_ref, key_ref, value_ref, sems):
    rows, count = query_ref.shape[0], key_ref.shape[0]
    some = pl.ds(0, count)
    copies = fetches(
        [
            (query_hbm, query_ref), (length_hbm, length_ref), (key_hbm.at[some], key_ref),
            (value_hbm.at[some], value_ref),
        ],
        sems,
    )
    copies[0].wait()
    copies[1].wait()
    attend_cache(scale, 0, count, rows, lambda r: length_ref[r], query_ref, key_ref, value_ref, copies[2].wait,
                 copies[3].wait, sum_ref, top_ref, whole_ref)


def middle_kernel(scale, pool, after_ref, length_hbm, query_hbm, key_hbm, value_hbm, tenant_hbm, row_hbm, inverse_hbm,
                  weight_hbm, sum_ref, top_ref, whole_ref, weight_ref,
                  query_ref, cosine_ref, sine_ref, back_ref, length_ref, key_ref, value_ref, tenant_ref, row_ref,
                  inverse_ref, sems):
    rows, count = query_ref.shape[0], key_ref.shape[0]
    some = pl.ds(rows - count, count)
    copies = fetches(
        [
            (query_hbm, query_ref), (length_hbm, length_ref), (tenant_hbm, tenant_ref), (row_hbm, row_ref),
            (inverse_hbm, inverse_ref), (key_hbm.at[some], key_ref), (value_hbm.at[some], value_ref),
            (weight_hbm, weight_ref),
        ],
        sems,
    )
    for copy in copies[:5]:
        copy.wait()
    lane = iota((rows, LANES), 1)
    slot_col = upright(slots_of(tenant_ref[...].astype(F32), pool))
    back_ref[...] = jnp.where(slot_col == lane.astype(F32), 1.0, 0.0).astype(BF16)
    angle = upright(row_ref[...].astype(F32)) * inverse_ref[...]
    sine = jnp.sin(angle)
    cosine_ref[...] = jnp.cos(angle)
    sine_ref[...] = jnp.where(lane < 64, -sine, sine)
    attend_cache(scale, rows - count, count, rows, lambda r: length_ref[r], query_ref, key_ref, value_ref,
                 copies[5].wait, copies[6].wait, sum_ref, top_ref, whole_ref)
    for copy in copies[7:]:
        copy.wait()


def join_kernel(after_ref, own_any, y1_any, y2_any, y3_any, near_ref, sems):
    rows = own_any.shape[0]
    blocks = enumerate((own_any, y1_any, y2_any, y3_any))
    for copy in fetches([(block, near_ref.at[pl.ds(k * rows, rows)]) for k, block in blocks], sems):
        copy.wait()


def late_kernel(scale, index_ref, near_ref, far_ref, weight_ref, query_ref, cosine_ref, sine_ref, *refs):
    state_refs, (projected_ref, entry_ref, mixed_ref, share_ref) = refs[:6], refs[6:]
    rows, depth = query_ref.shape[0], near_ref.shape[1]
    first = state_refs[0].shape[0] // GROUP
    me = index_ref[0]
    devices = weight_ref.shape[0] // depth

    def part(block, other):
        start = pl.multiple_of(other * depth, depth)
        return dot(block, weight_ref[pl.ds(start, depth), :])

    total = jnp.zeros((rows, 2 * LANES), F32)
    for shift in range(devices // 2):
        other = (me + devices - 2 * shift) % devices
        block = slice(shift * rows, (shift + 1) * rows)
        total += part(near_ref[block], other) + part(far_ref[block], other ^ 1)
    projected_ref[...] = total[:, LANES:]
    key = total[:, :LANES]
    key = (key * cosine_ref[...] + pltpu.roll(key, 64, 1) * sine_ref[...]).astype(BF16)
    entry_ref[...] = key
    key = key.astype(F32)
    halves = ((0, first, state_refs[:3]), (first, rows - first, state_refs[3:]))
    for h in range(GROUP):
        query = query_ref[:, h * LANES : (h + 1) * LANES].astype(F32)
        own = jnp.sum(query * key, axis=1, keepdims=True) * scale
        for start, many, (sums, tops, wholes) in halves:
            here, place = slice(h * many, (h + 1) * many), slice(h * rows + start, h * rows + start + many)
            mine, top = own[start : start + many], tops[here, :]
            highest = jnp.maximum(top, mine)
            old, new = jnp.exp(top - highest), jnp.exp(mine - highest)
            under = 1.0 / (old * wholes[here, :] + new)
            mixed_ref[place, :] = sums[here, :] * (old * under)
            share_ref[place, :] = new * under


def final_kernel(got_ref, back_ref, value_ref, key_ref, mixed_ref, share_ref, out_ref, entry_ref):
    rows = value_ref.shape[0]
    slots = got_ref.shape[0]
    delta = dot(back_ref[:, :slots], got_ref[...])
    value = (value_ref[...] + delta).astype(BF16)
    entry_ref[:, :LANES] = key_ref[...]
    entry_ref[:, LANES:] = value
    value = value.astype(F32)
    for h in range(GROUP):
        place = slice(h * rows, (h + 1) * rows)
        out_ref[:, h * LANES : (h + 1) * LANES] = (mixed_ref[place, :] + share_ref[place, :] * value).astype(BF16)


def on_device(hidden, queries, key_cache, value_cache, lengths, tenants, weight, down, up):
    rows, depth = hidden.shape
    peers = lax.axis_size("dp")
    count = lax.axis_size("tensor")
    slots = peers * CAPACITY
    pool, _, rank = down.shape
    chunks = depth // LANES + 1
    length = key_cache.shape[1]
    scale = HEAD_SIZE ** -0.5
    shape, vmem, dma = jax.ShapeDtypeStruct, pltpu.VMEM, pltpu.SemaphoreType.DMA
    params = lambda size: pltpu.CompilerParams(vmem_limit_bytes=size * MIB)
    far = lambda *arrays: [pltpu.with_memory_space_constraint(x, pltpu.HBM) for x in arrays]
    cost = lambda flops, size: pl.CostEstimate(flops=flops, bytes_accessed=size, transcendentals=0)

    tenant_row = tenants.reshape(1, rows)
    length_row = lengths.reshape(1, rows)
    me = lax.axis_index("tensor").astype(I32).reshape(1)
    over_core = lambda x: lax.ppermute(x, "tensor", [(i, i ^ 1) for i in range(count)])
    over_y = lambda x, k: lax.ppermute(x, "tensor", [(i, (i + 2 * k) % count) for i in range(count)])

    early = EARLY_ROWS
    late = rows - early
    states = lambda n: [shape((GROUP * n, LANES), F32)] * 3
    effort = lambda n: cost(4 * n * GROUP * length * LANES, 4 * n * length * LANES)
    inverse = ROPE_BASE ** (-(np.arange(HEAD_SIZE // 2, dtype=np.float32) * 2.0) / HEAD_SIZE)
    inverse = jnp.asarray(np.concatenate([inverse, inverse])[None, :], F32)

    with jax.named_scope("place"):
        placed, handed = pl.pallas_call(
            lambda *refs: place_kernel(pool, *refs),
            out_shape=[shape((slots * chunks, LANES), BF16), shape((rows, depth), BF16)],
            in_specs=[HBM] * 2, out_specs=[VMEM] * 2, compiler_params=params(8),
            scratch_shapes=[vmem((1, rows), I32), dma((2,))],
        )(*far(tenant_row, hidden))
    with jax.named_scope("rows_to_owners"):
        got = lax.all_to_all(
            placed.reshape(peers, chunks, CAPACITY, LANES), "dp", split_axis=0, concat_axis=0, tiled=True
        ).reshape(slots * chunks, LANES)
    with jax.named_scope("gather_hidden"):
        others = [over_y(handed, k) for k in (1, 2, 3)]
    with jax.named_scope("early"):
        first_state = pl.pallas_call(
            lambda *refs: early_kernel(scale, *refs),
            out_shape=states(early),
            in_specs=[ANY] + [HBM] * 4, out_specs=[VMEM] * 3,
            scratch_shapes=[pltpu.SMEM((rows,), I32), vmem((rows, GROUP * LANES), BF16)]
            + [vmem((early, length, LANES), BF16)] * 2 + [dma((4,))],
            compiler_params=params(12), cost_estimate=effort(early),
        )(placed, *far(lengths, queries, key_cache, value_cache))
    with jax.named_scope("down"):
        partial, ids, up_near = pl.pallas_call(
            down_kernel,
            out_shape=[
                shape((slots // 2, LANES), F32), shape((slots, LANES), F32), shape((pool * rank, LANES), BF16)
            ],
            in_specs=[VMEM] * 2 + [HBM, ANY], out_specs=[VMEM] * 3, compiler_params=params(16),
            scratch_shapes=[dma],
        )(got, jnp.swapaxes(down, 1, 2).reshape(pool * rank, depth), *far(up.reshape(pool * rank, LANES)),
          first_state[0])
    with jax.named_scope("reduce"):
        pair_sum = partial + over_core(partial)
        sums_y = [over_y(pair_sum, k) for k in (1, 2, 3)]
    with jax.named_scope("join"):
        near = pl.pallas_call(
            join_kernel, out_shape=shape((4 * rows, depth), BF16), in_specs=[ANY] * 5, out_specs=VMEM,
            scratch_shapes=[dma((4,))], compiler_params=params(4),
        )(pair_sum, handed, *others)
    with jax.named_scope("gather_core"):
        other = over_core(near)
    with jax.named_scope("up"):
        served = pl.pallas_call(
            up_kernel, out_shape=shape((slots, LANES), BF16),
            in_specs=[ANY] + [VMEM] * 6, out_specs=VMEM, compiler_params=params(8),
        )(near, pair_sum, *sums_y, ids, up_near)
    with jax.named_scope("answers"):
        returned = lax.all_to_all(
            served.reshape(peers, CAPACITY, LANES), "dp", split_axis=0, concat_axis=0, tiled=True
        ).reshape(slots, LANES)
    with jax.named_scope("middle"):
        *second_state, weight_near, queries_near, cosine, sine, back = pl.pallas_call(
            lambda *refs: middle_kernel(scale, pool, *refs),
            out_shape=states(late) + [
                shape(weight.shape, BF16), shape(queries.shape, BF16),
                shape((rows, LANES), F32), shape((rows, LANES), F32), shape((rows, LANES), BF16),
            ],
            in_specs=[ANY] + [HBM] * 8, out_specs=[VMEM] * 8,
            scratch_shapes=[pltpu.SMEM((rows,), I32)] + [vmem((late, length, LANES), BF16)] * 2
            + [vmem((1, rows), I32), vmem((1, rows), I32), vmem((1, LANES), F32), dma((8,))],
            compiler_params=params(12), cost_estimate=effort(late),
        )(served, *far(lengths, queries, key_cache, value_cache, tenant_row, length_row, inverse, weight))
    with jax.named_scope("late"):
        value, key, mixed, share = pl.pallas_call(
            lambda *refs: late_kernel(scale, *refs),
            out_shape=[shape((rows, LANES), F32), shape((rows, LANES), BF16)] + [shape((GROUP * rows, LANES), F32)] * 2,
            in_specs=[SMEM] + [VMEM] * 12, out_specs=[VMEM] * 4, compiler_params=params(8),
            cost_estimate=cost(2 * rows * count * depth * 2 * LANES, weight.size * 2),
        )(me, near, other, weight_near, queries_near, cosine, sine, *first_state, *second_state)
    with jax.named_scope("finish"):
        return tuple(pl.pallas_call(
            final_kernel,
            out_shape=[shape((rows, GROUP * LANES), BF16), shape((rows, 2 * LANES), BF16)],
            in_specs=[VMEM] * 6, out_specs=[VMEM] * 2, compiler_params=params(8),
        )(returned, back, value, key, mixed, share))


def solution(mesh):
    in_specs = (
        P("dp", "tensor"),
        P("dp", "tensor"),
        P("dp", None, "tensor"),
        P("dp", None, "tensor"),
        P("dp"),
        P("dp"),
        P(None, "tensor"),
        P("dp", "tensor", None),
        P("dp", None, "tensor"),
    )
    out_specs = (P("dp", "tensor"), P("dp", "tensor"))
    return jax.shard_map(
        on_device, mesh=mesh, in_specs=in_specs, out_specs=out_specs, check_vma=False
    )
```

```python
import jax
import jax.numpy as jnp
import numpy as np
from jax import lax
from jax.experimental import pallas as pl
from jax.experimental.pallas import tpu as pltpu
from jax.sharding import PartitionSpec as P

HEAD_SIZE = 128
GROUP = 8
CAPACITY = 2
LANES = 128
ROPE_BASE = 500000.0
MIB = 1 << 20
EARLY_ROWS = 16
TURN = 26

F32, BF16, I32 = jnp.float32, jnp.bfloat16, jnp.int32
VMEM = pl.BlockSpec(memory_space=pltpu.VMEM)
SMEM = pl.BlockSpec(memory_space=pltpu.SMEM)
HBM = pl.BlockSpec(memory_space=pltpu.HBM)
ANY = pl.BlockSpec(memory_space=pl.ANY)


def iota(shape, dim):
    return lax.broadcasted_iota(I32, shape, dim)


def dot(a, b):
    return jnp.dot(a, b, preferred_element_type=F32)


def dot_t(a, b):
    return lax.dot_general(a, b, (((1,), (1,)), ((), ())), preferred_element_type=F32)


def upright(row):
    n = row.shape[1]
    spread = jnp.broadcast_to(row, (n, n))
    return jnp.sum(jnp.where(iota((n, n), 0) == iota((n, n), 1), spread, 0.0), axis=1, keepdims=True)


def shuffle(chunks, forward):
    wide = 16 * chunks
    row, col = iota((wide, wide), 0), iota((wide, wide), 1)
    chunked, message = (col, row) if forward else (row, col)
    k, s, c = chunked >> 4, (chunked >> 1) & 7, chunked & 1
    return jnp.where(message == s * (2 * chunks) + k * 2 + c, 1.0, 0.0).astype(BF16)


def slots_of(tenant_row, pool, peers, turn):
    n = tenant_row.shape[1]
    owner_row = jnp.floor(tenant_row * (1.0 / pool)) - turn
    owner_row = jnp.where(owner_row < 0.0, owner_row + peers, owner_row)
    owner_col = upright(owner_row)
    same = (owner_col == owner_row) & (iota((n, n), 0) < iota((n, n), 1))
    rank = jnp.sum(jnp.where(same, 1.0, 0.0), axis=0, keepdims=True)
    return owner_row * CAPACITY + rank


def fetches(pairs, sems):
    copies = [pltpu.make_async_copy(source, target, sems.at[i]) for i, (source, target) in enumerate(pairs)]
    for copy in copies:
        copy.start()
    return copies


def place_kernel(pool, tenant_hbm, hidden_hbm, out_ref, hidden_ref, tenant_ref, sems):
    fetch_hidden = pltpu.make_async_copy(hidden_hbm, hidden_ref, sems.at[0])
    fetch_tenant = pltpu.make_async_copy(tenant_hbm, tenant_ref, sems.at[1])
    fetch_tenant.start()
    fetch_hidden.start()
    rows, width = hidden_ref.shape
    chunks = width // LANES + 1
    slots = out_ref.shape[0] // chunks
    mix = shuffle(chunks, True)
    fetch_tenant.wait()
    tenant_row = tenant_ref[...].astype(F32)
    slot_row = slots_of(tenant_row, pool, slots // CAPACITY, TURN)
    place = jnp.where(slot_row == iota((slots, rows), 0).astype(F32), 1.0, 0.0).astype(BF16)
    local = tenant_row - pool * jnp.floor(tenant_row * (1.0 / pool))
    local = jnp.broadcast_to(upright(local), (rows, LANES)).astype(BF16)
    fetch_hidden.wait()
    placed = jnp.concatenate([dot(place, hidden_ref[...]), dot(place, local)], axis=1).astype(BF16)
    groups = slots // 16
    side = jnp.concatenate(
        [
            jnp.concatenate(
                [placed[g * 16 : g * 16 + 16, k * LANES : (k + 1) * LANES] for k in range(chunks)], axis=0
            )
            for g in range(groups)
        ],
        axis=1,
    )
    turned = dot(mix, side).astype(BF16)
    wide = 16 * chunks
    for g in range(groups):
        out_ref[g * wide : (g + 1) * wide, :] = turned[:, g * LANES : (g + 1) * LANES]


def down_kernel(got_ref, down_ref, up_hbm, after_ref, partial_ref, ids_ref, up_ref, sem):
    fetch_up = pltpu.make_async_copy(up_hbm, up_ref, sem)
    fetch_up.start()
    slots = ids_ref.shape[0]
    chunks = got_ref.shape[0] // slots
    groups, wide = slots // 16, 16 * chunks
    side = jnp.concatenate([got_ref[g * wide : (g + 1) * wide, :] for g in range(groups)], axis=1)
    turned = dot(shuffle(chunks, False), side)
    ids = jnp.concatenate([turned[wide - 16 :, g * LANES : (g + 1) * LANES] for g in range(groups)], axis=0)
    turned = turned.astype(BF16)
    rows = jnp.concatenate(
        [
            jnp.concatenate(
                [turned[k * 16 : k * 16 + 16, g * LANES : (g + 1) * LANES] for k in range(chunks - 1)], axis=1
            )
            for g in range(groups)
        ],
        axis=0,
    )
    full = dot_t(rows, down_ref[...])
    lane = iota((slots, LANES), 1)
    right = (lane >= 64).astype(F32)
    total = jnp.zeros((slots, LANES), F32)
    for q in range(full.shape[1] // LANES):
        total += jnp.where(ids == right + 2.0 * q, full[:, q * LANES : (q + 1) * LANES], 0.0)
    total = total + pltpu.roll(total, 64, 1)
    half = slots // 2
    partial_ref[...] = jnp.where(lane[:half] < 64, total[:half], total[half:])
    ids_ref[...] = ids
    fetch_up.wait()


def up_kernel(after_ref, a_ref, b_ref, c_ref, d_ref, ids_ref, up_ref, out_ref):
    total = (a_ref[...] + b_ref[...]) + (c_ref[...] + d_ref[...])
    turned = pltpu.roll(total, 64, 1)
    left = iota(total.shape, 1) < 64
    both = jnp.concatenate([jnp.where(left, total, turned), jnp.where(left, turned, total)], axis=0)
    ids = ids_ref[...]
    right = (iota(ids.shape, 1) >= 64).astype(F32)
    spread = [
        jnp.where(ids == right + 2.0 * q, both, 0.0).astype(BF16) for q in range(up_ref.shape[0] // LANES)
    ]
    out_ref[...] = dot(jnp.concatenate(spread, axis=1), up_ref[...]).astype(BF16)


def attend_cache(scale, first, count, rows, length_at, query_ref, key_ref, value_ref, wait_key, wait_value, sum_ref,
                 top_ref, whole_ref):
    length = key_ref.shape[1]
    wide = count * GROUP
    by_head = jnp.concatenate([query_ref[:, h * LANES : (h + 1) * LANES] for h in range(GROUP)], axis=0)
    row, col = iota((wide, GROUP * rows), 0), iota((wide, GROUP * rows), 1)
    turn = jnp.where(col == (row % GROUP) * rows + row // GROUP + first, 1.0, 0.0).astype(BF16)
    by_row = dot(turn, by_head)
    position = iota((GROUP, length), 1)
    wait_key()
    scores = []
    for r in range(count):
        query = by_row[r * GROUP : (r + 1) * GROUP].astype(BF16)
        score = dot_t(query, key_ref[r]) * scale
        scores.append(jnp.where(position < length_at(first + r), score, -jnp.inf))
    scores = jnp.concatenate(scores, axis=0)
    top = jnp.max(scores, axis=1, keepdims=True)
    weights = jnp.exp(scores - top)
    whole = jnp.broadcast_to(jnp.sum(weights, axis=1, keepdims=True), (wide, LANES))
    top = jnp.broadcast_to(top, (wide, LANES))
    wait_value()
    for r in range(count):
        some = slice(r * GROUP, (r + 1) * GROUP)
        place = pl.ds(r, GROUP, stride=count)
        sum_ref[place, :] = dot(weights[some].astype(BF16), value_ref[r])
        top_ref[place, :] = top[some]
        whole_ref[place, :] = whole[some]


def early_kernel(scale, after_ref, length_hbm, query_hbm, key_hbm, value_hbm, sum_ref, top_ref, whole_ref, length_ref,
                 query_ref, key_ref, value_ref, sems):
    rows, count = query_ref.shape[0], key_ref.shape[0]
    some = pl.ds(0, count)
    copies = fetches(
        [
            (query_hbm, query_ref), (length_hbm, length_ref), (key_hbm.at[some], key_ref),
            (value_hbm.at[some], value_ref),
        ],
        sems,
    )
    copies[0].wait()
    copies[1].wait()
    attend_cache(scale, 0, count, rows, lambda r: length_ref[r], query_ref, key_ref, value_ref, copies[2].wait,
                 copies[3].wait, sum_ref, top_ref, whole_ref)


def middle_kernel(scale, pool, peers, after_ref, length_hbm, query_hbm, key_hbm, value_hbm, tenant_hbm, row_hbm, inverse_hbm,
                  weight_hbm, sum_ref, top_ref, whole_ref, weight_ref,
                  query_ref, cosine_ref, sine_ref, back_ref, length_ref, key_ref, value_ref, tenant_ref, row_ref,
                  inverse_ref, sems):
    rows, count = query_ref.shape[0], key_ref.shape[0]
    some = pl.ds(rows - count, count)
    copies = fetches(
        [
            (query_hbm, query_ref), (length_hbm, length_ref), (tenant_hbm, tenant_ref), (row_hbm, row_ref),
            (inverse_hbm, inverse_ref), (key_hbm.at[some], key_ref), (value_hbm.at[some], value_ref),
            (weight_hbm, weight_ref),
        ],
        sems,
    )
    for copy in copies[:5]:
        copy.wait()
    lane = iota((rows, LANES), 1)
    slot_col = upright(slots_of(tenant_ref[...].astype(F32), pool, peers, TURN))
    back_ref[...] = jnp.where(slot_col == lane.astype(F32), 1.0, 0.0).astype(BF16)
    angle = upright(row_ref[...].astype(F32)) * inverse_ref[...]
    sine = jnp.sin(angle)
    cosine_ref[...] = jnp.cos(angle)
    sine_ref[...] = jnp.where(lane < 64, -sine, sine)
    attend_cache(scale, rows - count, count, rows, lambda r: length_ref[r], query_ref, key_ref, value_ref,
                 copies[5].wait, copies[6].wait, sum_ref, top_ref, whole_ref)
    for copy in copies[7:]:
        copy.wait()


def join_kernel(after_ref, own_any, y1_any, y2_any, y3_any, near_ref, sems):
    rows = own_any.shape[0]
    blocks = enumerate((own_any, y1_any, y2_any, y3_any))
    for copy in fetches([(block, near_ref.at[pl.ds(k * rows, rows)]) for k, block in blocks], sems):
        copy.wait()


def late_kernel(scale, index_ref, near_ref, far_ref, weight_ref, query_ref, cosine_ref, sine_ref, *refs):
    state_refs, (projected_ref, entry_ref, mixed_ref, share_ref) = refs[:6], refs[6:]
    rows, depth = query_ref.shape[0], near_ref.shape[1]
    first = state_refs[0].shape[0] // GROUP
    me = index_ref[0]
    devices = weight_ref.shape[0] // depth

    def part(block, other):
        start = pl.multiple_of(other * depth, depth)
        return dot(block, weight_ref[pl.ds(start, depth), :])

    total = jnp.zeros((rows, 2 * LANES), F32)
    for shift in range(devices // 2):
        other = (me + devices - 2 * shift) % devices
        block = slice(shift * rows, (shift + 1) * rows)
        total += part(near_ref[block], other) + part(far_ref[block], other ^ 1)
    projected_ref[...] = total[:, LANES:]
    key = total[:, :LANES]
    key = (key * cosine_ref[...] + pltpu.roll(key, 64, 1) * sine_ref[...]).astype(BF16)
    entry_ref[...] = key
    key = key.astype(F32)
    halves = ((0, first, state_refs[:3]), (first, rows - first, state_refs[3:]))
    for h in range(GROUP):
        query = query_ref[:, h * LANES : (h + 1) * LANES].astype(F32)
        own = jnp.sum(query * key, axis=1, keepdims=True) * scale
        for start, many, (sums, tops, wholes) in halves:
            here, place = slice(h * many, (h + 1) * many), slice(h * rows + start, h * rows + start + many)
            mine, top = own[start : start + many], tops[here, :]
            highest = jnp.maximum(top, mine)
            old, new = jnp.exp(top - highest), jnp.exp(mine - highest)
            under = 1.0 / (old * wholes[here, :] + new)
            mixed_ref[place, :] = sums[here, :] * (old * under)
            share_ref[place, :] = new * under


def final_kernel(got_ref, back_ref, value_ref, key_ref, mixed_ref, share_ref, out_ref, entry_ref):
    rows = value_ref.shape[0]
    slots = got_ref.shape[0]
    delta = dot(back_ref[:, :slots], got_ref[...])
    value = (value_ref[...] + delta).astype(BF16)
    entry_ref[:, :LANES] = key_ref[...]
    entry_ref[:, LANES:] = value
    value = value.astype(F32)
    for h in range(GROUP):
        place = slice(h * rows, (h + 1) * rows)
        out_ref[:, h * LANES : (h + 1) * LANES] = (mixed_ref[place, :] + share_ref[place, :] * value).astype(BF16)


def on_device(hidden, queries, key_cache, value_cache, lengths, tenants, weight, down, up):
    rows, depth = hidden.shape
    peers = lax.axis_size("dp")
    count = lax.axis_size("tensor")
    slots = peers * CAPACITY
    pool, _, rank = down.shape
    chunks = depth // LANES + 1
    length = key_cache.shape[1]
    scale = HEAD_SIZE ** -0.5
    shape, vmem, dma = jax.ShapeDtypeStruct, pltpu.VMEM, pltpu.SemaphoreType.DMA
    params = lambda size: pltpu.CompilerParams(vmem_limit_bytes=size * MIB)
    far = lambda *arrays: [pltpu.with_memory_space_constraint(x, pltpu.HBM) for x in arrays]
    cost = lambda flops, size: pl.CostEstimate(flops=flops, bytes_accessed=size, transcendentals=0)

    tenant_row = tenants.reshape(1, rows)
    length_row = lengths.reshape(1, rows)
    me = lax.axis_index("tensor").astype(I32).reshape(1)
    over_core = lambda x: lax.ppermute(x, "tensor", [(i, i ^ 1) for i in range(count)])
    over_y = lambda x, k: lax.ppermute(x, "tensor", [(i, (i + 2 * k) % count) for i in range(count)])

    early = EARLY_ROWS
    ring = [[(k + TURN) % peers for k in range(peers)]]
    late = rows - early
    states = lambda n: [shape((GROUP * n, LANES), F32)] * 3
    effort = lambda n: cost(4 * n * GROUP * length * LANES, 4 * n * length * LANES)
    inverse = ROPE_BASE ** (-(np.arange(HEAD_SIZE // 2, dtype=np.float32) * 2.0) / HEAD_SIZE)
    inverse = jnp.asarray(np.concatenate([inverse, inverse])[None, :], F32)

    with jax.named_scope("place"):
        placed, handed = pl.pallas_call(
            lambda *refs: place_kernel(pool, *refs),
            out_shape=[shape((slots * chunks, LANES), BF16), shape((rows, depth), BF16)],
            in_specs=[HBM] * 2, out_specs=[VMEM] * 2, compiler_params=params(8),
            scratch_shapes=[vmem((1, rows), I32), dma((2,))],
        )(*far(tenant_row, hidden))
    with jax.named_scope("rows_to_owners"):
        got = lax.all_to_all(
            placed.reshape(peers, chunks, CAPACITY, LANES), "dp", split_axis=0, concat_axis=0, tiled=True, axis_index_groups=ring
        ).reshape(slots * chunks, LANES)
    with jax.named_scope("gather_hidden"):
        others = [over_y(handed, k) for k in (1, 2, 3)]
    with jax.named_scope("early"):
        first_state = pl.pallas_call(
            lambda *refs: early_kernel(scale, *refs),
            out_shape=states(early),
            in_specs=[ANY] + [HBM] * 4, out_specs=[VMEM] * 3,
            scratch_shapes=[pltpu.SMEM((rows,), I32), vmem((rows, GROUP * LANES), BF16)]
            + [vmem((early, length, LANES), BF16)] * 2 + [dma((4,))],
            compiler_params=params(12), cost_estimate=effort(early),
        )(placed, *far(lengths, queries, key_cache, value_cache))
    with jax.named_scope("down"):
        partial, ids, up_near = pl.pallas_call(
            down_kernel,
            out_shape=[
                shape((slots // 2, LANES), F32), shape((slots, LANES), F32), shape((pool * rank, LANES), BF16)
            ],
            in_specs=[VMEM] * 2 + [HBM, ANY], out_specs=[VMEM] * 3, compiler_params=params(16),
            scratch_shapes=[dma],
        )(got, jnp.swapaxes(down, 1, 2).reshape(pool * rank, depth), *far(up.reshape(pool * rank, LANES)),
          first_state[0])
    with jax.named_scope("reduce"):
        pair_sum = partial + over_core(partial)
        sums_y = [over_y(pair_sum, k) for k in (1, 2, 3)]
    with jax.named_scope("join"):
        near = pl.pallas_call(
            join_kernel, out_shape=shape((4 * rows, depth), BF16), in_specs=[ANY] * 5, out_specs=VMEM,
            scratch_shapes=[dma((4,))], compiler_params=params(4),
        )(pair_sum, handed, *others)
    with jax.named_scope("gather_core"):
        other = over_core(near)
    with jax.named_scope("up"):
        served = pl.pallas_call(
            up_kernel, out_shape=shape((slots, LANES), BF16),
            in_specs=[ANY] + [VMEM] * 6, out_specs=VMEM, compiler_params=params(8),
        )(near, pair_sum, *sums_y, ids, up_near)
    with jax.named_scope("answers"):
        returned = lax.all_to_all(
            served.reshape(peers, CAPACITY, LANES), "dp", split_axis=0, concat_axis=0, tiled=True, axis_index_groups=ring
        ).reshape(slots, LANES)
    with jax.named_scope("middle"):
        *second_state, weight_near, queries_near, cosine, sine, back = pl.pallas_call(
            lambda *refs: middle_kernel(scale, pool, peers, *refs),
            out_shape=states(late) + [
                shape(weight.shape, BF16), shape(queries.shape, BF16),
                shape((rows, LANES), F32), shape((rows, LANES), F32), shape((rows, LANES), BF16),
            ],
            in_specs=[ANY] + [HBM] * 8, out_specs=[VMEM] * 8,
            scratch_shapes=[pltpu.SMEM((rows,), I32)] + [vmem((late, length, LANES), BF16)] * 2
            + [vmem((1, rows), I32), vmem((1, rows), I32), vmem((1, LANES), F32), dma((8,))],
            compiler_params=params(12), cost_estimate=effort(late),
        )(served, *far(lengths, queries, key_cache, value_cache, tenant_row, length_row, inverse, weight))
    with jax.named_scope("late"):
        value, key, mixed, share = pl.pallas_call(
            lambda *refs: late_kernel(scale, *refs),
            out_shape=[shape((rows, LANES), F32), shape((rows, LANES), BF16)] + [shape((GROUP * rows, LANES), F32)] * 2,
            in_specs=[SMEM] + [VMEM] * 12, out_specs=[VMEM] * 4, compiler_params=params(8),
            cost_estimate=cost(2 * rows * count * depth * 2 * LANES, weight.size * 2),
        )(me, near, other, weight_near, queries_near, cosine, sine, *first_state, *second_state)
    with jax.named_scope("finish"):
        return tuple(pl.pallas_call(
            final_kernel,
            out_shape=[shape((rows, GROUP * LANES), BF16), shape((rows, 2 * LANES), BF16)],
            in_specs=[VMEM] * 6, out_specs=[VMEM] * 2, compiler_params=params(8),
        )(returned, back, value, key, mixed, share))


def solution(mesh):
    in_specs = (
        P("dp", "tensor"),
        P("dp", "tensor"),
        P("dp", None, "tensor"),
        P("dp", None, "tensor"),
        P("dp"),
        P("dp"),
        P(None, "tensor"),
        P("dp", "tensor", None),
        P("dp", None, "tensor"),
    )
    out_specs = (P("dp", "tensor"), P("dp", "tensor"))
    return jax.shard_map(
        on_device, mesh=mesh, in_specs=in_specs, out_specs=out_specs, check_vma=False
    )
```

```python
import jax
import jax.numpy as jnp
import numpy as np
from jax import lax
from jax.experimental import pallas as pl
from jax.experimental.pallas import tpu as pltpu
from jax.sharding import PartitionSpec as P

HEAD_SIZE = 128
GROUP = 8
CAPACITY = 2
LANES = 128
ROPE_BASE = 500000.0
MIB = 1 << 20
EARLY_ROWS = 8
INNER_ROWS = 16
TURN = 26

F32, BF16, I32 = jnp.float32, jnp.bfloat16, jnp.int32
VMEM = pl.BlockSpec(memory_space=pltpu.VMEM)
SMEM = pl.BlockSpec(memory_space=pltpu.SMEM)
HBM = pl.BlockSpec(memory_space=pltpu.HBM)
ANY = pl.BlockSpec(memory_space=pl.ANY)


def iota(shape, dim):
    return lax.broadcasted_iota(I32, shape, dim)


def dot(a, b):
    return jnp.dot(a, b, preferred_element_type=F32)


def dot_t(a, b):
    return lax.dot_general(a, b, (((1,), (1,)), ((), ())), preferred_element_type=F32)


def upright(row):
    n = row.shape[1]
    spread = jnp.broadcast_to(row, (n, n))
    return jnp.sum(jnp.where(iota((n, n), 0) == iota((n, n), 1), spread, 0.0), axis=1, keepdims=True)


def shuffle(chunks, forward):
    wide = 16 * chunks
    row, col = iota((wide, wide), 0), iota((wide, wide), 1)
    chunked, message = (col, row) if forward else (row, col)
    k, s, c = chunked >> 4, (chunked >> 1) & 7, chunked & 1
    return jnp.where(message == s * (2 * chunks) + k * 2 + c, 1.0, 0.0).astype(BF16)


def slots_of(tenant_row, pool, peers, turn):
    n = tenant_row.shape[1]
    owner_row = jnp.floor(tenant_row * (1.0 / pool)) - turn
    owner_row = jnp.where(owner_row < 0.0, owner_row + peers, owner_row)
    owner_col = upright(owner_row)
    same = (owner_col == owner_row) & (iota((n, n), 0) < iota((n, n), 1))
    rank = jnp.sum(jnp.where(same, 1.0, 0.0), axis=0, keepdims=True)
    return owner_row * CAPACITY + rank


def fetches(pairs, sems):
    copies = [pltpu.make_async_copy(source, target, sems.at[i]) for i, (source, target) in enumerate(pairs)]
    for copy in copies:
        copy.start()
    return copies


def place_kernel(pool, tenant_hbm, hidden_hbm, out_ref, hidden_ref, tenant_ref, sems):
    fetch_hidden = pltpu.make_async_copy(hidden_hbm, hidden_ref, sems.at[0])
    fetch_tenant = pltpu.make_async_copy(tenant_hbm, tenant_ref, sems.at[1])
    fetch_tenant.start()
    fetch_hidden.start()
    rows, width = hidden_ref.shape
    chunks = width // LANES + 1
    slots = out_ref.shape[0] // chunks
    mix = shuffle(chunks, True)
    fetch_tenant.wait()
    tenant_row = tenant_ref[...].astype(F32)
    slot_row = slots_of(tenant_row, pool, slots // CAPACITY, TURN)
    place = jnp.where(slot_row == iota((slots, rows), 0).astype(F32), 1.0, 0.0).astype(BF16)
    local = tenant_row - pool * jnp.floor(tenant_row * (1.0 / pool))
    local = jnp.broadcast_to(upright(local), (rows, LANES)).astype(BF16)
    fetch_hidden.wait()
    placed = jnp.concatenate([dot(place, hidden_ref[...]), dot(place, local)], axis=1).astype(BF16)
    groups = slots // 16
    side = jnp.concatenate(
        [
            jnp.concatenate(
                [placed[g * 16 : g * 16 + 16, k * LANES : (k + 1) * LANES] for k in range(chunks)], axis=0
            )
            for g in range(groups)
        ],
        axis=1,
    )
    turned = dot(mix, side).astype(BF16)
    wide = 16 * chunks
    for g in range(groups):
        out_ref[g * wide : (g + 1) * wide, :] = turned[:, g * LANES : (g + 1) * LANES]


def down_kernel(got_ref, down_ref, up_hbm, after_ref, partial_ref, ids_ref, up_ref, sem):
    fetch_up = pltpu.make_async_copy(up_hbm, up_ref, sem)
    fetch_up.start()
    slots = ids_ref.shape[0]
    chunks = got_ref.shape[0] // slots
    groups, wide = slots // 16, 16 * chunks
    side = jnp.concatenate([got_ref[g * wide : (g + 1) * wide, :] for g in range(groups)], axis=1)
    turned = dot(shuffle(chunks, False), side)
    ids = jnp.concatenate([turned[wide - 16 :, g * LANES : (g + 1) * LANES] for g in range(groups)], axis=0)
    turned = turned.astype(BF16)
    rows = jnp.concatenate(
        [
            jnp.concatenate(
                [turned[k * 16 : k * 16 + 16, g * LANES : (g + 1) * LANES] for k in range(chunks - 1)], axis=1
            )
            for g in range(groups)
        ],
        axis=0,
    )
    full = dot_t(rows, down_ref[...])
    lane = iota((slots, LANES), 1)
    right = (lane >= 64).astype(F32)
    total = jnp.zeros((slots, LANES), F32)
    for q in range(full.shape[1] // LANES):
        total += jnp.where(ids == right + 2.0 * q, full[:, q * LANES : (q + 1) * LANES], 0.0)
    total = total + pltpu.roll(total, 64, 1)
    half = slots // 2
    partial_ref[...] = jnp.where(lane[:half] < 64, total[:half], total[half:])
    ids_ref[...] = ids
    fetch_up.wait()


def up_kernel(after_ref, after2_ref, a_ref, b_ref, c_ref, d_ref, ids_ref, up_ref, out_ref):
    total = (a_ref[...] + b_ref[...]) + (c_ref[...] + d_ref[...])
    turned = pltpu.roll(total, 64, 1)
    left = iota(total.shape, 1) < 64
    both = jnp.concatenate([jnp.where(left, total, turned), jnp.where(left, turned, total)], axis=0)
    ids = ids_ref[...]
    right = (iota(ids.shape, 1) >= 64).astype(F32)
    spread = [
        jnp.where(ids == right + 2.0 * q, both, 0.0).astype(BF16) for q in range(up_ref.shape[0] // LANES)
    ]
    out_ref[...] = dot(jnp.concatenate(spread, axis=1), up_ref[...]).astype(BF16)


def attend_cache(scale, first, count, rows, length_at, query_ref, key_ref, value_ref, wait_key, wait_value, sum_ref,
                 top_ref, whole_ref):
    length = key_ref.shape[1]
    wide = count * GROUP
    by_head = jnp.concatenate([query_ref[:, h * LANES : (h + 1) * LANES] for h in range(GROUP)], axis=0)
    row, col = iota((wide, GROUP * rows), 0), iota((wide, GROUP * rows), 1)
    turn = jnp.where(col == (row % GROUP) * rows + row // GROUP + first, 1.0, 0.0).astype(BF16)
    by_row = dot(turn, by_head)
    position = iota((GROUP, length), 1)
    wait_key()
    scores = []
    for r in range(count):
        query = by_row[r * GROUP : (r + 1) * GROUP].astype(BF16)
        score = dot_t(query, key_ref[r]) * scale
        scores.append(jnp.where(position < length_at(first + r), score, -jnp.inf))
    scores = jnp.concatenate(scores, axis=0)
    top = jnp.max(scores, axis=1, keepdims=True)
    weights = jnp.exp(scores - top)
    whole = jnp.broadcast_to(jnp.sum(weights, axis=1, keepdims=True), (wide, LANES))
    top = jnp.broadcast_to(top, (wide, LANES))
    wait_value()
    for r in range(count):
        some = slice(r * GROUP, (r + 1) * GROUP)
        place = pl.ds(r, GROUP, stride=count)
        sum_ref[place, :] = dot(weights[some].astype(BF16), value_ref[r])
        top_ref[place, :] = top[some]
        whole_ref[place, :] = whole[some]


def cache_kernel(scale, first, after_ref, length_hbm, query_hbm, key_hbm, value_hbm, sum_ref, top_ref, whole_ref, length_ref,
                 query_ref, key_ref, value_ref, sems):
    rows, count = query_ref.shape[0], key_ref.shape[0]
    some = pl.ds(first, count)
    copies = fetches(
        [
            (query_hbm, query_ref), (length_hbm, length_ref), (key_hbm.at[some], key_ref),
            (value_hbm.at[some], value_ref),
        ],
        sems,
    )
    copies[0].wait()
    copies[1].wait()
    attend_cache(scale, first, count, rows, lambda r: length_ref[r], query_ref, key_ref, value_ref, copies[2].wait,
                 copies[3].wait, sum_ref, top_ref, whole_ref)


def tables_kernel(scale, pool, peers, after_ref, length_hbm, query_hbm, key_hbm, value_hbm, tenant_hbm, row_hbm,
                  inverse_hbm, weight_hbm, *refs):
    *state_refs, weight_ref, query_ref, cosine_ref, sine_ref, back_ref = refs[:-7]
    length_ref, key_ref, value_ref, tenant_ref, row_ref, inverse_ref, sems = refs[-7:]
    rows = query_ref.shape[0]
    count = key_ref.shape[0] if state_refs else 0
    some = pl.ds(rows - count, count)
    copies = fetches(
        [
            (query_hbm, query_ref), (length_hbm, length_ref), (tenant_hbm, tenant_ref), (row_hbm, row_ref),
            (inverse_hbm, inverse_ref), (weight_hbm, weight_ref),
        ][: 5 if count else 6]
        + ([(key_hbm.at[some], key_ref), (value_hbm.at[some], value_ref), (weight_hbm, weight_ref)] if count else []),
        sems,
    )
    for copy in copies[:5]:
        copy.wait()
    lane = iota((rows, LANES), 1)
    slot_col = upright(slots_of(tenant_ref[...].astype(F32), pool, peers, TURN))
    back_ref[...] = jnp.where(slot_col == lane.astype(F32), 1.0, 0.0).astype(BF16)
    angle = upright(row_ref[...].astype(F32)) * inverse_ref[...]
    sine = jnp.sin(angle)
    cosine_ref[...] = jnp.cos(angle)
    sine_ref[...] = jnp.where(lane < 64, -sine, sine)
    if count:
        attend_cache(scale, rows - count, count, rows, lambda r: length_ref[r], query_ref, key_ref, value_ref,
                     copies[5].wait, copies[6].wait, *state_refs)
    copies[-1].wait()


def join_kernel(after_ref, own_any, y1_any, y2_any, y3_any, near_ref, sems):
    rows = own_any.shape[0]
    blocks = enumerate((own_any, y1_any, y2_any, y3_any))
    for copy in fetches([(block, near_ref.at[pl.ds(k * rows, rows)]) for k, block in blocks], sems):
        copy.wait()


def late_kernel(scale, index_ref, near_ref, far_ref, weight_ref, query_ref, cosine_ref, sine_ref, *refs):
    state_refs, (projected_ref, entry_ref, mixed_ref, share_ref) = refs[:-4], refs[-4:]
    rows, depth = query_ref.shape[0], near_ref.shape[1]
    me = index_ref[0]
    devices = weight_ref.shape[0] // depth

    def part(block, other):
        start = pl.multiple_of(other * depth, depth)
        return dot(block, weight_ref[pl.ds(start, depth), :])

    total = jnp.zeros((rows, 2 * LANES), F32)
    for shift in range(devices // 2):
        other = (me + devices - 2 * shift) % devices
        block = slice(shift * rows, (shift + 1) * rows)
        total += part(near_ref[block], other) + part(far_ref[block], other ^ 1)
    projected_ref[...] = total[:, LANES:]
    key = total[:, :LANES]
    key = (key * cosine_ref[...] + pltpu.roll(key, 64, 1) * sine_ref[...]).astype(BF16)
    entry_ref[...] = key
    key = key.astype(F32)
    parts, start = [], 0
    for k in range(0, len(state_refs), 3):
        many = state_refs[k].shape[0] // GROUP
        parts.append((start, many, state_refs[k : k + 3]))
        start += many
    for h in range(GROUP):
        query = query_ref[:, h * LANES : (h + 1) * LANES].astype(F32)
        own = jnp.sum(query * key, axis=1, keepdims=True) * scale
        for start, many, (sums, tops, wholes) in parts:
            here, place = slice(h * many, (h + 1) * many), slice(h * rows + start, h * rows + start + many)
            mine, top = own[start : start + many], tops[here, :]
            highest = jnp.maximum(top, mine)
            old, new = jnp.exp(top - highest), jnp.exp(mine - highest)
            under = 1.0 / (old * wholes[here, :] + new)
            mixed_ref[place, :] = sums[here, :] * (old * under)
            share_ref[place, :] = new * under


def final_kernel(got_ref, back_ref, value_ref, key_ref, mixed_ref, share_ref, out_ref, entry_ref):
    rows = value_ref.shape[0]
    slots = got_ref.shape[0]
    delta = dot(back_ref[:, :slots], got_ref[...])
    value = (value_ref[...] + delta).astype(BF16)
    entry_ref[:, :LANES] = key_ref[...]
    entry_ref[:, LANES:] = value
    value = value.astype(F32)
    for h in range(GROUP):
        place = slice(h * rows, (h + 1) * rows)
        out_ref[:, h * LANES : (h + 1) * LANES] = (mixed_ref[place, :] + share_ref[place, :] * value).astype(BF16)


def on_device(hidden, queries, key_cache, value_cache, lengths, tenants, weight, down, up):
    rows, depth = hidden.shape
    peers = lax.axis_size("dp")
    count = lax.axis_size("tensor")
    slots = peers * CAPACITY
    pool, _, rank = down.shape
    chunks = depth // LANES + 1
    length = key_cache.shape[1]
    scale = HEAD_SIZE ** -0.5
    shape, vmem, dma = jax.ShapeDtypeStruct, pltpu.VMEM, pltpu.SemaphoreType.DMA
    params = lambda size: pltpu.CompilerParams(vmem_limit_bytes=size * MIB)
    far = lambda *arrays: [pltpu.with_memory_space_constraint(x, pltpu.HBM) for x in arrays]
    cost = lambda flops, size: pl.CostEstimate(flops=flops, bytes_accessed=size, transcendentals=0)

    tenant_row = tenants.reshape(1, rows)
    length_row = lengths.reshape(1, rows)
    me = lax.axis_index("tensor").astype(I32).reshape(1)
    over_core = lambda x: lax.ppermute(x, "tensor", [(i, i ^ 1) for i in range(count)])
    over_y = lambda x, k: lax.ppermute(x, "tensor", [(i, (i + 2 * k) % count) for i in range(count)])

    early = EARLY_ROWS
    ring = [[(k + TURN) % peers for k in range(peers)]]
    inner = INNER_ROWS
    late = rows - early - inner
    states = lambda n: [shape((GROUP * n, LANES), F32)] * 3
    effort = lambda n: cost(4 * n * GROUP * length * LANES, 4 * n * length * LANES)
    inverse = ROPE_BASE ** (-(np.arange(HEAD_SIZE // 2, dtype=np.float32) * 2.0) / HEAD_SIZE)
    inverse = jnp.asarray(np.concatenate([inverse, inverse])[None, :], F32)

    def attend(first, many, after):
        return pl.pallas_call(
            lambda *refs: cache_kernel(scale, first, *refs),
            out_shape=states(many),
            in_specs=[ANY] + [HBM] * 4, out_specs=[VMEM] * 3,
            scratch_shapes=[pltpu.SMEM((rows,), I32), vmem((rows, GROUP * LANES), BF16)]
            + [vmem((many, length, LANES), BF16)] * 2 + [dma((4,))],
            compiler_params=params(14), cost_estimate=effort(many),
        )(after, *far(lengths, queries, key_cache, value_cache))

    with jax.named_scope("place"):
        placed, handed = pl.pallas_call(
            lambda *refs: place_kernel(pool, *refs),
            out_shape=[shape((slots * chunks, LANES), BF16), shape((rows, depth), BF16)],
            in_specs=[HBM] * 2, out_specs=[VMEM] * 2, compiler_params=params(8),
            scratch_shapes=[vmem((1, rows), I32), dma((2,))],
        )(*far(tenant_row, hidden))
    with jax.named_scope("rows_to_owners"):
        got = lax.all_to_all(
            placed.reshape(peers, chunks, CAPACITY, LANES), "dp", split_axis=0, concat_axis=0, tiled=True, axis_index_groups=ring
        ).reshape(slots * chunks, LANES)
    with jax.named_scope("gather_hidden"):
        others = [over_y(handed, k) for k in (1, 2, 3)]
    with jax.named_scope("early"):
        first_state = attend(0, early, placed)
    with jax.named_scope("down"):
        partial, ids, up_near = pl.pallas_call(
            down_kernel,
            out_shape=[
                shape((slots // 2, LANES), F32), shape((slots, LANES), F32), shape((pool * rank, LANES), BF16)
            ],
            in_specs=[VMEM] * 2 + [HBM, ANY], out_specs=[VMEM] * 3, compiler_params=params(16),
            scratch_shapes=[dma],
        )(got, jnp.swapaxes(down, 1, 2).reshape(pool * rank, depth), *far(up.reshape(pool * rank, LANES)),
          first_state[0])
    with jax.named_scope("reduce"):
        pair_sum = partial + over_core(partial)
        sums_y = [over_y(pair_sum, k) for k in (1, 2, 3)]
    with jax.named_scope("join"):
        near = pl.pallas_call(
            join_kernel, out_shape=shape((4 * rows, depth), BF16), in_specs=[ANY] * 5, out_specs=VMEM,
            scratch_shapes=[dma((4,))], compiler_params=params(4),
        )(pair_sum, handed, *others)
    with jax.named_scope("gather_core"):
        other = over_core(near)
    with jax.named_scope("inner"):
        second_state = attend(early, inner, pair_sum) if inner else []
    with jax.named_scope("up"):
        served = pl.pallas_call(
            up_kernel, out_shape=shape((slots, LANES), BF16),
            in_specs=[ANY] * 2 + [VMEM] * 6, out_specs=VMEM, compiler_params=params(8),
        )(near, second_state[0] if inner else near, pair_sum, *sums_y, ids, up_near)
    with jax.named_scope("answers"):
        returned = lax.all_to_all(
            served.reshape(peers, CAPACITY, LANES), "dp", split_axis=0, concat_axis=0, tiled=True, axis_index_groups=ring
        ).reshape(slots, LANES)
    with jax.named_scope("tables"):
        *third_state, weight_near, queries_near, cosine, sine, back = pl.pallas_call(
            lambda *refs: tables_kernel(scale, pool, peers, *refs),
            out_shape=(states(late) if late else []) + [
                shape(weight.shape, BF16), shape(queries.shape, BF16),
                shape((rows, LANES), F32), shape((rows, LANES), F32), shape((rows, LANES), BF16),
            ],
            in_specs=[ANY] + [HBM] * 8, out_specs=[VMEM] * (8 if late else 5),
            scratch_shapes=[pltpu.SMEM((rows,), I32)] + [vmem((max(late, 1), length, LANES), BF16)] * 2
            + [vmem((1, rows), I32), vmem((1, rows), I32), vmem((1, LANES), F32), dma((8,))],
            compiler_params=params(14), cost_estimate=effort(max(late, 8)),
        )(served, *far(lengths, queries, key_cache, value_cache, tenant_row, length_row, inverse, weight))
    past = [*first_state, *second_state, *third_state]
    with jax.named_scope("late"):
        value, key, mixed, share = pl.pallas_call(
            lambda *refs: late_kernel(scale, *refs),
            out_shape=[shape((rows, LANES), F32), shape((rows, LANES), BF16)] + [shape((GROUP * rows, LANES), F32)] * 2,
            in_specs=[SMEM] + [VMEM] * (6 + len(past)), out_specs=[VMEM] * 4, compiler_params=params(8),
            cost_estimate=cost(2 * rows * count * depth * 2 * LANES, weight.size * 2),
        )(me, near, other, weight_near, queries_near, cosine, sine, *past)
    with jax.named_scope("finish"):
        return tuple(pl.pallas_call(
            final_kernel,
            out_shape=[shape((rows, GROUP * LANES), BF16), shape((rows, 2 * LANES), BF16)],
            in_specs=[VMEM] * 6, out_specs=[VMEM] * 2, compiler_params=params(8),
        )(returned, back, value, key, mixed, share))


def solution(mesh):
    in_specs = (
        P("dp", "tensor"),
        P("dp", "tensor"),
        P("dp", None, "tensor"),
        P("dp", None, "tensor"),
        P("dp"),
        P("dp"),
        P(None, "tensor"),
        P("dp", "tensor", None),
        P("dp", None, "tensor"),
    )
    out_specs = (P("dp", "tensor"), P("dp", "tensor"))
    return jax.shard_map(
        on_device, mesh=mesh, in_specs=in_specs, out_specs=out_specs, check_vma=False
    )
```

```python
import jax
import jax.numpy as jnp
import numpy as np
from jax import lax
from jax.experimental import pallas as pl
from jax.experimental.pallas import tpu as pltpu
from jax.sharding import PartitionSpec as P

HEAD_SIZE = 128
GROUP = 8
CAPACITY = 2
LANES = 128
ROPE_BASE = 500000.0
MIB = 1 << 20
TURN = 26
MARKS = 3

F32, BF16, I32 = jnp.float32, jnp.bfloat16, jnp.int32
VMEM = pl.BlockSpec(memory_space=pltpu.VMEM)
SMEM = pl.BlockSpec(memory_space=pltpu.SMEM)
HBM = pl.BlockSpec(memory_space=pltpu.HBM)
ANY = pl.BlockSpec(memory_space=pl.ANY)


def iota(shape, dim):
    return lax.broadcasted_iota(I32, shape, dim)


def dot(a, b):
    return jnp.dot(a, b, preferred_element_type=F32)


def dot_t(a, b):
    return lax.dot_general(a, b, (((1,), (1,)), ((), ())), preferred_element_type=F32)


def upright(row):
    n = row.shape[1]
    spread = jnp.broadcast_to(row, (n, n))
    return jnp.sum(jnp.where(iota((n, n), 0) == iota((n, n), 1), spread, 0.0), axis=1, keepdims=True)


def shuffle(chunks, forward):
    wide = 16 * chunks
    row, col = iota((wide, wide), 0), iota((wide, wide), 1)
    chunked, message = (col, row) if forward else (row, col)
    k, s, c = chunked >> 4, (chunked >> 1) & 7, chunked & 1
    return jnp.where(message == s * (2 * chunks) + k * 2 + c, 1.0, 0.0).astype(BF16)


def slots_of(tenant_row, pool, peers, turn):
    n = tenant_row.shape[1]
    owner_row = jnp.floor(tenant_row * (1.0 / pool)) - turn
    owner_row = jnp.where(owner_row < 0.0, owner_row + peers, owner_row)
    owner_col = upright(owner_row)
    same = (owner_col == owner_row) & (iota((n, n), 0) < iota((n, n), 1))
    rank = jnp.sum(jnp.where(same, 1.0, 0.0), axis=0, keepdims=True)
    return owner_row * CAPACITY + rank


def fetches(pairs, sems):
    copies = [pltpu.make_async_copy(source, target, sems.at[i]) for i, (source, target) in enumerate(pairs)]
    for copy in copies:
        copy.start()
    return copies


def place_kernel(pool, tenant_hbm, hidden_hbm, out_ref, hidden_ref, tenant_ref, sems):
    fetch_hidden = pltpu.make_async_copy(hidden_hbm, hidden_ref, sems.at[0])
    fetch_tenant = pltpu.make_async_copy(tenant_hbm, tenant_ref, sems.at[1])
    fetch_tenant.start()
    fetch_hidden.start()
    rows, width = hidden_ref.shape
    chunks = width // LANES + 1
    slots = out_ref.shape[0] // chunks
    mix = shuffle(chunks, True)
    fetch_tenant.wait()
    tenant_row = tenant_ref[...].astype(F32)
    slot_row = slots_of(tenant_row, pool, slots // CAPACITY, TURN)
    place = jnp.where(slot_row == iota((slots, rows), 0).astype(F32), 1.0, 0.0).astype(BF16)
    local = tenant_row - pool * jnp.floor(tenant_row * (1.0 / pool))
    local = jnp.broadcast_to(upright(local), (rows, LANES)).astype(BF16)
    fetch_hidden.wait()
    placed = jnp.concatenate([dot(place, hidden_ref[...]), dot(place, local)], axis=1).astype(BF16)
    groups = slots // 16
    side = jnp.concatenate(
        [
            jnp.concatenate(
                [placed[g * 16 : g * 16 + 16, k * LANES : (k + 1) * LANES] for k in range(chunks)], axis=0
            )
            for g in range(groups)
        ],
        axis=1,
    )
    turned = dot(mix, side).astype(BF16)
    wide = 16 * chunks
    for g in range(groups):
        out_ref[g * wide : (g + 1) * wide, :] = turned[:, g * LANES : (g + 1) * LANES]


def down_kernel(got_ref, down_ref, up_hbm, query_hbm, length_hbm, after_ref, partial_ref, ids_ref, up_ref, query_ref,
                length_ref, sems):
    copies = fetches([(up_hbm, up_ref), (query_hbm, query_ref), (length_hbm, length_ref)], sems)
    slots = ids_ref.shape[0]
    chunks = got_ref.shape[0] // slots
    groups, wide = slots // 16, 16 * chunks
    side = jnp.concatenate([got_ref[g * wide : (g + 1) * wide, :] for g in range(groups)], axis=1)
    turned = dot(shuffle(chunks, False), side)
    ids = jnp.concatenate([turned[wide - 16 :, g * LANES : (g + 1) * LANES] for g in range(groups)], axis=0)
    turned = turned.astype(BF16)
    rows = jnp.concatenate(
        [
            jnp.concatenate(
                [turned[k * 16 : k * 16 + 16, g * LANES : (g + 1) * LANES] for k in range(chunks - 1)], axis=1
            )
            for g in range(groups)
        ],
        axis=0,
    )
    full = dot_t(rows, down_ref[...])
    lane = iota((slots, LANES), 1)
    right = (lane >= 64).astype(F32)
    total = jnp.zeros((slots, LANES), F32)
    for q in range(full.shape[1] // LANES):
        total += jnp.where(ids == right + 2.0 * q, full[:, q * LANES : (q + 1) * LANES], 0.0)
    total = total + pltpu.roll(total, 64, 1)
    half = slots // 2
    partial_ref[...] = jnp.where(lane[:half] < 64, total[:half], total[half:])
    ids_ref[...] = ids
    for copy in copies:
        copy.wait()


def up_kernel(after_ref, after2_ref, a_ref, b_ref, c_ref, d_ref, ids_ref, up_ref, out_ref):
    total = (a_ref[...] + b_ref[...]) + (c_ref[...] + d_ref[...])
    turned = pltpu.roll(total, 64, 1)
    left = iota(total.shape, 1) < 64
    both = jnp.concatenate([jnp.where(left, total, turned), jnp.where(left, turned, total)], axis=0)
    ids = ids_ref[...]
    right = (iota(ids.shape, 1) >= 64).astype(F32)
    spread = [
        jnp.where(ids == right + 2.0 * q, both, 0.0).astype(BF16) for q in range(up_ref.shape[0] // LANES)
    ]
    out_ref[...] = dot(jnp.concatenate(spread, axis=1), up_ref[...]).astype(BF16)


def cache_kernel(scale, after_ref, length_ref, query_ref, key_ref, value_ref, sum_ref, top_ref, whole_ref):
    rows, length = key_ref.shape[0], key_ref.shape[1]
    wide = rows * GROUP
    by_head = jnp.concatenate([query_ref[:, h * LANES : (h + 1) * LANES] for h in range(GROUP)], axis=0)
    row, col = iota((wide, wide), 0), iota((wide, wide), 1)
    turn = jnp.where(col == (row % GROUP) * rows + row // GROUP, 1.0, 0.0).astype(BF16)
    by_row = dot(turn, by_head)
    position = iota((GROUP, length), 1).astype(F32)
    limit = jnp.broadcast_to(upright(length_ref[...].astype(F32)), (rows, length))
    scores = []
    for r in range(rows):
        query = by_row[r * GROUP : (r + 1) * GROUP].astype(BF16)
        score = dot_t(query, key_ref[r]) * scale
        scores.append(jnp.where(position < limit[r : r + 1], score, -jnp.inf))
    scores = jnp.concatenate(scores, axis=0)
    top = jnp.max(scores, axis=1, keepdims=True)
    weights = jnp.exp(scores - top)
    whole = jnp.broadcast_to(jnp.sum(weights, axis=1, keepdims=True), (wide, LANES))
    top = jnp.broadcast_to(top, (wide, LANES))
    for r in range(rows):
        some = slice(r * GROUP, (r + 1) * GROUP)
        place = pl.ds(r, GROUP, stride=rows)
        sum_ref[place, :] = dot(weights[some].astype(BF16), value_ref[r])
        top_ref[place, :] = top[some]
        whole_ref[place, :] = whole[some]


def mark_kernel(*refs):
    out_ref = refs[-1]
    out_ref[...] = jnp.zeros(out_ref.shape, F32)


def tables_kernel(pool, peers, after_ref, tenant_hbm, row_hbm, inverse_hbm, weight_hbm, weight_ref, cosine_ref, sine_ref,
                  back_ref, tenant_ref, row_ref, inverse_ref, sems):
    rows = back_ref.shape[0]
    copies = fetches(
        [(tenant_hbm, tenant_ref), (row_hbm, row_ref), (inverse_hbm, inverse_ref), (weight_hbm, weight_ref)], sems
    )
    for copy in copies[:3]:
        copy.wait()
    lane = iota((rows, LANES), 1)
    slot_col = upright(slots_of(tenant_ref[...].astype(F32), pool, peers, TURN))
    back_ref[...] = jnp.where(slot_col == lane.astype(F32), 1.0, 0.0).astype(BF16)
    angle = upright(row_ref[...].astype(F32)) * inverse_ref[...]
    sine = jnp.sin(angle)
    cosine_ref[...] = jnp.cos(angle)
    sine_ref[...] = jnp.where(lane < 64, -sine, sine)
    copies[-1].wait()


def join_kernel(after_ref, own_any, y1_any, y2_any, y3_any, near_ref, sems):
    rows = own_any.shape[0]
    blocks = enumerate((own_any, y1_any, y2_any, y3_any))
    for copy in fetches([(block, near_ref.at[pl.ds(k * rows, rows)]) for k, block in blocks], sems):
        copy.wait()


def late_kernel(scale, index_ref, near_ref, far_ref, weight_ref, query_ref, cosine_ref, sine_ref, sum_ref, top_ref,
                whole_ref, projected_ref, entry_ref, mixed_ref, share_ref):
    rows, depth = query_ref.shape[0], near_ref.shape[1]
    me = index_ref[0]
    devices = weight_ref.shape[0] // depth

    def part(block, other):
        start = pl.multiple_of(other * depth, depth)
        return dot(block, weight_ref[pl.ds(start, depth), :])

    total = jnp.zeros((rows, 2 * LANES), F32)
    for shift in range(devices // 2):
        other = (me + devices - 2 * shift) % devices
        block = slice(shift * rows, (shift + 1) * rows)
        total += part(near_ref[block], other) + part(far_ref[block], other ^ 1)
    projected_ref[...] = total[:, LANES:]
    key = total[:, :LANES]
    key = (key * cosine_ref[...] + pltpu.roll(key, 64, 1) * sine_ref[...]).astype(BF16)
    entry_ref[...] = key
    key = key.astype(F32)
    for h in range(GROUP):
        place = slice(h * rows, (h + 1) * rows)
        query = query_ref[:, h * LANES : (h + 1) * LANES].astype(F32)
        own = jnp.sum(query * key, axis=1, keepdims=True) * scale
        top = top_ref[place, :]
        highest = jnp.maximum(top, own)
        old, new = jnp.exp(top - highest), jnp.exp(own - highest)
        under = 1.0 / (old * whole_ref[place, :] + new)
        mixed_ref[place, :] = sum_ref[place, :] * (old * under)
        share_ref[place, :] = new * under


def final_kernel(got_ref, back_ref, value_ref, key_ref, mixed_ref, share_ref, out_ref, entry_ref):
    rows = value_ref.shape[0]
    slots = got_ref.shape[0]
    delta = dot(back_ref[:, :slots], got_ref[...])
    value = (value_ref[...] + delta).astype(BF16)
    entry_ref[:, :LANES] = key_ref[...]
    entry_ref[:, LANES:] = value
    value = value.astype(F32)
    for h in range(GROUP):
        place = slice(h * rows, (h + 1) * rows)
        out_ref[:, h * LANES : (h + 1) * LANES] = (mixed_ref[place, :] + share_ref[place, :] * value).astype(BF16)


def on_device(hidden, queries, key_cache, value_cache, lengths, tenants, weight, down, up):
    rows, depth = hidden.shape
    peers = lax.axis_size("dp")
    count = lax.axis_size("tensor")
    slots = peers * CAPACITY
    pool, _, rank = down.shape
    chunks = depth // LANES + 1
    scale = HEAD_SIZE ** -0.5
    shape, vmem, dma = jax.ShapeDtypeStruct, pltpu.VMEM, pltpu.SemaphoreType.DMA
    params = lambda size: pltpu.CompilerParams(vmem_limit_bytes=size * MIB)
    far = lambda *arrays: [pltpu.with_memory_space_constraint(x, pltpu.HBM) for x in arrays]
    cost = lambda flops, size: pl.CostEstimate(flops=flops, bytes_accessed=size, transcendentals=0)

    tenant_row = tenants.reshape(1, rows)
    length_row = lengths.reshape(1, rows)
    me = lax.axis_index("tensor").astype(I32).reshape(1)
    over_core = lambda x: lax.ppermute(x, "tensor", [(i, i ^ 1) for i in range(count)])
    over_y = lambda x, k: lax.ppermute(x, "tensor", [(i, (i + 2 * k) % count) for i in range(count)])

    ring = [[(k + TURN) % peers for k in range(peers)]]
    inverse = ROPE_BASE ** (-(np.arange(HEAD_SIZE // 2, dtype=np.float32) * 2.0) / HEAD_SIZE)
    inverse = jnp.asarray(np.concatenate([inverse, inverse])[None, :], F32)

    with jax.named_scope("place"):
        placed, handed = pl.pallas_call(
            lambda *refs: place_kernel(pool, *refs),
            out_shape=[shape((slots * chunks, LANES), BF16), shape((rows, depth), BF16)],
            in_specs=[HBM] * 2, out_specs=[VMEM] * 2, compiler_params=params(8),
            scratch_shapes=[vmem((1, rows), I32), dma((2,))],
        )(*far(tenant_row, hidden))
    with jax.named_scope("rows_to_owners"):
        got = lax.all_to_all(
            placed.reshape(peers, chunks, CAPACITY, LANES), "dp", split_axis=0, concat_axis=0, tiled=True, axis_index_groups=ring
        ).reshape(slots * chunks, LANES)
    with jax.named_scope("gather_hidden"):
        others = [over_y(handed, k) for k in (1, 2, 3)]
    with jax.named_scope("mark"):
        mark = pl.pallas_call(
            mark_kernel, out_shape=shape((8, LANES), F32), in_specs=[ANY] + [HBM] * 2, out_specs=VMEM,
            compiler_params=params(2),
        )(placed, *far(key_cache, value_cache))
    with jax.named_scope("down"):
        partial, ids, up_near, queries_near, length_near = pl.pallas_call(
            down_kernel,
            out_shape=[
                shape((slots // 2, LANES), F32), shape((slots, LANES), F32), shape((pool * rank, LANES), BF16),
                shape(queries.shape, BF16), shape((1, rows), I32),
            ],
            in_specs=[VMEM] * 2 + [HBM] * 3 + [ANY], out_specs=[VMEM] * 5, compiler_params=params(8),
            scratch_shapes=[dma((3,))],
        )(got, jnp.swapaxes(down, 1, 2).reshape(pool * rank, depth),
          *far(up.reshape(pool * rank, LANES), queries, length_row), mark)
    with jax.named_scope("reduce"):
        pair_sum = partial + over_core(partial)
        sums_y = [over_y(pair_sum, k) for k in (1, 2, 3)]
    with jax.named_scope("join"):
        near = pl.pallas_call(
            join_kernel, out_shape=shape((4 * rows, depth), BF16), in_specs=[ANY] * 5, out_specs=VMEM,
            scratch_shapes=[dma((4,))], compiler_params=params(4),
        )(pair_sum, handed, *others)
    with jax.named_scope("gather_core"):
        other = over_core(near)
    with jax.named_scope("mark2"):
        mark = pl.pallas_call(
            mark_kernel, out_shape=shape((8, LANES), F32), in_specs=[ANY] + [HBM] * MARKS, out_specs=VMEM,
            compiler_params=params(2),
        )(pair_sum, *far(key_cache, value_cache, weight)[:MARKS])
    with jax.named_scope("cache"):
        states = pl.pallas_call(
            lambda *refs: cache_kernel(scale, *refs),
            out_shape=[shape((GROUP * rows, LANES), F32)] * 3,
            in_specs=[ANY] + [VMEM] * 4, out_specs=[VMEM] * 3, compiler_params=params(8),
        )(mark, length_near, queries_near, key_cache, value_cache)
    with jax.named_scope("up"):
        served = pl.pallas_call(
            up_kernel, out_shape=shape((slots, LANES), BF16),
            in_specs=[ANY] * 2 + [VMEM] * 6, out_specs=VMEM, compiler_params=params(8),
        )(near, states[0], pair_sum, *sums_y, ids, up_near)
    with jax.named_scope("answers"):
        returned = lax.all_to_all(
            served.reshape(peers, CAPACITY, LANES), "dp", split_axis=0, concat_axis=0, tiled=True, axis_index_groups=ring
        ).reshape(slots, LANES)
    with jax.named_scope("tables"):
        weight_near, cosine, sine, back = pl.pallas_call(
            lambda *refs: tables_kernel(pool, peers, *refs),
            out_shape=[
                shape(weight.shape, BF16), shape((rows, LANES), F32), shape((rows, LANES), F32),
                shape((rows, LANES), BF16),
            ],
            in_specs=[ANY] + [HBM] * 4, out_specs=[VMEM] * 4,
            scratch_shapes=[vmem((1, rows), I32), vmem((1, rows), I32), vmem((1, LANES), F32), dma((4,))],
            compiler_params=params(8),
        )(served, *far(tenant_row, length_row, inverse, weight))
    with jax.named_scope("late"):
        value, key, mixed, share = pl.pallas_call(
            lambda *refs: late_kernel(scale, *refs),
            out_shape=[shape((rows, LANES), F32), shape((rows, LANES), BF16)] + [shape((GROUP * rows, LANES), F32)] * 2,
            in_specs=[SMEM] + [VMEM] * 9, out_specs=[VMEM] * 4, compiler_params=params(8),
            cost_estimate=cost(2 * rows * count * depth * 2 * LANES, weight.size * 2),
        )(me, near, other, weight_near, queries_near, cosine, sine, *states)
    with jax.named_scope("finish"):
        return tuple(pl.pallas_call(
            final_kernel,
            out_shape=[shape((rows, GROUP * LANES), BF16), shape((rows, 2 * LANES), BF16)],
            in_specs=[VMEM] * 6, out_specs=[VMEM] * 2, compiler_params=params(8),
        )(returned, back, value, key, mixed, share))


def solution(mesh):
    in_specs = (
        P("dp", "tensor"),
        P("dp", "tensor"),
        P("dp", None, "tensor"),
        P("dp", None, "tensor"),
        P("dp"),
        P("dp"),
        P(None, "tensor"),
        P("dp", "tensor", None),
        P("dp", None, "tensor"),
    )
    out_specs = (P("dp", "tensor"), P("dp", "tensor"))
    return jax.shard_map(
        on_device, mesh=mesh, in_specs=in_specs, out_specs=out_specs, check_vma=False
    )
```

```python
import jax
import jax.numpy as jnp
import numpy as np
from jax import lax
from jax.experimental import pallas as pl
from jax.experimental.pallas import tpu as pltpu
from jax.sharding import PartitionSpec as P

HEAD_SIZE = 128
GROUP = 8
CAPACITY = 2
LANES = 128
ROPE_BASE = 500000.0
MIB = 1 << 20
TURN = 22
BACK_TURN = 18
MARKS = 3

F32, BF16, I32 = jnp.float32, jnp.bfloat16, jnp.int32
VMEM = pl.BlockSpec(memory_space=pltpu.VMEM)
SMEM = pl.BlockSpec(memory_space=pltpu.SMEM)
HBM = pl.BlockSpec(memory_space=pltpu.HBM)
ANY = pl.BlockSpec(memory_space=pl.ANY)


def iota(shape, dim):
    return lax.broadcasted_iota(I32, shape, dim)


def dot(a, b):
    return jnp.dot(a, b, preferred_element_type=F32)


def dot_t(a, b):
    return lax.dot_general(a, b, (((1,), (1,)), ((), ())), preferred_element_type=F32)


def upright(row):
    n = row.shape[1]
    spread = jnp.broadcast_to(row, (n, n))
    return jnp.sum(jnp.where(iota((n, n), 0) == iota((n, n), 1), spread, 0.0), axis=1, keepdims=True)


def shuffle(chunks, forward):
    wide = 16 * chunks
    row, col = iota((wide, wide), 0), iota((wide, wide), 1)
    chunked, message = (col, row) if forward else (row, col)
    k, s, c = chunked >> 4, (chunked >> 1) & 7, chunked & 1
    return jnp.where(message == s * (2 * chunks) + k * 2 + c, 1.0, 0.0).astype(BF16)


def slots_of(tenant_row, pool, peers, turn):
    n = tenant_row.shape[1]
    owner_row = jnp.floor(tenant_row * (1.0 / pool)) - turn
    owner_row = jnp.where(owner_row < 0.0, owner_row + peers, owner_row)
    owner_col = upright(owner_row)
    same = (owner_col == owner_row) & (iota((n, n), 0) < iota((n, n), 1))
    rank = jnp.sum(jnp.where(same, 1.0, 0.0), axis=0, keepdims=True)
    return owner_row * CAPACITY + rank


def fetches(pairs, sems):
    copies = [pltpu.make_async_copy(source, target, sems.at[i]) for i, (source, target) in enumerate(pairs)]
    for copy in copies:
        copy.start()
    return copies


def place_kernel(pool, tenant_hbm, hidden_hbm, out_ref, hidden_ref, tenant_ref, sems):
    fetch_hidden = pltpu.make_async_copy(hidden_hbm, hidden_ref, sems.at[0])
    fetch_tenant = pltpu.make_async_copy(tenant_hbm, tenant_ref, sems.at[1])
    fetch_tenant.start()
    fetch_hidden.start()
    rows, width = hidden_ref.shape
    chunks = width // LANES + 1
    slots = out_ref.shape[0] // chunks
    mix = shuffle(chunks, True)
    fetch_tenant.wait()
    tenant_row = tenant_ref[...].astype(F32)
    slot_row = slots_of(tenant_row, pool, slots // CAPACITY, TURN)
    place = jnp.where(slot_row == iota((slots, rows), 0).astype(F32), 1.0, 0.0).astype(BF16)
    local = tenant_row - pool * jnp.floor(tenant_row * (1.0 / pool))
    local = jnp.broadcast_to(upright(local), (rows, LANES)).astype(BF16)
    fetch_hidden.wait()
    placed = jnp.concatenate([dot(place, hidden_ref[...]), dot(place, local)], axis=1).astype(BF16)
    groups = slots // 16
    side = jnp.concatenate(
        [
            jnp.concatenate(
                [placed[g * 16 : g * 16 + 16, k * LANES : (k + 1) * LANES] for k in range(chunks)], axis=0
            )
            for g in range(groups)
        ],
        axis=1,
    )
    turned = dot(mix, side).astype(BF16)
    wide = 16 * chunks
    for g in range(groups):
        out_ref[g * wide : (g + 1) * wide, :] = turned[:, g * LANES : (g + 1) * LANES]


def down_kernel(got_ref, down_ref, up_hbm, query_hbm, length_hbm, after_ref, partial_ref, ids_ref, up_ref, query_ref,
                length_ref, sems):
    copies = fetches([(up_hbm, up_ref), (query_hbm, query_ref), (length_hbm, length_ref)], sems)
    slots = ids_ref.shape[0]
    chunks = got_ref.shape[0] // slots
    groups, wide = slots // 16, 16 * chunks
    side = jnp.concatenate([got_ref[g * wide : (g + 1) * wide, :] for g in range(groups)], axis=1)
    turned = dot(shuffle(chunks, False), side)
    ids = jnp.concatenate([turned[wide - 16 :, g * LANES : (g + 1) * LANES] for g in range(groups)], axis=0)
    turned = turned.astype(BF16)
    rows = jnp.concatenate(
        [
            jnp.concatenate(
                [turned[k * 16 : k * 16 + 16, g * LANES : (g + 1) * LANES] for k in range(chunks - 1)], axis=1
            )
            for g in range(groups)
        ],
        axis=0,
    )
    full = dot_t(rows, down_ref[...])
    lane = iota((slots, LANES), 1)
    right = (lane >= 64).astype(F32)
    total = jnp.zeros((slots, LANES), F32)
    for q in range(full.shape[1] // LANES):
        total += jnp.where(ids == right + 2.0 * q, full[:, q * LANES : (q + 1) * LANES], 0.0)
    total = total + pltpu.roll(total, 64, 1)
    half = slots // 2
    partial_ref[...] = jnp.where(lane[:half] < 64, total[:half], total[half:])
    ids_ref[...] = ids
    for copy in copies:
        copy.wait()


def up_kernel(after_ref, after2_ref, a_ref, b_ref, c_ref, d_ref, ids_ref, up_ref, out_ref):
    rows = out_ref.shape[0]
    head = (BACK_TURN - TURN) * CAPACITY % rows
    total = (a_ref[...] + b_ref[...]) + (c_ref[...] + d_ref[...])
    turned = pltpu.roll(total, 64, 1)
    left = iota(total.shape, 1) < 64
    both = jnp.concatenate([jnp.where(left, total, turned), jnp.where(left, turned, total)], axis=0)
    ids = ids_ref[...]
    right = (iota(ids.shape, 1) >= 64).astype(F32)
    spread = [
        jnp.where(ids == right + 2.0 * q, both, 0.0).astype(BF16) for q in range(up_ref.shape[0] // LANES)
    ]
    served = dot(jnp.concatenate(spread, axis=1), up_ref[...])
    if head:
        served = jnp.concatenate([served[head:], served[:head]], axis=0)
    out_ref[...] = served.astype(BF16)


def cache_kernel(scale, after_ref, length_ref, query_ref, key_ref, value_ref, sum_ref, top_ref, whole_ref):
    rows, length = key_ref.shape[0], key_ref.shape[1]
    wide = rows * GROUP
    by_head = jnp.concatenate([query_ref[:, h * LANES : (h + 1) * LANES] for h in range(GROUP)], axis=0)
    row, col = iota((wide, wide), 0), iota((wide, wide), 1)
    turn = jnp.where(col == (row % GROUP) * rows + row // GROUP, 1.0, 0.0).astype(BF16)
    by_row = dot(turn, by_head)
    position = iota((GROUP, length), 1).astype(F32)
    limit = jnp.broadcast_to(upright(length_ref[...].astype(F32)), (rows, length))
    scores = []
    for r in range(rows):
        query = by_row[r * GROUP : (r + 1) * GROUP].astype(BF16)
        score = dot_t(query, key_ref[r]) * scale
        scores.append(jnp.where(position < limit[r : r + 1], score, -jnp.inf))
    scores = jnp.concatenate(scores, axis=0)
    top = jnp.max(scores, axis=1, keepdims=True)
    weights = jnp.exp(scores - top)
    whole = jnp.broadcast_to(jnp.sum(weights, axis=1, keepdims=True), (wide, LANES))
    top = jnp.broadcast_to(top, (wide, LANES))
    for r in range(rows):
        some = slice(r * GROUP, (r + 1) * GROUP)
        place = pl.ds(r, GROUP, stride=rows)
        sum_ref[place, :] = dot(weights[some].astype(BF16), value_ref[r])
        top_ref[place, :] = top[some]
        whole_ref[place, :] = whole[some]


def mark_kernel(*refs):
    out_ref = refs[-1]
    out_ref[...] = jnp.zeros(out_ref.shape, F32)


def tables_kernel(pool, peers, after_ref, tenant_hbm, row_hbm, inverse_hbm, weight_hbm, weight_ref, cosine_ref, sine_ref,
                  back_ref, tenant_ref, row_ref, inverse_ref, sems):
    rows = back_ref.shape[0]
    copies = fetches(
        [(tenant_hbm, tenant_ref), (row_hbm, row_ref), (inverse_hbm, inverse_ref), (weight_hbm, weight_ref)], sems
    )
    for copy in copies[:3]:
        copy.wait()
    lane = iota((rows, LANES), 1)
    slot_col = upright(slots_of(tenant_ref[...].astype(F32), pool, peers, BACK_TURN))
    back_ref[...] = jnp.where(slot_col == lane.astype(F32), 1.0, 0.0).astype(BF16)
    angle = upright(row_ref[...].astype(F32)) * inverse_ref[...]
    sine = jnp.sin(angle)
    cosine_ref[...] = jnp.cos(angle)
    sine_ref[...] = jnp.where(lane < 64, -sine, sine)
    copies[-1].wait()


def join_kernel(after_ref, own_any, y1_any, y2_any, y3_any, near_ref, sems):
    rows = own_any.shape[0]
    blocks = enumerate((own_any, y1_any, y2_any, y3_any))
    for copy in fetches([(block, near_ref.at[pl.ds(k * rows, rows)]) for k, block in blocks], sems):
        copy.wait()


def late_kernel(scale, index_ref, near_ref, far_ref, weight_ref, query_ref, cosine_ref, sine_ref, sum_ref, top_ref,
                whole_ref, projected_ref, entry_ref, mixed_ref, share_ref):
    rows, depth = query_ref.shape[0], near_ref.shape[1]
    me = index_ref[0]
    devices = weight_ref.shape[0] // depth

    def part(block, other):
        start = pl.multiple_of(other * depth, depth)
        return dot(block, weight_ref[pl.ds(start, depth), :])

    total = jnp.zeros((rows, 2 * LANES), F32)
    for shift in range(devices // 2):
        other = (me + devices - 2 * shift) % devices
        block = slice(shift * rows, (shift + 1) * rows)
        total += part(near_ref[block], other) + part(far_ref[block], other ^ 1)
    projected_ref[...] = total[:, LANES:]
    key = total[:, :LANES]
    key = (key * cosine_ref[...] + pltpu.roll(key, 64, 1) * sine_ref[...]).astype(BF16)
    entry_ref[...] = key
    key = key.astype(F32)
    for h in range(GROUP):
        place = slice(h * rows, (h + 1) * rows)
        query = query_ref[:, h * LANES : (h + 1) * LANES].astype(F32)
        own = jnp.sum(query * key, axis=1, keepdims=True) * scale
        top = top_ref[place, :]
        highest = jnp.maximum(top, own)
        old, new = jnp.exp(top - highest), jnp.exp(own - highest)
        under = 1.0 / (old * whole_ref[place, :] + new)
        mixed_ref[place, :] = sum_ref[place, :] * (old * under)
        share_ref[place, :] = new * under


def final_kernel(got_ref, back_ref, value_ref, key_ref, mixed_ref, share_ref, out_ref, entry_ref):
    rows = value_ref.shape[0]
    slots = got_ref.shape[0]
    delta = dot(back_ref[:, :slots], got_ref[...])
    value = (value_ref[...] + delta).astype(BF16)
    entry_ref[:, :LANES] = key_ref[...]
    entry_ref[:, LANES:] = value
    value = value.astype(F32)
    for h in range(GROUP):
        place = slice(h * rows, (h + 1) * rows)
        out_ref[:, h * LANES : (h + 1) * LANES] = (mixed_ref[place, :] + share_ref[place, :] * value).astype(BF16)


def on_device(hidden, queries, key_cache, value_cache, lengths, tenants, weight, down, up):
    rows, depth = hidden.shape
    peers = lax.axis_size("dp")
    count = lax.axis_size("tensor")
    slots = peers * CAPACITY
    pool, _, rank = down.shape
    chunks = depth // LANES + 1
    scale = HEAD_SIZE ** -0.5
    shape, vmem, dma = jax.ShapeDtypeStruct, pltpu.VMEM, pltpu.SemaphoreType.DMA
    params = lambda size: pltpu.CompilerParams(vmem_limit_bytes=size * MIB)
    far = lambda *arrays: [pltpu.with_memory_space_constraint(x, pltpu.HBM) for x in arrays]
    cost = lambda flops, size: pl.CostEstimate(flops=flops, bytes_accessed=size, transcendentals=0)

    tenant_row = tenants.reshape(1, rows)
    length_row = lengths.reshape(1, rows)
    me = lax.axis_index("tensor").astype(I32).reshape(1)
    over_core = lambda x: lax.ppermute(x, "tensor", [(i, i ^ 1) for i in range(count)])
    over_y = lambda x, k: lax.ppermute(x, "tensor", [(i, (i + 2 * k) % count) for i in range(count)])

    ring = [[(k + TURN) % peers for k in range(peers)]]
    back_ring = [[(k + BACK_TURN) % peers for k in range(peers)]]
    inverse = ROPE_BASE ** (-(np.arange(HEAD_SIZE // 2, dtype=np.float32) * 2.0) / HEAD_SIZE)
    inverse = jnp.asarray(np.concatenate([inverse, inverse])[None, :], F32)

    with jax.named_scope("place"):
        placed, handed = pl.pallas_call(
            lambda *refs: place_kernel(pool, *refs),
            out_shape=[shape((slots * chunks, LANES), BF16), shape((rows, depth), BF16)],
            in_specs=[HBM] * 2, out_specs=[VMEM] * 2, compiler_params=params(8),
            scratch_shapes=[vmem((1, rows), I32), dma((2,))],
        )(*far(tenant_row, hidden))
    with jax.named_scope("rows_to_owners"):
        got = lax.all_to_all(
            placed.reshape(peers, chunks, CAPACITY, LANES), "dp", split_axis=0, concat_axis=0, tiled=True, axis_index_groups=ring
        ).reshape(slots * chunks, LANES)
    with jax.named_scope("gather_hidden"):
        others = [over_y(handed, k) for k in (1, 2, 3)]
    with jax.named_scope("mark"):
        mark = pl.pallas_call(
            mark_kernel, out_shape=shape((8, LANES), F32), in_specs=[ANY] + [HBM] * 2, out_specs=VMEM,
            compiler_params=params(2),
        )(placed, *far(key_cache, value_cache))
    with jax.named_scope("down"):
        partial, ids, up_near, queries_near, length_near = pl.pallas_call(
            down_kernel,
            out_shape=[
                shape((slots // 2, LANES), F32), shape((slots, LANES), F32), shape((pool * rank, LANES), BF16),
                shape(queries.shape, BF16), shape((1, rows), I32),
            ],
            in_specs=[VMEM] * 2 + [HBM] * 3 + [ANY], out_specs=[VMEM] * 5, compiler_params=params(8),
            scratch_shapes=[dma((3,))],
        )(got, jnp.swapaxes(down, 1, 2).reshape(pool * rank, depth),
          *far(up.reshape(pool * rank, LANES), queries, length_row), mark)
    with jax.named_scope("reduce"):
        pair_sum = partial + over_core(partial)
        sums_y = [over_y(pair_sum, k) for k in (1, 2, 3)]
    with jax.named_scope("join"):
        near = pl.pallas_call(
            join_kernel, out_shape=shape((4 * rows, depth), BF16), in_specs=[ANY] * 5, out_specs=VMEM,
            scratch_shapes=[dma((4,))], compiler_params=params(4),
        )(pair_sum, handed, *others)
    with jax.named_scope("gather_core"):
        other = over_core(near)
    with jax.named_scope("mark2"):
        mark = pl.pallas_call(
            mark_kernel, out_shape=shape((8, LANES), F32), in_specs=[ANY] + [HBM] * MARKS, out_specs=VMEM,
            compiler_params=params(2),
        )(pair_sum, *far(key_cache, value_cache, weight)[:MARKS])
    with jax.named_scope("cache"):
        states = pl.pallas_call(
            lambda *refs: cache_kernel(scale, *refs),
            out_shape=[shape((GROUP * rows, LANES), F32)] * 3,
            in_specs=[ANY] + [VMEM] * 4, out_specs=[VMEM] * 3, compiler_params=params(8),
        )(mark, length_near, queries_near, key_cache, value_cache)
    with jax.named_scope("up"):
        served = pl.pallas_call(
            up_kernel, out_shape=shape((slots, LANES), BF16),
            in_specs=[ANY] * 2 + [VMEM] * 6, out_specs=VMEM, compiler_params=params(8),
        )(near, states[0], pair_sum, *sums_y, ids, up_near)
    with jax.named_scope("answers"):
        returned = lax.all_to_all(
            served.reshape(peers, CAPACITY, LANES), "dp", split_axis=0, concat_axis=0, tiled=True, axis_index_groups=back_ring
        ).reshape(slots, LANES)
    with jax.named_scope("tables"):
        weight_near, cosine, sine, back = pl.pallas_call(
            lambda *refs: tables_kernel(pool, peers, *refs),
            out_shape=[
                shape(weight.shape, BF16), shape((rows, LANES), F32), shape((rows, LANES), F32),
                shape((rows, LANES), BF16),
            ],
            in_specs=[ANY] + [HBM] * 4, out_specs=[VMEM] * 4,
            scratch_shapes=[vmem((1, rows), I32), vmem((1, rows), I32), vmem((1, LANES), F32), dma((4,))],
            compiler_params=params(8),
        )(served, *far(tenant_row, length_row, inverse, weight))
    with jax.named_scope("late"):
        value, key, mixed, share = pl.pallas_call(
            lambda *refs: late_kernel(scale, *refs),
            out_shape=[shape((rows, LANES), F32), shape((rows, LANES), BF16)] + [shape((GROUP * rows, LANES), F32)] * 2,
            in_specs=[SMEM] + [VMEM] * 9, out_specs=[VMEM] * 4, compiler_params=params(8),
            cost_estimate=cost(2 * rows * count * depth * 2 * LANES, weight.size * 2),
        )(me, near, other, weight_near, queries_near, cosine, sine, *states)
    with jax.named_scope("finish"):
        return tuple(pl.pallas_call(
            final_kernel,
            out_shape=[shape((rows, GROUP * LANES), BF16), shape((rows, 2 * LANES), BF16)],
            in_specs=[VMEM] * 6, out_specs=[VMEM] * 2, compiler_params=params(8),
        )(returned, back, value, key, mixed, share))


def solution(mesh):
    in_specs = (
        P("dp", "tensor"),
        P("dp", "tensor"),
        P("dp", None, "tensor"),
        P("dp", None, "tensor"),
        P("dp"),
        P("dp"),
        P(None, "tensor"),
        P("dp", "tensor", None),
        P("dp", None, "tensor"),
    )
    out_specs = (P("dp", "tensor"), P("dp", "tensor"))
    return jax.shard_map(
        on_device, mesh=mesh, in_specs=in_specs, out_specs=out_specs, check_vma=False
    )
```

```python
import jax
import jax.numpy as jnp
import numpy as np
from jax import lax
from jax.experimental import pallas as pl
from jax.experimental.pallas import tpu as pltpu
from jax.sharding import PartitionSpec as P

HEAD_SIZE = 128
GROUP = 8
CAPACITY = 2
LANES = 128
ROPE_BASE = 500000.0
MIB = 1 << 20
TURN = 22
BACK_TURN = 18
MARKS = 3
AHEAD_CHIPS = 2

F32, BF16, I32 = jnp.float32, jnp.bfloat16, jnp.int32
VMEM = pl.BlockSpec(memory_space=pltpu.VMEM)
SMEM = pl.BlockSpec(memory_space=pltpu.SMEM)
HBM = pl.BlockSpec(memory_space=pltpu.HBM)
ANY = pl.BlockSpec(memory_space=pl.ANY)


def iota(shape, dim):
    return lax.broadcasted_iota(I32, shape, dim)


def dot(a, b):
    return jnp.dot(a, b, preferred_element_type=F32)


def dot_t(a, b):
    return lax.dot_general(a, b, (((1,), (1,)), ((), ())), preferred_element_type=F32)


def upright(row):
    n = row.shape[1]
    spread = jnp.broadcast_to(row, (n, n))
    return jnp.sum(jnp.where(iota((n, n), 0) == iota((n, n), 1), spread, 0.0), axis=1, keepdims=True)


def shuffle(chunks, forward):
    wide = 16 * chunks
    row, col = iota((wide, wide), 0), iota((wide, wide), 1)
    chunked, message = (col, row) if forward else (row, col)
    k, s, c = chunked >> 4, (chunked >> 1) & 7, chunked & 1
    return jnp.where(message == s * (2 * chunks) + k * 2 + c, 1.0, 0.0).astype(BF16)


def slots_of(tenant_row, pool, peers, turn):
    n = tenant_row.shape[1]
    owner_row = jnp.floor(tenant_row * (1.0 / pool)) - turn
    owner_row = jnp.where(owner_row < 0.0, owner_row + peers, owner_row)
    owner_col = upright(owner_row)
    same = (owner_col == owner_row) & (iota((n, n), 0) < iota((n, n), 1))
    rank = jnp.sum(jnp.where(same, 1.0, 0.0), axis=0, keepdims=True)
    return owner_row * CAPACITY + rank


def fetches(pairs, sems):
    copies = [pltpu.make_async_copy(source, target, sems.at[i]) for i, (source, target) in enumerate(pairs)]
    for copy in copies:
        copy.start()
    return copies


def place_kernel(pool, tenant_hbm, hidden_hbm, out_ref, hidden_ref, tenant_ref, sems):
    fetch_hidden = pltpu.make_async_copy(hidden_hbm, hidden_ref, sems.at[0])
    fetch_tenant = pltpu.make_async_copy(tenant_hbm, tenant_ref, sems.at[1])
    fetch_tenant.start()
    fetch_hidden.start()
    rows, width = hidden_ref.shape
    chunks = width // LANES + 1
    slots = out_ref.shape[0] // chunks
    mix = shuffle(chunks, True)
    fetch_tenant.wait()
    tenant_row = tenant_ref[...].astype(F32)
    slot_row = slots_of(tenant_row, pool, slots // CAPACITY, TURN)
    place = jnp.where(slot_row == iota((slots, rows), 0).astype(F32), 1.0, 0.0).astype(BF16)
    local = tenant_row - pool * jnp.floor(tenant_row * (1.0 / pool))
    local = jnp.broadcast_to(upright(local), (rows, LANES)).astype(BF16)
    fetch_hidden.wait()
    placed = jnp.concatenate([dot(place, hidden_ref[...]), dot(place, local)], axis=1).astype(BF16)
    groups = slots // 16
    side = jnp.concatenate(
        [
            jnp.concatenate(
                [placed[g * 16 : g * 16 + 16, k * LANES : (k + 1) * LANES] for k in range(chunks)], axis=0
            )
            for g in range(groups)
        ],
        axis=1,
    )
    turned = dot(mix, side).astype(BF16)
    wide = 16 * chunks
    for g in range(groups):
        out_ref[g * wide : (g + 1) * wide, :] = turned[:, g * LANES : (g + 1) * LANES]


def down_kernel(got_ref, down_ref, up_hbm, query_hbm, length_hbm, after_ref, partial_ref, ids_ref, up_ref, query_ref,
                length_ref, sems):
    copies = fetches([(up_hbm, up_ref), (query_hbm, query_ref), (length_hbm, length_ref)], sems)
    slots = ids_ref.shape[0]
    chunks = got_ref.shape[0] // slots
    groups, wide = slots // 16, 16 * chunks
    side = jnp.concatenate([got_ref[g * wide : (g + 1) * wide, :] for g in range(groups)], axis=1)
    turned = dot(shuffle(chunks, False), side)
    ids = jnp.concatenate([turned[wide - 16 :, g * LANES : (g + 1) * LANES] for g in range(groups)], axis=0)
    turned = turned.astype(BF16)
    rows = jnp.concatenate(
        [
            jnp.concatenate(
                [turned[k * 16 : k * 16 + 16, g * LANES : (g + 1) * LANES] for k in range(chunks - 1)], axis=1
            )
            for g in range(groups)
        ],
        axis=0,
    )
    full = dot_t(rows, down_ref[...])
    lane = iota((slots, LANES), 1)
    right = (lane >= 64).astype(F32)
    total = jnp.zeros((slots, LANES), F32)
    for q in range(full.shape[1] // LANES):
        total += jnp.where(ids == right + 2.0 * q, full[:, q * LANES : (q + 1) * LANES], 0.0)
    total = total + pltpu.roll(total, 64, 1)
    half = slots // 2
    partial_ref[...] = jnp.where(lane[:half] < 64, total[:half], total[half:])
    ids_ref[...] = ids
    for copy in copies:
        copy.wait()


def up_kernel(after_ref, after2_ref, a_ref, b_ref, c_ref, d_ref, ids_ref, up_ref, out_ref):
    rows = out_ref.shape[0]
    head = (BACK_TURN - TURN) * CAPACITY % rows
    total = (a_ref[...] + b_ref[...]) + (c_ref[...] + d_ref[...])
    turned = pltpu.roll(total, 64, 1)
    left = iota(total.shape, 1) < 64
    both = jnp.concatenate([jnp.where(left, total, turned), jnp.where(left, turned, total)], axis=0)
    ids = ids_ref[...]
    right = (iota(ids.shape, 1) >= 64).astype(F32)
    spread = [
        jnp.where(ids == right + 2.0 * q, both, 0.0).astype(BF16) for q in range(up_ref.shape[0] // LANES)
    ]
    served = dot(jnp.concatenate(spread, axis=1), up_ref[...])
    if head:
        served = jnp.concatenate([served[head:], served[:head]], axis=0)
    out_ref[...] = served.astype(BF16)


def cache_kernel(scale, after_ref, length_ref, query_ref, key_ref, value_ref, weight_hbm, sum_ref, top_ref, whole_ref,
                 weight_ref, sem):
    fetch_weight = pltpu.make_async_copy(weight_hbm.at[pl.ds(0, weight_ref.shape[0])], weight_ref, sem)
    fetch_weight.start()
    rows, length = key_ref.shape[0], key_ref.shape[1]
    wide = rows * GROUP
    by_head = jnp.concatenate([query_ref[:, h * LANES : (h + 1) * LANES] for h in range(GROUP)], axis=0)
    row, col = iota((wide, wide), 0), iota((wide, wide), 1)
    turn = jnp.where(col == (row % GROUP) * rows + row // GROUP, 1.0, 0.0).astype(BF16)
    by_row = dot(turn, by_head)
    position = iota((GROUP, length), 1).astype(F32)
    limit = jnp.broadcast_to(upright(length_ref[...].astype(F32)), (rows, length))
    scores = []
    for r in range(rows):
        query = by_row[r * GROUP : (r + 1) * GROUP].astype(BF16)
        score = dot_t(query, key_ref[r]) * scale
        scores.append(jnp.where(position < limit[r : r + 1], score, -jnp.inf))
    scores = jnp.concatenate(scores, axis=0)
    top = jnp.max(scores, axis=1, keepdims=True)
    weights = jnp.exp(scores - top)
    whole = jnp.broadcast_to(jnp.sum(weights, axis=1, keepdims=True), (wide, LANES))
    top = jnp.broadcast_to(top, (wide, LANES))
    for r in range(rows):
        some = slice(r * GROUP, (r + 1) * GROUP)
        place = pl.ds(r, GROUP, stride=rows)
        sum_ref[place, :] = dot(weights[some].astype(BF16), value_ref[r])
        top_ref[place, :] = top[some]
        whole_ref[place, :] = whole[some]
    fetch_weight.wait()


def mark_kernel(*refs):
    out_ref = refs[-1]
    out_ref[...] = jnp.zeros(out_ref.shape, F32)


def tables_kernel(pool, peers, after_ref, tenant_hbm, row_hbm, inverse_hbm, weight_hbm, weight_ref, cosine_ref, sine_ref,
                  back_ref, tenant_ref, row_ref, inverse_ref, sems):
    rows = back_ref.shape[0]
    copies = fetches(
        [
            (tenant_hbm, tenant_ref), (row_hbm, row_ref), (inverse_hbm, inverse_ref),
            (weight_hbm.at[pl.ds(weight_hbm.shape[0] - weight_ref.shape[0], weight_ref.shape[0])], weight_ref),
        ],
        sems,
    )
    for copy in copies[:3]:
        copy.wait()
    lane = iota((rows, LANES), 1)
    slot_col = upright(slots_of(tenant_ref[...].astype(F32), pool, peers, BACK_TURN))
    back_ref[...] = jnp.where(slot_col == lane.astype(F32), 1.0, 0.0).astype(BF16)
    angle = upright(row_ref[...].astype(F32)) * inverse_ref[...]
    sine = jnp.sin(angle)
    cosine_ref[...] = jnp.cos(angle)
    sine_ref[...] = jnp.where(lane < 64, -sine, sine)
    copies[-1].wait()


def join_kernel(after_ref, own_any, y1_any, y2_any, y3_any, near_ref, sems):
    rows = own_any.shape[0]
    blocks = enumerate((own_any, y1_any, y2_any, y3_any))
    for copy in fetches([(block, near_ref.at[pl.ds(k * rows, rows)]) for k, block in blocks], sems):
        copy.wait()


def late_kernel(scale, index_ref, near_ref, far_ref, first_ref, second_ref, query_ref, cosine_ref, sine_ref, sum_ref, top_ref,
                whole_ref, projected_ref, entry_ref, mixed_ref, share_ref):
    rows, depth = query_ref.shape[0], near_ref.shape[1]
    me = index_ref[0]
    chips = near_ref.shape[0] // rows
    mine, core = me // 2, me % 2
    split = first_ref.shape[0] // (2 * depth)
    total = jnp.zeros((rows, 2 * LANES), F32)
    for chip in range(chips):
        place = pl.ds(pl.multiple_of((mine + chips - chip) % chips * rows, rows), rows)
        weight_ref, base = (first_ref, chip) if chip < split else (second_ref, chip - split)
        for block_ref, half in ((near_ref, core), (far_ref, 1 - core)):
            start = pl.multiple_of((2 * base + half) * depth, depth)
            total += dot(block_ref[place, :], weight_ref[pl.ds(start, depth), :])
    projected_ref[...] = total[:, LANES:]
    key = total[:, :LANES]
    key = (key * cosine_ref[...] + pltpu.roll(key, 64, 1) * sine_ref[...]).astype(BF16)
    entry_ref[...] = key
    key = key.astype(F32)
    for h in range(GROUP):
        place = slice(h * rows, (h + 1) * rows)
        query = query_ref[:, h * LANES : (h + 1) * LANES].astype(F32)
        own = jnp.sum(query * key, axis=1, keepdims=True) * scale
        top = top_ref[place, :]
        highest = jnp.maximum(top, own)
        old, new = jnp.exp(top - highest), jnp.exp(own - highest)
        under = 1.0 / (old * whole_ref[place, :] + new)
        mixed_ref[place, :] = sum_ref[place, :] * (old * under)
        share_ref[place, :] = new * under


def final_kernel(got_ref, back_ref, value_ref, key_ref, mixed_ref, share_ref, out_ref, entry_ref):
    rows = value_ref.shape[0]
    slots = got_ref.shape[0]
    delta = dot(back_ref[:, :slots], got_ref[...])
    value = (value_ref[...] + delta).astype(BF16)
    entry_ref[:, :LANES] = key_ref[...]
    entry_ref[:, LANES:] = value
    value = value.astype(F32)
    for h in range(GROUP):
        place = slice(h * rows, (h + 1) * rows)
        out_ref[:, h * LANES : (h + 1) * LANES] = (mixed_ref[place, :] + share_ref[place, :] * value).astype(BF16)


def on_device(hidden, queries, key_cache, value_cache, lengths, tenants, weight, down, up):
    rows, depth = hidden.shape
    peers = lax.axis_size("dp")
    count = lax.axis_size("tensor")
    slots = peers * CAPACITY
    pool, _, rank = down.shape
    chunks = depth // LANES + 1
    scale = HEAD_SIZE ** -0.5
    shape, vmem, dma = jax.ShapeDtypeStruct, pltpu.VMEM, pltpu.SemaphoreType.DMA
    params = lambda size: pltpu.CompilerParams(vmem_limit_bytes=size * MIB)
    far = lambda *arrays: [pltpu.with_memory_space_constraint(x, pltpu.HBM) for x in arrays]
    cost = lambda flops, size: pl.CostEstimate(flops=flops, bytes_accessed=size, transcendentals=0)

    tenant_row = tenants.reshape(1, rows)
    length_row = lengths.reshape(1, rows)
    me = lax.axis_index("tensor").astype(I32).reshape(1)
    over_core = lambda x: lax.ppermute(x, "tensor", [(i, i ^ 1) for i in range(count)])
    over_y = lambda x, k: lax.ppermute(x, "tensor", [(i, (i + 2 * k) % count) for i in range(count)])

    ahead = AHEAD_CHIPS * 2 * depth
    ring = [[(k + TURN) % peers for k in range(peers)]]
    back_ring = [[(k + BACK_TURN) % peers for k in range(peers)]]
    inverse = ROPE_BASE ** (-(np.arange(HEAD_SIZE // 2, dtype=np.float32) * 2.0) / HEAD_SIZE)
    inverse = jnp.asarray(np.concatenate([inverse, inverse])[None, :], F32)

    with jax.named_scope("place"):
        placed, handed = pl.pallas_call(
            lambda *refs: place_kernel(pool, *refs),
            out_shape=[shape((slots * chunks, LANES), BF16), shape((rows, depth), BF16)],
            in_specs=[HBM] * 2, out_specs=[VMEM] * 2, compiler_params=params(8),
            scratch_shapes=[vmem((1, rows), I32), dma((2,))],
        )(*far(tenant_row, hidden))
    with jax.named_scope("rows_to_owners"):
        got = lax.all_to_all(
            placed.reshape(peers, chunks, CAPACITY, LANES), "dp", split_axis=0, concat_axis=0, tiled=True, axis_index_groups=ring
        ).reshape(slots * chunks, LANES)
    with jax.named_scope("gather_hidden"):
        others = [over_y(handed, k) for k in (1, 2, 3)]
    with jax.named_scope("mark"):
        mark = pl.pallas_call(
            mark_kernel, out_shape=shape((8, LANES), F32), in_specs=[ANY] + [HBM] * 2, out_specs=VMEM,
            compiler_params=params(2),
        )(placed, *far(key_cache, value_cache))
    with jax.named_scope("down"):
        partial, ids, up_near, queries_near, length_near = pl.pallas_call(
            down_kernel,
            out_shape=[
                shape((slots // 2, LANES), F32), shape((slots, LANES), F32), shape((pool * rank, LANES), BF16),
                shape(queries.shape, BF16), shape((1, rows), I32),
            ],
            in_specs=[VMEM] * 2 + [HBM] * 3 + [ANY], out_specs=[VMEM] * 5, compiler_params=params(8),
            scratch_shapes=[dma((3,))],
        )(got, jnp.swapaxes(down, 1, 2).reshape(pool * rank, depth),
          *far(up.reshape(pool * rank, LANES), queries, length_row), mark)
    with jax.named_scope("reduce"):
        pair_sum = partial + over_core(partial)
        sums_y = [over_y(pair_sum, k) for k in (1, 2, 3)]
    with jax.named_scope("join"):
        near = pl.pallas_call(
            join_kernel, out_shape=shape((4 * rows, depth), BF16), in_specs=[ANY] * 5, out_specs=VMEM,
            scratch_shapes=[dma((4,))], compiler_params=params(4),
        )(pair_sum, handed, *others)
    with jax.named_scope("gather_core"):
        other = over_core(near)
    with jax.named_scope("mark2"):
        mark = pl.pallas_call(
            mark_kernel, out_shape=shape((8, LANES), F32), in_specs=[ANY] + [HBM] * MARKS, out_specs=VMEM,
            compiler_params=params(2),
        )(pair_sum, *far(key_cache, value_cache, weight)[:MARKS])
    with jax.named_scope("cache"):
        *states, weight_first = pl.pallas_call(
            lambda *refs: cache_kernel(scale, *refs),
            out_shape=[shape((GROUP * rows, LANES), F32)] * 3 + [shape((ahead, 2 * LANES), BF16)],
            in_specs=[ANY] + [VMEM] * 4 + [HBM], out_specs=[VMEM] * 4, compiler_params=params(8),
            scratch_shapes=[dma],
        )(mark, length_near, queries_near, key_cache, value_cache, *far(weight))
    with jax.named_scope("up"):
        served = pl.pallas_call(
            up_kernel, out_shape=shape((slots, LANES), BF16),
            in_specs=[ANY] * 2 + [VMEM] * 6, out_specs=VMEM, compiler_params=params(8),
        )(near, states[0], pair_sum, *sums_y, ids, up_near)
    with jax.named_scope("answers"):
        returned = lax.all_to_all(
            served.reshape(peers, CAPACITY, LANES), "dp", split_axis=0, concat_axis=0, tiled=True, axis_index_groups=back_ring
        ).reshape(slots, LANES)
    with jax.named_scope("tables"):
        weight_second, cosine, sine, back = pl.pallas_call(
            lambda *refs: tables_kernel(pool, peers, *refs),
            out_shape=[
                shape((count * depth - ahead, 2 * LANES), BF16), shape((rows, LANES), F32), shape((rows, LANES), F32),
                shape((rows, LANES), BF16),
            ],
            in_specs=[ANY] + [HBM] * 4, out_specs=[VMEM] * 4,
            scratch_shapes=[vmem((1, rows), I32), vmem((1, rows), I32), vmem((1, LANES), F32), dma((4,))],
            compiler_params=params(8),
        )(served, *far(tenant_row, length_row, inverse, weight))
    with jax.named_scope("late"):
        value, key, mixed, share = pl.pallas_call(
            lambda *refs: late_kernel(scale, *refs),
            out_shape=[shape((rows, LANES), F32), shape((rows, LANES), BF16)] + [shape((GROUP * rows, LANES), F32)] * 2,
            in_specs=[SMEM] + [VMEM] * 10, out_specs=[VMEM] * 4, compiler_params=params(8),
            cost_estimate=cost(2 * rows * count * depth * 2 * LANES, weight.size * 2),
        )(me, near, other, weight_first, weight_second, queries_near, cosine, sine, *states)
    with jax.named_scope("finish"):
        return tuple(pl.pallas_call(
            final_kernel,
            out_shape=[shape((rows, GROUP * LANES), BF16), shape((rows, 2 * LANES), BF16)],
            in_specs=[VMEM] * 6, out_specs=[VMEM] * 2, compiler_params=params(8),
        )(returned, back, value, key, mixed, share))


def solution(mesh):
    in_specs = (
        P("dp", "tensor"),
        P("dp", "tensor"),
        P("dp", None, "tensor"),
        P("dp", None, "tensor"),
        P("dp"),
        P("dp"),
        P(None, "tensor"),
        P("dp", "tensor", None),
        P("dp", None, "tensor"),
    )
    out_specs = (P("dp", "tensor"), P("dp", "tensor"))
    return jax.shard_map(
        on_device, mesh=mesh, in_specs=in_specs, out_specs=out_specs, check_vma=False
    )
```

```python
import jax
import jax.numpy as jnp
import numpy as np
from jax import lax
from jax.experimental import pallas as pl
from jax.experimental.pallas import tpu as pltpu
from jax.sharding import PartitionSpec as P

HEAD_SIZE = 128
GROUP = 8
CAPACITY = 2
LANES = 128
ROPE_BASE = 500000.0
MIB = 1 << 20
TURN = 22
BACK_TURN = 18
MARKS = 3
AHEAD_CHIPS = 2

F32, BF16, I32 = jnp.float32, jnp.bfloat16, jnp.int32
VMEM = pl.BlockSpec(memory_space=pltpu.VMEM)
SMEM = pl.BlockSpec(memory_space=pltpu.SMEM)
HBM = pl.BlockSpec(memory_space=pltpu.HBM)
ANY = pl.BlockSpec(memory_space=pl.ANY)


def iota(shape, dim):
    return lax.broadcasted_iota(I32, shape, dim)


def dot(a, b):
    return jnp.dot(a, b, preferred_element_type=F32)


def dot_t(a, b):
    return lax.dot_general(a, b, (((1,), (1,)), ((), ())), preferred_element_type=F32)


def upright(row):
    n = row.shape[1]
    spread = jnp.broadcast_to(row, (n, n))
    return jnp.sum(jnp.where(iota((n, n), 0) == iota((n, n), 1), spread, 0.0), axis=1, keepdims=True)


def shuffle(chunks, forward):
    wide = 16 * chunks
    row, col = iota((wide, wide), 0), iota((wide, wide), 1)
    chunked, message = (col, row) if forward else (row, col)
    k, s, c = chunked >> 4, (chunked >> 1) & 7, chunked & 1
    return jnp.where(message == s * (2 * chunks) + k * 2 + c, 1.0, 0.0).astype(BF16)


def slots_of(tenant_row, pool, peers, turn):
    n = tenant_row.shape[1]
    owner_row = jnp.floor(tenant_row * (1.0 / pool)) - turn
    owner_row = jnp.where(owner_row < 0.0, owner_row + peers, owner_row)
    owner_col = upright(owner_row)
    same = (owner_col == owner_row) & (iota((n, n), 0) < iota((n, n), 1))
    rank = jnp.sum(jnp.where(same, 1.0, 0.0), axis=0, keepdims=True)
    return owner_row * CAPACITY + rank


def fetches(pairs, sems):
    copies = [pltpu.make_async_copy(source, target, sems.at[i]) for i, (source, target) in enumerate(pairs)]
    for copy in copies:
        copy.start()
    return copies


def place_kernel(pool, tenant_hbm, hidden_hbm, out_ref, hidden_ref, tenant_ref, sems):
    fetch_hidden = pltpu.make_async_copy(hidden_hbm, hidden_ref, sems.at[0])
    fetch_tenant = pltpu.make_async_copy(tenant_hbm, tenant_ref, sems.at[1])
    fetch_tenant.start()
    fetch_hidden.start()
    rows, width = hidden_ref.shape
    chunks = width // LANES + 1
    slots = out_ref.shape[0] // chunks
    mix = shuffle(chunks, True)
    fetch_tenant.wait()
    tenant_row = tenant_ref[...].astype(F32)
    slot_row = slots_of(tenant_row, pool, slots // CAPACITY, TURN)
    place = jnp.where(slot_row == iota((slots, rows), 0).astype(F32), 1.0, 0.0).astype(BF16)
    local = tenant_row - pool * jnp.floor(tenant_row * (1.0 / pool))
    local = jnp.broadcast_to(upright(local), (rows, LANES)).astype(BF16)
    fetch_hidden.wait()
    placed = jnp.concatenate([dot(place, hidden_ref[...]), dot(place, local)], axis=1).astype(BF16)
    groups = slots // 16
    side = jnp.concatenate(
        [
            jnp.concatenate(
                [placed[g * 16 : g * 16 + 16, k * LANES : (k + 1) * LANES] for k in range(chunks)], axis=0
            )
            for g in range(groups)
        ],
        axis=1,
    )
    turned = dot(mix, side).astype(BF16)
    wide = 16 * chunks
    for g in range(groups):
        out_ref[g * wide : (g + 1) * wide, :] = turned[:, g * LANES : (g + 1) * LANES]


def down_kernel(got_ref, down_ref, up_hbm, query_hbm, length_hbm, after_ref, partial_ref, ids_ref, up_ref, query_ref,
                length_ref, sems):
    copies = fetches([(up_hbm, up_ref), (query_hbm, query_ref), (length_hbm, length_ref)], sems)
    slots = ids_ref.shape[0]
    chunks = got_ref.shape[0] // slots
    groups, wide = slots // 16, 16 * chunks
    side = jnp.concatenate([got_ref[g * wide : (g + 1) * wide, :] for g in range(groups)], axis=1)
    turned = dot(shuffle(chunks, False), side)
    ids = jnp.concatenate([turned[wide - 16 :, g * LANES : (g + 1) * LANES] for g in range(groups)], axis=0)
    turned = turned.astype(BF16)
    rows = jnp.concatenate(
        [
            jnp.concatenate(
                [turned[k * 16 : k * 16 + 16, g * LANES : (g + 1) * LANES] for k in range(chunks - 1)], axis=1
            )
            for g in range(groups)
        ],
        axis=0,
    )
    full = dot_t(rows, down_ref[...])
    lane = iota((slots, LANES), 1)
    right = (lane >= 64).astype(F32)
    total = jnp.zeros((slots, LANES), F32)
    for q in range(full.shape[1] // LANES):
        total += jnp.where(ids == right + 2.0 * q, full[:, q * LANES : (q + 1) * LANES], 0.0)
    total = total + pltpu.roll(total, 64, 1)
    half = slots // 2
    partial_ref[...] = jnp.where(lane[:half] < 64, total[:half], total[half:])
    ids_ref[...] = ids
    for copy in copies:
        copy.wait()


def up_kernel(after_ref, after2_ref, a_ref, b_ref, c_ref, d_ref, ids_ref, up_ref, out_ref):
    rows = out_ref.shape[0]
    head = (BACK_TURN - TURN) * CAPACITY % rows
    total = (a_ref[...] + b_ref[...]) + (c_ref[...] + d_ref[...])
    turned = pltpu.roll(total, 64, 1)
    left = iota(total.shape, 1) < 64
    both = jnp.concatenate([jnp.where(left, total, turned), jnp.where(left, turned, total)], axis=0)
    ids = ids_ref[...]
    right = (iota(ids.shape, 1) >= 64).astype(F32)
    spread = [
        jnp.where(ids == right + 2.0 * q, both, 0.0).astype(BF16) for q in range(up_ref.shape[0] // LANES)
    ]
    served = dot(jnp.concatenate(spread, axis=1), up_ref[...])
    if head:
        served = jnp.concatenate([served[head:], served[:head]], axis=0)
    out_ref[...] = served.astype(BF16)


def cache_kernel(scale, after_ref, length_ref, query_ref, key_ref, value_ref, weight_hbm, sum_ref, top_ref, whole_ref,
                 weight_ref, sem):
    fetch_weight = pltpu.make_async_copy(weight_hbm.at[pl.ds(0, weight_ref.shape[0])], weight_ref, sem)
    fetch_weight.start()
    rows, length = key_ref.shape[0], key_ref.shape[1]
    wide = rows * GROUP
    by_head = jnp.concatenate([query_ref[:, h * LANES : (h + 1) * LANES] for h in range(GROUP)], axis=0)
    row, col = iota((wide, wide), 0), iota((wide, wide), 1)
    turn = jnp.where(col == (row % GROUP) * rows + row // GROUP, 1.0, 0.0).astype(BF16)
    by_row = dot(turn, by_head)
    position = iota((GROUP, length), 1).astype(F32)
    limit = jnp.broadcast_to(upright(length_ref[...].astype(F32)), (rows, length))
    scores = []
    for r in range(rows):
        query = by_row[r * GROUP : (r + 1) * GROUP].astype(BF16)
        score = dot_t(query, key_ref[r]) * scale
        scores.append(jnp.where(position < limit[r : r + 1], score, -jnp.inf))
    scores = jnp.concatenate(scores, axis=0)
    top = jnp.max(scores, axis=1, keepdims=True)
    weights = jnp.exp(scores - top)
    whole = jnp.broadcast_to(jnp.sum(weights, axis=1, keepdims=True), (wide, LANES))
    top = jnp.broadcast_to(top, (wide, LANES))
    for r in range(rows):
        some = slice(r * GROUP, (r + 1) * GROUP)
        place = pl.ds(r, GROUP, stride=rows)
        sum_ref[place, :] = dot(weights[some].astype(BF16), value_ref[r])
        top_ref[place, :] = top[some]
        whole_ref[place, :] = whole[some]
    fetch_weight.wait()


def mark_kernel(*refs):
    out_ref = refs[-1]
    out_ref[...] = jnp.zeros(out_ref.shape, F32)


def tables_kernel(pool, peers, after_ref, tenant_hbm, row_hbm, inverse_hbm, weight_hbm, weight_ref, cosine_ref, sine_ref,
                  back_ref, tenant_ref, row_ref, inverse_ref, sems):
    rows = back_ref.shape[0]
    copies = fetches(
        [
            (tenant_hbm, tenant_ref), (row_hbm, row_ref), (inverse_hbm, inverse_ref),
            (weight_hbm.at[pl.ds(weight_hbm.shape[0] - weight_ref.shape[0], weight_ref.shape[0])], weight_ref),
        ],
        sems,
    )
    for copy in copies[:3]:
        copy.wait()
    lane = iota((rows, LANES), 1)
    slot_col = upright(slots_of(tenant_ref[...].astype(F32), pool, peers, BACK_TURN))
    back_ref[...] = jnp.where(slot_col == lane.astype(F32), 1.0, 0.0).astype(BF16)
    angle = upright(row_ref[...].astype(F32)) * inverse_ref[...]
    sine = jnp.sin(angle)
    cosine_ref[...] = jnp.cos(angle)
    sine_ref[...] = jnp.where(lane < 64, -sine, sine)
    copies[-1].wait()


def join_kernel(after_ref, own_any, y1_any, y2_any, y3_any, near_ref, sems):
    rows = own_any.shape[0]
    blocks = enumerate((own_any, y1_any, y2_any, y3_any))
    for copy in fetches([(block, near_ref.at[pl.ds(k * rows, rows)]) for k, block in blocks], sems):
        copy.wait()


def late_kernel(scale, index_ref, near_ref, far_ref, first_ref, second_ref, query_ref, cosine_ref, sine_ref, sum_ref, top_ref,
                whole_ref, projected_ref, entry_ref, mixed_ref, share_ref):
    rows, depth = query_ref.shape[0], near_ref.shape[1]
    me = index_ref[0]
    chips = near_ref.shape[0] // rows
    mine, core = me // 2, me % 2
    split = first_ref.shape[0] // (2 * depth)
    total = jnp.zeros((rows, 2 * LANES), F32)
    for chip in range(chips):
        place = pl.ds(pl.multiple_of((mine + chips - chip) % chips * rows, rows), rows)
        weight_ref, base = (first_ref, chip) if chip < split else (second_ref, chip - split)
        for block_ref, half in ((near_ref, core), (far_ref, 1 - core)):
            start = pl.multiple_of((2 * base + half) * depth, depth)
            total += dot(block_ref[place, :], weight_ref[pl.ds(start, depth), :])
    projected_ref[...] = total[:, LANES:]
    key = total[:, :LANES]
    key = (key * cosine_ref[...] + pltpu.roll(key, 64, 1) * sine_ref[...]).astype(BF16)
    entry_ref[...] = key
    key = key.astype(F32)
    for h in range(GROUP):
        place = slice(h * rows, (h + 1) * rows)
        query = query_ref[:, h * LANES : (h + 1) * LANES].astype(F32)
        own = jnp.sum(query * key, axis=1, keepdims=True) * scale
        top = top_ref[place, :]
        highest = jnp.maximum(top, own)
        old, new = jnp.exp(top - highest), jnp.exp(own - highest)
        under = 1.0 / (old * whole_ref[place, :] + new)
        mixed_ref[place, :] = sum_ref[place, :] * (old * under)
        share_ref[place, :] = new * under


def final_kernel(got_ref, back_ref, value_ref, key_ref, mixed_ref, share_ref, out_ref, entry_ref):
    rows = value_ref.shape[0]
    slots = got_ref.shape[0]
    delta = dot(back_ref[:, :slots], got_ref[...])
    value = (value_ref[...] + delta).astype(BF16)
    entry_ref[:, :LANES] = key_ref[...]
    entry_ref[:, LANES:] = value
    value = value.astype(F32)
    for h in range(GROUP):
        place = slice(h * rows, (h + 1) * rows)
        out_ref[:, h * LANES : (h + 1) * LANES] = (mixed_ref[place, :] + share_ref[place, :] * value).astype(BF16)


def on_device(hidden, queries, key_cache, value_cache, lengths, tenants, weight, down, up):
    rows, depth = hidden.shape
    peers = lax.axis_size("dp")
    count = lax.axis_size("tensor")
    slots = peers * CAPACITY
    pool, _, rank = down.shape
    chunks = depth // LANES + 1
    scale = HEAD_SIZE ** -0.5
    shape, vmem, dma = jax.ShapeDtypeStruct, pltpu.VMEM, pltpu.SemaphoreType.DMA
    params = lambda size: pltpu.CompilerParams(vmem_limit_bytes=size * MIB)
    far = lambda *arrays: [pltpu.with_memory_space_constraint(x, pltpu.HBM) for x in arrays]
    cost = lambda flops, size: pl.CostEstimate(flops=flops, bytes_accessed=size, transcendentals=0)

    tenant_row = tenants.reshape(1, rows)
    length_row = lengths.reshape(1, rows)
    me = lax.axis_index("tensor").astype(I32).reshape(1)
    over_core = lambda x: lax.ppermute(x, "tensor", [(i, i ^ 1) for i in range(count)])
    over_y = lambda x, k: lax.ppermute(x, "tensor", [(i, (i + 2 * k) % count) for i in range(count)])

    ahead = AHEAD_CHIPS * 2 * depth
    ring = [[(k + TURN) % peers for k in range(peers)]]
    back_ring = [[(k + BACK_TURN) % peers for k in range(peers)]]
    inverse = ROPE_BASE ** (-(np.arange(HEAD_SIZE // 2, dtype=np.float32) * 2.0) / HEAD_SIZE)
    inverse = jnp.asarray(np.concatenate([inverse, inverse])[None, :], F32)

    with jax.named_scope("place"):
        placed, handed = pl.pallas_call(
            lambda *refs: place_kernel(pool, *refs),
            out_shape=[shape((slots * chunks, LANES), BF16), shape((rows, depth), BF16)],
            in_specs=[HBM] * 2, out_specs=[VMEM] * 2, compiler_params=params(8),
            scratch_shapes=[vmem((1, rows), I32), dma((2,))],
        )(*far(tenant_row, hidden))
    with jax.named_scope("rows_to_owners"):
        got = lax.all_to_all(
            placed.reshape(peers, chunks, CAPACITY, LANES), "dp", split_axis=0, concat_axis=0, tiled=True, axis_index_groups=ring
        ).reshape(slots * chunks, LANES)
    with jax.named_scope("gather_hidden"):
        sent = {k: over_y(handed, k) for k in (2, 1, 3)}
        others = [sent[k] for k in (1, 2, 3)]
    with jax.named_scope("mark"):
        mark = pl.pallas_call(
            mark_kernel, out_shape=shape((8, LANES), F32), in_specs=[ANY] + [HBM] * 2, out_specs=VMEM,
            compiler_params=params(2),
        )(placed, *far(key_cache, value_cache))
    with jax.named_scope("down"):
        partial, ids, up_near, queries_near, length_near = pl.pallas_call(
            down_kernel,
            out_shape=[
                shape((slots // 2, LANES), F32), shape((slots, LANES), F32), shape((pool * rank, LANES), BF16),
                shape(queries.shape, BF16), shape((1, rows), I32),
            ],
            in_specs=[VMEM] * 2 + [HBM] * 3 + [ANY], out_specs=[VMEM] * 5, compiler_params=params(8),
            scratch_shapes=[dma((3,))],
        )(got, jnp.swapaxes(down, 1, 2).reshape(pool * rank, depth),
          *far(up.reshape(pool * rank, LANES), queries, length_row), mark)
    with jax.named_scope("reduce"):
        pair_sum = partial + over_core(partial)
        sums_y = [over_y(pair_sum, k) for k in (1, 2, 3)]
    with jax.named_scope("join"):
        near = pl.pallas_call(
            join_kernel, out_shape=shape((4 * rows, depth), BF16), in_specs=[ANY] * 5, out_specs=VMEM,
            scratch_shapes=[dma((4,))], compiler_params=params(4),
        )(pair_sum, handed, *others)
    with jax.named_scope("gather_core"):
        other = over_core(near)
    with jax.named_scope("mark2"):
        mark = pl.pallas_call(
            mark_kernel, out_shape=shape((8, LANES), F32), in_specs=[ANY] + [HBM] * MARKS, out_specs=VMEM,
            compiler_params=params(2),
        )(pair_sum, *far(key_cache, value_cache, weight)[:MARKS])
    with jax.named_scope("cache"):
        *states, weight_first = pl.pallas_call(
            lambda *refs: cache_kernel(scale, *refs),
            out_shape=[shape((GROUP * rows, LANES), F32)] * 3 + [shape((ahead, 2 * LANES), BF16)],
            in_specs=[ANY] + [VMEM] * 4 + [HBM], out_specs=[VMEM] * 4, compiler_params=params(8),
            scratch_shapes=[dma],
        )(mark, length_near, queries_near, key_cache, value_cache, *far(weight))
    with jax.named_scope("up"):
        served = pl.pallas_call(
            up_kernel, out_shape=shape((slots, LANES), BF16),
            in_specs=[ANY] * 2 + [VMEM] * 6, out_specs=VMEM, compiler_params=params(8),
        )(near, states[0], pair_sum, *sums_y, ids, up_near)
    with jax.named_scope("answers"):
        returned = lax.all_to_all(
            served.reshape(peers, CAPACITY, LANES), "dp", split_axis=0, concat_axis=0, tiled=True, axis_index_groups=back_ring
        ).reshape(slots, LANES)
    with jax.named_scope("tables"):
        weight_second, cosine, sine, back = pl.pallas_call(
            lambda *refs: tables_kernel(pool, peers, *refs),
            out_shape=[
                shape((count * depth - ahead, 2 * LANES), BF16), shape((rows, LANES), F32), shape((rows, LANES), F32),
                shape((rows, LANES), BF16),
            ],
            in_specs=[ANY] + [HBM] * 4, out_specs=[VMEM] * 4,
            scratch_shapes=[vmem((1, rows), I32), vmem((1, rows), I32), vmem((1, LANES), F32), dma((4,))],
            compiler_params=params(8),
        )(served, *far(tenant_row, length_row, inverse, weight))
    with jax.named_scope("late"):
        value, key, mixed, share = pl.pallas_call(
            lambda *refs: late_kernel(scale, *refs),
            out_shape=[shape((rows, LANES), F32), shape((rows, LANES), BF16)] + [shape((GROUP * rows, LANES), F32)] * 2,
            in_specs=[SMEM] + [VMEM] * 10, out_specs=[VMEM] * 4, compiler_params=params(8),
            cost_estimate=cost(2 * rows * count * depth * 2 * LANES, weight.size * 2),
        )(me, near, other, weight_first, weight_second, queries_near, cosine, sine, *states)
    with jax.named_scope("finish"):
        return tuple(pl.pallas_call(
            final_kernel,
            out_shape=[shape((rows, GROUP * LANES), BF16), shape((rows, 2 * LANES), BF16)],
            in_specs=[VMEM] * 6, out_specs=[VMEM] * 2, compiler_params=params(8),
        )(returned, back, value, key, mixed, share))


def solution(mesh):
    in_specs = (
        P("dp", "tensor"),
        P("dp", "tensor"),
        P("dp", None, "tensor"),
        P("dp", None, "tensor"),
        P("dp"),
        P("dp"),
        P(None, "tensor"),
        P("dp", "tensor", None),
        P("dp", None, "tensor"),
    )
    out_specs = (P("dp", "tensor"), P("dp", "tensor"))
    return jax.shard_map(
        on_device, mesh=mesh, in_specs=in_specs, out_specs=out_specs, check_vma=False
    )
```
